32 devices in a mesh: groups: 2 (over x), expert: 16 (over z, y, core).
Axes of the slice: x: 2, y: 2, z: 4, core: 2. Of those that a mesh axis runs over, the one named last changes fastest.
Arguments:
- hidden_in: bfloat16 [4096, 2048], P(('groups', 'expert')), parts along dimension 0, may hold values from -6 to 6
- norm_gain: float32 [2048], replicated, may hold values from 0.1 to 1.9
- router_weight: bfloat16 [2048, 16], replicated, may hold values from -0.125 to 0.125
- expert_ids: int32 [4096, 8], P(('groups', 'expert')), parts along dimension 0, may hold values from 0 to 15, all different within a row; in each aligned block of 128 rows (0 to 127, 128 to 255, ...) at most 96 rows name the same one
- w_gate: bfloat16 [16, 2048, 768], P('expert'), may hold values from -0.125 to 0.125
- w_up: bfloat16 [16, 2048, 768], P('expert'), may hold values from -0.125 to 0.125
- w_down: bfloat16 [16, 768, 2048], P('expert'), may hold values from -0.21875 to 0.21875
Outputs:
- combined: bfloat16 [4096, 2048], P(('groups', 'expert')), parts along dimension 0
The draws below stay inside these ranges and needn't reach their ends.
There are 2 independent parts, one for each index of `groups`. The reference program is written for one: setup_inputs(seed, part) draws one part's arguments, and reference() takes and returns one part's arrays. A program takes and returns all parts, laid end to end along the dimension named above; an argument that names none is the same for every part. Nothing has to cross between parts.
Inputs may be any that keep to these rules, and one draw needn't show every extreme that they name: `expert_ids`: each row names 8 different experts; within each aligned block of 128 rows (the rows of one device) no expert is named by more than 96 rows, a bound that some block reaches.
All inputs are finite; a program needn't handle non-finite values.
Results may differ from the reference program's by a relative error of at most 0.0074.
Values may be sent and summed in bfloat16 or wider, within the bound.
No kernel may reach another device: no remote copies, remote signals or barrier semaphores. Data moves between devices by JAX's collectives and lax.ppermute only.
A program may use at most 128 MiB of HBM per device.

```python
import math
import jax
import jax.numpy as jnp
import numpy as np
from jax import lax

D = 2048
FF = 768
TOP = 8
TOK_DEV = 128
EXPERTS = 16
CAP = 96
TOKENS = 2048


def shard_levels(rng, shape, pieces, smallest, largest):
    gain = 1.0
    for axis_at, shards_of in pieces:
        heights = jax.random.uniform(jax.random.fold_in(jax.random.fold_in(rng, 6), axis_at), (shards_of,), jnp.float32, smallest / len(pieces), largest / len(pieces))
        gain = gain * jnp.repeat(jnp.exp(heights), shape[axis_at] // shards_of).reshape((-1,) + (1,) * (len(shape) - 1 - axis_at))
    return gain


def assign_block(own_key, own, number, rows, count, top, reach, skew):
    sequence = jax.random.permutation(own_key, count)
    crowded, common = shares(count, rows * top, reach, skew, True), shares(count, rows * top, reach, skew, False)
    places = jnp.arange(count)

    def named(lengths, offset_by):
        used = int((lengths > 0).sum())
        fixed = max(1, used // 4)
        passed = fixed + (places - fixed + offset_by * (used - fixed)) % max(1, count - fixed)
        return jnp.zeros((count,), jnp.int32).at[sequence[jnp.where(places < fixed, places, passed)]].set(jnp.asarray(lengths, jnp.int32))

    lengths = jnp.where(number % 4 == 0, named(crowded, number // 4), named(common, number - number // 4 - 1))
    mixed = jax.random.permutation(jax.random.fold_in(own, 3), count)
    donor, receiver = mixed[0:count // 2 * 2:2], mixed[1:count // 2 * 2:2]
    margin = jnp.minimum(lengths[donor] - 1, reach - lengths[receiver]) // 2
    margin = jnp.where((donor == sequence[0]) | (receiver == sequence[0]) | (lengths[receiver] == 0), 0, jnp.maximum(margin, 0))
    passed = jax.random.randint(jax.random.fold_in(own, 4), (count // 2,), 0, 1 << 20) % (margin + 1)
    lengths = lengths.at[donor].add(-passed).at[receiver].add(passed)
    items = jnp.searchsorted(jnp.cumsum(lengths), jnp.arange(rows * top), side="right").astype(jnp.int32)
    table = items.reshape(top, rows).T
    table = table[jax.random.permutation(jax.random.fold_in(own, 1), rows)]
    offset_by = jax.random.randint(jax.random.fold_in(own, 2), (rows, 1), 0, top)
    return jnp.take_along_axis(table, (jnp.arange(top)[None, :] + offset_by) % top, axis=1)


def shares(count, total, bound, slope, full):
    loads = [(1 << 20) // math.isqrt(grade ** slope) + 1 for grade in range(1, count + 1)]
    largest = bound if full else min(bound, max(-(-total // count), total * loads[0] // sum(loads)))
    least = 1 if total - largest >= count - 1 else 0
    holding, spare = [largest] + [least] * (count - 1), total - largest - least * (count - 1)
    while spare > 0:
        free = [i for i in range(1, count) if holding[i] < largest] or [i for i in range(1, count) if holding[i] < bound]
        mass, left = sum([loads[i] for i in free]), spare
        for i in free:
            more = min(bound - holding[i], max(1, left * loads[i] // mass), spare)
            holding[i] = holding[i] + more
            spare = spare - more
    return np.array(holding)


def normal_values(own_key, shape, spread, bound, split=(), held_as=jnp.bfloat16):
    values = spread * jax.random.normal(own_key, shape, jnp.float32)
    if split:
        values = values * shard_levels(own_key, shape, split, -0.22, 0.18)
    return jnp.clip(values, -bound, bound).astype(held_as)


def setup_inputs(seed: int = 0, part: int = 0) -> dict:
    key_of = jax.random.split(jax.random.key(seed), 8)
    part_splits = jax.random.split(jax.random.fold_in(key_of[7], part), 8)
    hidden_in = normal_values(part_splits[0], (TOKENS, D), 1.0, 6.0, ((0, 16),))
    norm_gain = jnp.clip(1.0 + 0.18 * jax.random.normal(key_of[1], (D,), jnp.float32), 0.1, 1.9)
    router_weight = normal_values(key_of[2], (D, EXPERTS), D ** -0.5, 0.125)
    expert_ids_keys = jax.random.split(jax.random.fold_in(part_splits[3], 1), TOKENS // TOK_DEV)
    expert_ids_turns = jax.random.permutation(jax.random.fold_in(part_splits[3], 3), TOKENS // TOK_DEV)
    expert_ids = jax.vmap(lambda own, number: assign_block(jax.random.fold_in(part_splits[3], 2), own, number, TOK_DEV, EXPERTS, TOP, CAP, 2))(expert_ids_keys, expert_ids_turns).reshape((TOKENS, TOP))
    w_gate = normal_values(key_of[4], (EXPERTS, D, FF), D ** -0.5, 0.125, ((0, 16),))
    w_up = normal_values(key_of[5], (EXPERTS, D, FF), D ** -0.5, 0.125, ((0, 16),))
    w_down = normal_values(key_of[6], (EXPERTS, FF, D), FF ** -0.5, 0.21875, ((0, 16),))
    return {"hidden_in": hidden_in, "norm_gain": norm_gain, "router_weight": router_weight, "expert_ids": expert_ids, "w_gate": w_gate, "w_up": w_up, "w_down": w_down}


def expert_mlp(item):
    rows, gate_w, up_w, down_w = item
    gate_act = jnp.dot(rows, gate_w, preferred_element_type=jnp.float32)
    up_act = jnp.dot(rows, up_w, preferred_element_type=jnp.float32)
    hidden = (jax.nn.silu(gate_act) * up_act).astype(jnp.bfloat16)
    return jnp.dot(hidden, down_w, preferred_element_type=jnp.float32).astype(jnp.bfloat16)

def reference(hidden_in, norm_gain, router_weight, expert_ids, w_gate, w_up, w_down):
    as_float = hidden_in.astype(jnp.float32)
    inv_rms = lax.rsqrt(lax.optimization_barrier(jnp.mean(as_float * as_float, axis=1, keepdims=True)) + 1e-06)
    normed = (as_float * inv_rms * norm_gain).astype(jnp.bfloat16)
    logits = jnp.dot(normed, router_weight, preferred_element_type=jnp.float32)
    exp_logits = jnp.exp(logits)
    picked = jnp.take_along_axis(exp_logits, expert_ids, axis=1)
    route_w = picked / lax.optimization_barrier(jnp.sum(picked, axis=1, keepdims=True))
    blocks = TOKENS // TOK_DEV
    flat_ids = expert_ids.reshape(blocks, TOK_DEV * TOP).astype(jnp.int32)
    onehot = (flat_ids[:, :, None] == jnp.arange(EXPERTS, dtype=jnp.int32)[None, None, :]).astype(jnp.int32)
    before = jnp.cumsum(onehot, axis=1) - onehot
    slot_index = lax.optimization_barrier(jnp.sum(before * onehot, axis=2)).astype(jnp.int32)
    block_index = jnp.arange(blocks, dtype=jnp.int32)[:, None]
    dest_index = (flat_ids * (blocks * CAP) + block_index * CAP + slot_index).reshape(-1).astype(jnp.int32)
    token_rows = jnp.repeat(normed, TOP, axis=0)
    packed = jnp.zeros((EXPERTS * blocks * CAP, D), jnp.bfloat16).at[dest_index].set(token_rows)
    packed = packed.reshape(EXPERTS, blocks * CAP, D)
    expert_out = lax.map(expert_mlp, (packed, w_gate, w_up, w_down)).reshape(EXPERTS * blocks * CAP, D)
    gathered = expert_out[dest_index].reshape(TOKENS, TOP, D)
    combined = lax.optimization_barrier(jnp.sum(gathered.astype(jnp.float32) * route_w[:, :, None], axis=1)).astype(jnp.bfloat16)
    return combined
```

```python
import jax
import jax.numpy as jnp
from jax import lax
from jax.sharding import PartitionSpec as P


def local(hidden_in, norm_gain, router_weight, expert_ids, w_gate, w_up, w_down):
    num_experts = router_weight.shape[1]
    local_experts = w_gate.shape[0]
    as_float = hidden_in.astype(jnp.float32)
    inv_rms = lax.rsqrt(jnp.mean(as_float * as_float, axis=1, keepdims=True) + 1e-06)
    normed = (as_float * inv_rms * norm_gain).astype(jnp.bfloat16)
    everyone = lax.all_gather(normed, "expert", axis=0, tiled=True)
    logits = jnp.dot(normed, router_weight, preferred_element_type=jnp.float32)
    expert_iota = jnp.arange(num_experts, dtype=jnp.int32)
    named = jnp.any(expert_ids[:, :, None] == expert_iota[None, None, :], axis=1)
    picked = jnp.where(named, jnp.exp(logits), 0.0)
    route_w = picked / jnp.sum(picked, axis=1, keepdims=True)
    weights = lax.all_gather(route_w, "expert", axis=0, tiled=True)
    first = lax.axis_index("expert") * local_experts
    total = 0.0
    for e in range(local_experts):
        mine = lax.dynamic_slice_in_dim(weights, first + e, 1, axis=1)
        gate_act = jnp.dot(everyone, w_gate[e], preferred_element_type=jnp.float32)
        up_act = jnp.dot(everyone, w_up[e], preferred_element_type=jnp.float32)
        hidden = (jax.nn.silu(gate_act) * up_act).astype(jnp.bfloat16)
        out = jnp.dot(hidden, w_down[e], preferred_element_type=jnp.float32)
        total = total + out * mine
    return lax.psum_scatter(
        total.astype(jnp.bfloat16), "expert", scatter_dimension=0, tiled=True
    )


def solution(mesh):
    in_specs = (
        P(("groups", "expert"), None),
        P(),
        P(),
        P(("groups", "expert"), None),
        P("expert", None, None),
        P("expert", None, None),
        P("expert", None, None),
    )
    out_specs = P(("groups", "expert"), None)
    return jax.shard_map(local, mesh=mesh, in_specs=in_specs, out_specs=out_specs, check_vma=False)
```

```python
import functools

import jax
import jax.numpy as jnp
from jax import lax
from jax.experimental import pallas as pl
from jax.experimental.pallas import tpu as pltpu
from jax.sharding import PartitionSpec as P

MIB = 1 << 20


def pack_kernel(x_ref, gain_ref, router_ref, ids_ref, out_ref):
    rows, width = x_ref.shape
    num_experts = router_ref.shape[1]
    as_float = x_ref[...].astype(jnp.float32)
    inv_rms = lax.rsqrt(jnp.mean(as_float * as_float, axis=1, keepdims=True) + 1e-06)
    normed = (as_float * inv_rms * gain_ref[...]).astype(jnp.bfloat16)
    out_ref[:, :width] = normed
    logits = jnp.dot(normed, router_ref[...], preferred_element_type=jnp.float32)
    ids = ids_ref[...]
    lane = lax.broadcasted_iota(jnp.int32, (rows, num_experts), 1)
    named = lane == ids[:, 0:1]
    for k in range(1, ids.shape[1]):
        named = named | (lane == ids[:, k : k + 1])
    picked = jnp.where(named, jnp.exp(logits), 0.0)
    weight = picked / jnp.sum(picked, axis=1, keepdims=True)
    high = weight.astype(jnp.bfloat16).astype(jnp.float32)
    parts = [high, weight - high]
    spare = out_ref.shape[1] - width - 2 * num_experts
    if spare:
        parts.append(jnp.zeros((rows, spare), jnp.float32))
    out_ref[:, width:] = jnp.concatenate(parts, axis=1).astype(jnp.bfloat16)


def pack(hidden_in, norm_gain, router_weight, expert_ids):
    rows, width = hidden_in.shape
    lanes = -(-2 * router_weight.shape[1] // 128) * 128
    return pl.pallas_call(
        pack_kernel,
        out_shape=jax.ShapeDtypeStruct((rows, width + lanes), jnp.bfloat16),
        compiler_params=pltpu.CompilerParams(vmem_limit_bytes=32 * MIB),
        name="pack_rows",
    )(hidden_in, norm_gain[None, :], router_weight, expert_ids)


def ffn_kernel(sides, valid_ref, *refs):
    per_side = (len(refs) - 7 - 2 * sides) // sides
    shards = refs[: sides * per_side]
    gate_ref, up_ref, down_ref, mine_ref = refs[sides * per_side : sides * per_side + 4]
    outs = refs[sides * per_side + 4 : sides * per_side + 4 + 2 * sides]
    x_ref, acc_ref, sems = refs[-3:]
    step, steps = pl.program_id(0), pl.num_programs(0)
    width = gate_ref.shape[0]
    rows = shards[0].shape[0]

    def copies(side):
        return [
            pltpu.make_async_copy(
                shards[side * per_side + i],
                x_ref.at[side, pl.ds(i * rows, rows), :],
                sems.at[side, i],
            )
            for i in range(per_side)
        ]

    for side in range(sides):

        @pl.when((valid_ref[side] == 1) & (step == 0))
        def _():
            for copy in copies(side):
                copy.start()

    for side in range(sides):

        @pl.when((valid_ref[side] == 1) & (step == 0))
        def _():
            for copy in copies(side):
                copy.wait()

        @pl.when(valid_ref[side] == 1)
        def _():
            x = x_ref[side, :, :width]
            gate_act = jnp.dot(x, gate_ref[...], preferred_element_type=jnp.float32)
            up_act = jnp.dot(x, up_ref[...], preferred_element_type=jnp.float32)
            hidden = (gate_act / (1.0 + jnp.exp(-gate_act)) * up_act).astype(jnp.bfloat16)
            out = jnp.dot(hidden, down_ref[...], preferred_element_type=jnp.float32)

            @pl.when(step == 0)
            def _():
                acc_ref[side] = out

            @pl.when(step > 0)
            def _():
                acc_ref[side] += out

            @pl.when(step == steps - 1)
            def _():
                parts = x_ref[side, :, width:].astype(jnp.float32) * mine_ref[...]
                weight = jnp.sum(parts, axis=1, keepdims=True)
                done = (acc_ref[side] * weight).astype(jnp.bfloat16)
                half = done.shape[0] // 2
                outs[2 * side][...] = done[:half]
                outs[2 * side + 1][...] = done[half:]


def ffn(sides, valid, w_gate, w_up, w_down, mine):
    count, per_side = len(sides), len(sides[0])
    rows, packed = sides[0][0].shape
    width, depth = w_gate.shape
    tile = 256 if depth % 256 == 0 else depth
    half = (rows * per_side // 2, width)
    all_rows = rows * per_side
    flat = [s for side in sides for s in side]
    outs = pl.pallas_call(
        functools.partial(ffn_kernel, count),
        out_shape=[jax.ShapeDtypeStruct(half, jnp.bfloat16)] * (2 * count),
        grid_spec=pltpu.PrefetchScalarGridSpec(
            num_scalar_prefetch=1,
            grid=(depth // tile,),
            in_specs=[pl.BlockSpec(memory_space=pl.ANY)] * len(flat)
            + [
                pl.BlockSpec((width, tile), lambda j, v: (0, j)),
                pl.BlockSpec((width, tile), lambda j, v: (0, j)),
                pl.BlockSpec((tile, width), lambda j, v: (j, 0)),
                pl.BlockSpec((1, packed - width), lambda j, v: (0, 0)),
            ],
            out_specs=[pl.BlockSpec(half, lambda j, v: (0, 0))] * (2 * count),
            scratch_shapes=[
                pltpu.VMEM((count, all_rows, packed), jnp.bfloat16),
                pltpu.VMEM((count, all_rows, width), jnp.float32),
                pltpu.SemaphoreType.DMA((count, per_side)),
            ],
        ),
        compiler_params=pltpu.CompilerParams(vmem_limit_bytes=48 * MIB),
        cost_estimate=pl.CostEstimate(
            flops=6 * all_rows * width * depth,
            bytes_accessed=6 * width * depth + 4 * count * all_rows * width,
            transcendentals=all_rows * depth,
        ),
        name="expert_ffn",
    )(valid, *flat, w_gate, w_up, w_down, mine)
    return [(outs[2 * i], outs[2 * i + 1]) for i in range(count)]


def add(*terms):
    return sum(t.astype(jnp.float32) for t in terms).astype(jnp.bfloat16)


def local(planes, columns, cores, hidden_in, norm_gain, router_weight, expert_ids, *weights):
    w_gate, w_up, w_down = weights
    rows = hidden_in.shape[0]
    num_experts = router_weight.shape[1]
    local_experts = w_gate.shape[0]
    place = lax.axis_index("expert")
    plane = place // (columns * cores)

    def send(x, dz, dy, dc, low, high):
        pairs = []
        for z in range(low, high):
            for y in range(columns):
                for c in range(cores):
                    there = ((z + dz) * columns + (y + dy) % columns) * cores + (c + dc) % cores
                    pairs.append(((z * columns + y) * cores + c, there))
        return lax.ppermute(x, "expert", pairs)

    def across(x, low, high):
        mine = [x] + [send(x, 0, d, 0, low, high) for d in range(1, columns)]
        return mine + [send(m, 0, 0, d, low, high) for d in range(1, cores) for m in mine]

    def back(pair, low, high):
        kept, sent = pair
        held = add(kept, send(sent, 0, 0, 1, low, high)) if cores > 1 else kept
        if columns > 1:
            return add(held[:rows], send(held[rows:], 0, 1, 0, low, high))
        return held

    packed = pack(hidden_in, norm_gain, router_weight, expert_ids)
    lane = jnp.arange(packed.shape[1] - hidden_in.shape[1], dtype=jnp.int32)[None, :]

    def run(sides, valid):
        total = None
        for e in range(local_experts):
            here = place * local_experts + e
            mine = ((lane == here) | (lane == num_experts + here)).astype(jnp.float32)
            outs = ffn(sides, valid, w_gate[e], w_up[e], w_down[e], mine)
            if total is None:
                total = outs
            else:
                total = [tuple(map(add, a, b)) for a, b in zip(total, outs)]
        return total

    below, above = [packed], [packed]
    for s in range(1, planes):
        below.append(send(below[-1], 1, 0, 0, s - 1, planes - 1))
        above.append(send(above[-1], -1, 0, 0, 1, planes - s + 1))
    own = run([across(packed, 0, planes)], jnp.ones((1,), jnp.int32))[0]
    results = []
    for s in range(1, planes):
        valid = jnp.stack([plane >= s, plane + s < planes]).astype(jnp.int32)
        results.append(
            run([across(below[s], s, planes), across(above[s], 0, planes - s)], valid)
        )
    down = up = None
    for s in range(planes - 1, 0, -1):
        low, high = results[s - 1]
        low, high = back(low, s, planes), back(high, 0, planes - s)
        if down is not None:
            low, high = add(low, down), add(high, up)
        down = send(low, -1, 0, 0, s, planes)
        up = send(high, 1, 0, 0, 0, planes - s)
    if down is None:
        return back(own, 0, planes)
    return add(back(own, 0, planes), down, up)


def solution(mesh):
    in_specs = (
        P(("groups", "expert"), None),
        P(),
        P(),
        P(("groups", "expert"), None),
        P("expert", None, None),
        P("expert", None, None),
        P("expert", None, None),
    )
    out_specs = P(("groups", "expert"), None)
    count = mesh.shape["expert"]
    cores = 2 if count % 2 == 0 else 1
    columns = max(1, 4 // mesh.shape["groups"])
    if count % (cores * columns):
        columns = 1
    planes = count // (cores * columns)
    return jax.shard_map(
        functools.partial(local, planes, columns, cores),
        mesh=mesh,
        in_specs=in_specs,
        out_specs=out_specs,
        check_vma=False,
    )
```

```python
import functools

import jax
import jax.numpy as jnp
from jax import lax
from jax.experimental import pallas as pl
from jax.experimental.pallas import tpu as pltpu
from jax.sharding import PartitionSpec as P

MIB = 1 << 20


def pack_kernel(x_ref, gain_ref, router_ref, ids_ref, out_ref):
    rows, width = x_ref.shape
    num_experts = router_ref.shape[0]
    as_float = x_ref[...].astype(jnp.float32)
    inv_rms = lax.rsqrt(jnp.mean(as_float * as_float, axis=1, keepdims=True) + 1e-06)
    normed = (as_float * inv_rms * gain_ref[...]).astype(jnp.bfloat16)
    out_ref[:, :width] = normed
    logits = lax.dot_general(
        router_ref[...], normed, (((1,), (1,)), ((), ())), preferred_element_type=jnp.float32
    )
    ids = ids_ref[...]
    expert = lax.broadcasted_iota(jnp.int32, (num_experts, rows), 0)
    named = expert == ids[0:1, :]
    for k in range(1, ids.shape[0]):
        named = named | (expert == ids[k : k + 1, :])
    picked = jnp.where(named, jnp.exp(logits), 0.0)
    weight = picked / jnp.sum(picked, axis=0, keepdims=True)
    high = weight.astype(jnp.bfloat16).astype(jnp.float32)
    parts = [high, weight - high]
    spare = out_ref.shape[1] - width - 2 * num_experts
    if spare:
        parts.append(jnp.zeros((spare, rows), jnp.float32))
    out_ref[:, width:] = jnp.concatenate(parts, axis=0).T.astype(jnp.bfloat16)


def pack(hidden_in, norm_gain, router_weight, expert_ids):
    rows, width = hidden_in.shape
    lanes = -(-2 * router_weight.shape[1] // 128) * 128
    return pl.pallas_call(
        pack_kernel,
        out_shape=jax.ShapeDtypeStruct((rows, width + lanes), jnp.bfloat16),
        compiler_params=pltpu.CompilerParams(vmem_limit_bytes=16 * MIB),
        name="pack_rows",
    )(hidden_in, norm_gain[None, :], router_weight.T, expert_ids.T)


def ffn_kernel(heights, splits, *refs):
    count = len(heights)
    shards = refs[:count]
    gate_ref, up_ref, down_ref, mine_ref = refs[count : count + 4]
    outs = refs[count + 4 : count + 4 + len(splits)]
    x_ref, hidden_ref, weight_ref = refs[-3:]
    width, depth = gate_ref.shape
    top = 0
    for shard, height in zip(shards, heights):
        x_ref[top : top + height, :] = shard[:, :width]
        parts = shard[:, width:].astype(jnp.float32) * mine_ref[...]
        weight_ref[top : top + height, :] = jnp.sum(parts, axis=1, keepdims=True)
        top += height
    tile = 256 if depth % 256 == 0 else depth

    @pl.loop(0, depth // tile)
    def _(j):
        at = pl.ds(pl.multiple_of(j * tile, tile), tile)
        gate_act = jnp.dot(x_ref[...], gate_ref[:, at], preferred_element_type=jnp.float32)
        up_act = jnp.dot(x_ref[...], up_ref[:, at], preferred_element_type=jnp.float32)
        hidden = gate_act / (1.0 + jnp.exp(-gate_act)) * up_act
        hidden_ref[:, at] = hidden.astype(jnp.bfloat16)

    step = 512 if width % 512 == 0 else width

    @pl.loop(0, width // step)
    def _(j):
        at = pl.ds(pl.multiple_of(j * step, step), step)
        out = jnp.dot(hidden_ref[...], down_ref[:, at], preferred_element_type=jnp.float32)
        done = (out * weight_ref[...]).astype(jnp.bfloat16)
        first = 0
        for out_ref, height in zip(outs, splits):
            out_ref[:, at] = done[first : first + height]
            first += height


def ffn(shards, splits, w_gate, w_up, w_down, mine):
    width, depth = w_gate.shape
    heights = [s.shape[0] for s in shards]
    rows = sum(heights)
    return pl.pallas_call(
        functools.partial(ffn_kernel, heights, splits),
        out_shape=[jax.ShapeDtypeStruct((h, width), jnp.bfloat16) for h in splits],
        scratch_shapes=[
            pltpu.VMEM((rows, width), jnp.bfloat16),
            pltpu.VMEM((rows, depth), jnp.bfloat16),
            pltpu.VMEM((rows, 1), jnp.float32),
        ],
        compiler_params=pltpu.CompilerParams(vmem_limit_bytes=20 * MIB),
        cost_estimate=pl.CostEstimate(
            flops=6 * rows * width * depth,
            bytes_accessed=6 * width * depth + 4 * rows * width,
            transcendentals=rows * depth,
        ),
        name="expert_ffn",
    )(*shards, w_gate, w_up, w_down, mine)


def add(*terms):
    return sum(t.astype(jnp.float32) for t in terms).astype(jnp.bfloat16)


def local(ring, hidden_in, norm_gain, router_weight, expert_ids, w_gate, w_up, w_down):
    rows = hidden_in.shape[0]
    num_experts = router_weight.shape[1]
    local_experts = w_gate.shape[0]
    chips = len(ring)
    full, even = (chips - 1) // 2, chips % 2 == 0
    half = rows // 2

    def shift(by):
        pairs = [
            (2 * ring[p] + c, 2 * ring[(p + by) % chips] + c)
            for p in range(chips)
            for c in range(2)
        ]
        return lambda x: lax.ppermute(x, "expert", pairs)

    ahead, behind = shift(1), shift(-1)

    def sibling(x):
        return lax.ppermute(x, "expert", [(d, d ^ 1) for d in range(2 * chips)])

    packed = pack(hidden_in, norm_gain, router_weight, expert_ids)
    lane = jnp.arange(packed.shape[1] - hidden_in.shape[1], dtype=jnp.int32)[None, :]
    place = lax.axis_index("expert")

    def run(shards, splits):
        total = None
        for e in range(local_experts):
            here = place * local_experts + e
            mine = ((lane == here) | (lane == num_experts + here)).astype(jnp.float32)
            outs = ffn(shards, splits, w_gate[e], w_up[e], w_down[e], mine)
            total = outs if total is None else list(map(add, total, outs))
        return total

    from_behind, from_ahead = [packed], [packed]
    for _ in range(full):
        from_behind.append(ahead(from_behind[-1]))
        from_ahead.append(behind(from_ahead[-1]))
    kept, sent = run([packed, sibling(packed)], [rows, rows])
    own = add(kept, sibling(sent))
    sums = []
    for k in range(1, full + 1):
        low, high = from_behind[k], from_ahead[k]
        low_out, high_out, sent = run(
            [low, high, sibling(low), sibling(high)], [rows, rows, 2 * rows]
        )
        came = sibling(sent)
        sums.append((add(low_out, came[:rows]), add(high_out, came[rows:])))
    low = high = None
    if even:
        first, second = ahead(from_behind[full][:half]), behind(from_ahead[full][half:])
        kept, sent = run([first, second, sibling(first), sibling(second)], [rows, rows])
        far = add(kept, sibling(sent))
        low, high = behind(far[:half]), ahead(far[half:])
    for k in range(full, 0, -1):
        low_sum, high_sum = sums[k - 1]
        if low is not None and low.shape[0] < rows:
            low = jnp.concatenate([add(low_sum[:half], low), low_sum[half:]], axis=0)
            high = jnp.concatenate([high_sum[:half], add(high_sum[half:], high)], axis=0)
        elif low is not None:
            low, high = add(low_sum, low), add(high_sum, high)
        else:
            low, high = low_sum, high_sum
        low, high = behind(low), ahead(high)
    return own if low is None else add(own, low, high)


def solution(mesh):
    in_specs = (
        P(("groups", "expert"), None),
        P(),
        P(),
        P(("groups", "expert"), None),
        P("expert", None, None),
        P("expert", None, None),
        P("expert", None, None),
    )
    out_specs = P(("groups", "expert"), None)
    chips = mesh.shape["expert"] // 2
    columns = max(1, 4 // mesh.shape["groups"])
    if columns == 2 and chips % 2 == 0:
        ring = list(range(0, chips, 2)) + list(range(chips - 1, 0, -2))
    else:
        ring = list(range(chips))
    return jax.shard_map(
        functools.partial(local, ring),
        mesh=mesh,
        in_specs=in_specs,
        out_specs=out_specs,
        check_vma=False,
    )
```

```python
import functools

import jax
import jax.numpy as jnp
from jax import lax
from jax.experimental import pallas as pl
from jax.experimental.pallas import tpu as pltpu
from jax.sharding import PartitionSpec as P

MIB = 1 << 20


def pack_kernel(x_ref, gain_ref, router_ref, ids_ref, out_ref):
    rows, width = x_ref.shape
    num_experts = router_ref.shape[0]
    as_float = x_ref[...].astype(jnp.float32)
    inv_rms = lax.rsqrt(jnp.mean(as_float * as_float, axis=1, keepdims=True) + 1e-06)
    normed = (as_float * inv_rms * gain_ref[...]).astype(jnp.bfloat16)
    out_ref[:, :width] = normed
    logits = lax.dot_general(
        router_ref[...], normed, (((1,), (1,)), ((), ())), preferred_element_type=jnp.float32
    )
    ids = ids_ref[...]
    expert = lax.broadcasted_iota(jnp.int32, (num_experts, rows), 0)
    named = expert == ids[0:1, :]
    for k in range(1, ids.shape[0]):
        named = named | (expert == ids[k : k + 1, :])
    picked = jnp.where(named, jnp.exp(logits), 0.0)
    weight = picked / jnp.sum(picked, axis=0, keepdims=True)
    high = weight.astype(jnp.bfloat16).astype(jnp.float32)
    parts = [high, weight - high]
    spare = out_ref.shape[1] - width - 2 * num_experts
    if spare:
        parts.append(jnp.zeros((spare, rows), jnp.float32))
    out_ref[:, width:] = jnp.concatenate(parts, axis=0).T.astype(jnp.bfloat16)


def pack(hidden_in, norm_gain, router_weight, expert_ids):
    rows, width = hidden_in.shape
    lanes = -(-2 * router_weight.shape[1] // 128) * 128
    return pl.pallas_call(
        pack_kernel,
        out_shape=jax.ShapeDtypeStruct((rows, width + lanes), jnp.bfloat16),
        compiler_params=pltpu.CompilerParams(vmem_limit_bytes=16 * MIB),
        name="pack_rows",
    )(hidden_in, norm_gain[None, :], router_weight.T, expert_ids.T)


def ffn_kernel(heights, splits, *refs):
    count = len(heights)
    shards = refs[:count]
    gate_ref, up_ref, down_ref, mine_ref = refs[count : count + 4]
    outs = refs[count + 4 : count + 4 + len(splits)]
    x_ref, hidden_ref, weight_ref = refs[-3:]
    width, depth = gate_ref.shape
    top = 0
    for shard, height in zip(shards, heights):
        x_ref[top : top + height, :] = shard[:, :width]
        parts = shard[:, width:].astype(jnp.float32) * mine_ref[...]
        weight_ref[top : top + height, :] = jnp.sum(parts, axis=1, keepdims=True)
        top += height
    tile = 256 if depth % 256 == 0 else depth

    @pl.loop(0, depth // tile)
    def _(j):
        at = pl.ds(pl.multiple_of(j * tile, tile), tile)
        gate_act = jnp.dot(x_ref[...], gate_ref[:, at], preferred_element_type=jnp.float32)
        up_act = jnp.dot(x_ref[...], up_ref[:, at], preferred_element_type=jnp.float32)
        hidden = gate_act / (1.0 + jnp.exp(-gate_act)) * up_act
        hidden_ref[:, at] = hidden.astype(jnp.bfloat16)

    step = 512 if width % 512 == 0 else width

    @pl.loop(0, width // step)
    def _(j):
        at = pl.ds(pl.multiple_of(j * step, step), step)
        out = jnp.dot(hidden_ref[...], down_ref[:, at], preferred_element_type=jnp.float32)
        done = (out * weight_ref[...]).astype(jnp.bfloat16)
        first = 0
        for out_ref, height in zip(outs, splits):
            out_ref[:, at] = done[first : first + height]
            first += height


def ffn(shards, splits, w_gate, w_up, w_down, mine):
    width, depth = w_gate.shape
    heights = [s.shape[0] for s in shards]
    rows = sum(heights)
    return pl.pallas_call(
        functools.partial(ffn_kernel, heights, splits),
        out_shape=[jax.ShapeDtypeStruct((h, width), jnp.bfloat16) for h in splits],
        scratch_shapes=[
            pltpu.VMEM((rows, width), jnp.bfloat16),
            pltpu.VMEM((rows, depth), jnp.bfloat16),
            pltpu.VMEM((rows, 1), jnp.float32),
        ],
        compiler_params=pltpu.CompilerParams(vmem_limit_bytes=20 * MIB),
        cost_estimate=pl.CostEstimate(
            flops=6 * rows * width * depth,
            bytes_accessed=6 * width * depth + 4 * rows * width,
            transcendentals=rows * depth,
        ),
        name="expert_ffn",
    )(*shards, w_gate, w_up, w_down, mine)


def add(*terms):
    return sum(t.astype(jnp.float32) for t in terms).astype(jnp.bfloat16)


def local(ring, hidden_in, norm_gain, router_weight, expert_ids, w_gate, w_up, w_down):
    rows = hidden_in.shape[0]
    num_experts = router_weight.shape[1]
    local_experts = w_gate.shape[0]
    chips = len(ring)
    full, even = (chips - 1) // 2, chips % 2 == 0
    half = rows // 2

    def shift(by):
        pairs = [
            (2 * ring[p] + c, 2 * ring[(p + by) % chips] + c)
            for p in range(chips)
            for c in range(2)
        ]
        return lambda x: lax.ppermute(x, "expert", pairs)

    ahead, behind = shift(1), shift(-1)

    def sibling(x):
        return lax.ppermute(x, "expert", [(d, d ^ 1) for d in range(2 * chips)])

    packed = pack(hidden_in, norm_gain, router_weight, expert_ids)
    lane = jnp.arange(packed.shape[1] - hidden_in.shape[1], dtype=jnp.int32)[None, :]
    place = lax.axis_index("expert")

    def run(shards, splits):
        total = None
        for e in range(local_experts):
            here = place * local_experts + e
            mine = ((lane == here) | (lane == num_experts + here)).astype(jnp.float32)
            outs = ffn(shards, splits, w_gate[e], w_up[e], w_down[e], mine)
            total = outs if total is None else list(map(add, total, outs))
        return total

    def near(low, high):
        low_out, high_out, sent = run(
            [low, high, sibling(low), sibling(high)], [rows, rows, 2 * rows]
        )
        return low_out, high_out, sent

    kept, sent = run([packed, sibling(packed)], [rows, rows])
    sums, low, high, tied = [], packed, packed, sent
    for k in range(1, full + 1):
        low, high = ahead(low), behind(high)
        low, high, tied = lax.optimization_barrier((low, high, tied))
        if k == 1:
            sent = tied
        else:
            sums[-1] = sums[-1][:2] + (tied,)
        if k < full or not even:
            sums.append(near(low, high))
            tied = sums[-1][2]
    sums = [(a, b, sibling(c)) for a, b, c in sums]
    own = add(kept, sibling(sent))
    far = None
    if even:
        first, second = ahead(low[:half]), behind(high[half:])
        kept, sent = run([first, second, sibling(first), sibling(second)], [rows, rows])
        far = add(kept, sibling(sent))
        if full:
            low, high, far = lax.optimization_barrier((low, high, far))
            last = near(low, high)
    low = high = None
    if even:
        low, high = behind(far[:half]), ahead(far[half:])
        if full:
            low, high, sent = lax.optimization_barrier((low, high, last[2]))
            sums.append(last[:2] + (sibling(sent),))
    for k in range(full, 0, -1):
        low_out, high_out, came = sums[k - 1]
        low_sum, high_sum = add(low_out, came[:rows]), add(high_out, came[rows:])
        if low is not None and low.shape[0] < rows:
            low = jnp.concatenate([add(low_sum[:half], low), low_sum[half:]], axis=0)
            high = jnp.concatenate([high_sum[:half], add(high_sum[half:], high)], axis=0)
        elif low is not None:
            low, high = add(low_sum, low), add(high_sum, high)
        else:
            low, high = low_sum, high_sum
        low, high = behind(low), ahead(high)
    return own if low is None else add(own, low, high)


def solution(mesh):
    in_specs = (
        P(("groups", "expert"), None),
        P(),
        P(),
        P(("groups", "expert"), None),
        P("expert", None, None),
        P("expert", None, None),
        P("expert", None, None),
    )
    out_specs = P(("groups", "expert"), None)
    chips = mesh.shape["expert"] // 2
    columns = max(1, 4 // mesh.shape["groups"])
    if columns == 2 and chips % 2 == 0:
        ring = list(range(0, chips, 2)) + list(range(chips - 1, 0, -2))
    else:
        ring = list(range(chips))
    return jax.shard_map(
        functools.partial(local, ring),
        mesh=mesh,
        in_specs=in_specs,
        out_specs=out_specs,
        check_vma=False,
    )
```

```python
import functools

import jax
import jax.numpy as jnp
from jax import lax
from jax.experimental import pallas as pl
from jax.experimental.pallas import tpu as pltpu
from jax.sharding import PartitionSpec as P

MIB = 1 << 20


def pack_kernel(x_ref, gain_ref, router_ref, ids_ref, out_ref):
    rows, width = x_ref.shape
    num_experts = router_ref.shape[0]
    as_float = x_ref[...].astype(jnp.float32)
    inv_rms = lax.rsqrt(jnp.mean(as_float * as_float, axis=1, keepdims=True) + 1e-06)
    normed = (as_float * inv_rms * gain_ref[...]).astype(jnp.bfloat16)
    out_ref[:, :width] = normed
    logits = lax.dot_general(
        router_ref[...], normed, (((1,), (1,)), ((), ())), preferred_element_type=jnp.float32
    )
    ids = ids_ref[...]
    expert = lax.broadcasted_iota(jnp.int32, (num_experts, rows), 0)
    named = expert == ids[0:1, :]
    for k in range(1, ids.shape[0]):
        named = named | (expert == ids[k : k + 1, :])
    picked = jnp.where(named, jnp.exp(logits), 0.0)
    weight = picked / jnp.sum(picked, axis=0, keepdims=True)
    high = weight.astype(jnp.bfloat16).astype(jnp.float32)
    parts = [high, weight - high]
    spare = out_ref.shape[1] - width - 2 * num_experts
    if spare:
        parts.append(jnp.zeros((spare, rows), jnp.float32))
    out_ref[:, width:] = jnp.concatenate(parts, axis=0).T.astype(jnp.bfloat16)


def pack(hidden_in, norm_gain, router_weight, expert_ids):
    rows, width = hidden_in.shape
    lanes = -(-2 * router_weight.shape[1] // 128) * 128
    return pl.pallas_call(
        pack_kernel,
        out_shape=jax.ShapeDtypeStruct((rows, width + lanes), jnp.bfloat16),
        compiler_params=pltpu.CompilerParams(vmem_limit_bytes=16 * MIB),
        name="pack_rows",
    )(hidden_in, norm_gain[None, :], router_weight.T, expert_ids.T)


def ffn_kernel(heights, splits, *refs):
    count = len(heights)
    shards = refs[:count]
    gate_ref, up_ref, down_ref, mine_ref = refs[count : count + 4]
    outs = refs[count + 4 : count + 4 + len(splits)]
    x_ref, hidden_ref, weight_ref = refs[-3:]
    width, depth = gate_ref.shape
    top = 0
    for shard, height in zip(shards, heights):
        x_ref[top : top + height, :] = shard[:, :width]
        parts = shard[:, width:].astype(jnp.float32) * mine_ref[...]
        weight_ref[top : top + height, :] = jnp.sum(parts, axis=1, keepdims=True)
        top += height
    tile = 256 if depth % 256 == 0 else depth

    @pl.loop(0, depth // tile)
    def _(j):
        at = pl.ds(pl.multiple_of(j * tile, tile), tile)
        gate_act = jnp.dot(x_ref[...], gate_ref[:, at], preferred_element_type=jnp.float32)
        up_act = jnp.dot(x_ref[...], up_ref[:, at], preferred_element_type=jnp.float32)
        hidden = gate_act / (1.0 + jnp.exp(-gate_act)) * up_act
        hidden_ref[:, at] = hidden.astype(jnp.bfloat16)

    step = 512 if width % 512 == 0 else width

    @pl.loop(0, width // step)
    def _(j):
        at = pl.ds(pl.multiple_of(j * step, step), step)
        out = jnp.dot(hidden_ref[...], down_ref[:, at], preferred_element_type=jnp.float32)
        done = (out * weight_ref[...]).astype(jnp.bfloat16)
        first = 0
        for out_ref, height in zip(outs, splits):
            out_ref[:, at] = done[first : first + height]
            first += height


def ffn(shards, splits, w_gate, w_up, w_down, mine):
    width, depth = w_gate.shape
    heights = [s.shape[0] for s in shards]
    rows = sum(heights)
    return pl.pallas_call(
        functools.partial(ffn_kernel, heights, splits),
        out_shape=[jax.ShapeDtypeStruct((h, width), jnp.bfloat16) for h in splits],
        scratch_shapes=[
            pltpu.VMEM((rows, width), jnp.bfloat16),
            pltpu.VMEM((rows, depth), jnp.bfloat16),
            pltpu.VMEM((rows, 1), jnp.float32),
        ],
        compiler_params=pltpu.CompilerParams(vmem_limit_bytes=20 * MIB),
        cost_estimate=pl.CostEstimate(
            flops=6 * rows * width * depth,
            bytes_accessed=6 * width * depth + 4 * rows * width,
            transcendentals=rows * depth,
        ),
        name="expert_ffn",
    )(*shards, w_gate, w_up, w_down, mine)


def fetch_kernel(turn, core_ref, *refs):
    count = (len(refs) - 1) // (2 if turn else 3)
    sources, outs, sems = refs[:count], refs[-1 - count : -1], refs[-1]
    copies = [
        pltpu.make_async_copy(source, out, sems.at[i])
        for i, (source, out) in enumerate(zip(sources, outs))
    ]

    @pl.when(core_ref[0] == turn)
    def _():
        for copy in copies:
            copy.start()
        for copy in copies:
            copy.wait()


def fetch(turn, core, sources, held=()):
    count = len(sources)
    return pl.pallas_call(
        functools.partial(fetch_kernel, turn),
        out_shape=[jax.ShapeDtypeStruct(s.shape, s.dtype) for s in sources],
        in_specs=[pl.BlockSpec(memory_space=pltpu.SMEM)]
        + [pl.BlockSpec(memory_space=pltpu.HBM)] * count
        + [pl.BlockSpec(memory_space=pltpu.VMEM)] * len(held),
        out_specs=[pl.BlockSpec(memory_space=pltpu.VMEM)] * count,
        scratch_shapes=[pltpu.SemaphoreType.DMA((count,))],
        input_output_aliases={1 + count + i: i for i in range(len(held))},
        compiler_params=pltpu.CompilerParams(vmem_limit_bytes=43 * MIB),
        name="fetch_weights",
    )(core, *sources, *held)


def add(*terms):
    return sum(t.astype(jnp.float32) for t in terms).astype(jnp.bfloat16)


def local(ring, hidden_in, norm_gain, router_weight, expert_ids, w_gate, w_up, w_down):
    rows = hidden_in.shape[0]
    num_experts = router_weight.shape[1]
    local_experts = w_gate.shape[0]
    chips = len(ring)
    full, even = (chips - 1) // 2, chips % 2 == 0
    half = rows // 2

    def shift(by):
        pairs = [
            (2 * ring[p] + c, 2 * ring[(p + by) % chips] + c)
            for p in range(chips)
            for c in range(2)
        ]
        return lambda x: lax.ppermute(x, "expert", pairs)

    ahead, behind = shift(1), shift(-1)

    def sibling(x):
        return lax.ppermute(x, "expert", [(d, d ^ 1) for d in range(2 * chips)])

    packed = pack(hidden_in, norm_gain, router_weight, expert_ids)
    lane = jnp.arange(packed.shape[1] - hidden_in.shape[1], dtype=jnp.int32)[None, :]
    place = lax.axis_index("expert")
    core = (place % 2).astype(jnp.int32)[None]
    sources = [w[e] for e in range(local_experts) for w in (w_gate, w_up, w_down)]
    packed, held = lax.optimization_barrier((packed, fetch(1, core, sources)))
    weights = fetch(0, core, sources, held)

    def run(shards, splits):
        total = None
        for e in range(local_experts):
            here = place * local_experts + e
            mine = ((lane == here) | (lane == num_experts + here)).astype(jnp.float32)
            outs = ffn(shards, splits, *weights[3 * e : 3 * e + 3], mine)
            total = outs if total is None else list(map(add, total, outs))
        return total

    def near(low, high):
        low_out, high_out, sent = run(
            [low, high, sibling(low), sibling(high)], [rows, rows, 2 * rows]
        )
        return low_out, high_out, sent

    kept, sent = run([packed, sibling(packed)], [rows, rows])
    sums, low, high, tied = [], packed, packed, sent
    for k in range(1, full + 1):
        low, high = ahead(low), behind(high)
        low, high, tied = lax.optimization_barrier((low, high, tied))
        if k == 1:
            sent = tied
        else:
            sums[-1] = sums[-1][:2] + (tied,)
        if k < full or not even:
            sums.append(near(low, high))
            tied = sums[-1][2]
    sums = [(a, b, sibling(c)) for a, b, c in sums]
    own = add(kept, sibling(sent))
    far = None
    if even:
        first, second = ahead(low[:half]), behind(high[half:])
        kept, sent = run([first, second, sibling(first), sibling(second)], [rows, rows])
        far = add(kept, sibling(sent))
        if full:
            low, high, far = lax.optimization_barrier((low, high, far))
            last = near(low, high)
    low = high = None
    if even:
        low, high = behind(far[:half]), ahead(far[half:])
        if full:
            low, high, sent = lax.optimization_barrier((low, high, last[2]))
            sums.append(last[:2] + (sibling(sent),))
    for k in range(full, 0, -1):
        low_out, high_out, came = sums[k - 1]
        low_sum, high_sum = add(low_out, came[:rows]), add(high_out, came[rows:])
        if low is not None and low.shape[0] < rows:
            low = jnp.concatenate([add(low_sum[:half], low), low_sum[half:]], axis=0)
            high = jnp.concatenate([high_sum[:half], add(high_sum[half:], high)], axis=0)
        elif low is not None:
            low, high = add(low_sum, low), add(high_sum, high)
        else:
            low, high = low_sum, high_sum
        low, high = behind(low), ahead(high)
    return own if low is None else add(own, low, high)


def solution(mesh):
    in_specs = (
        P(("groups", "expert"), None),
        P(),
        P(),
        P(("groups", "expert"), None),
        P("expert", None, None),
        P("expert", None, None),
        P("expert", None, None),
    )
    out_specs = P(("groups", "expert"), None)
    chips = mesh.shape["expert"] // 2
    columns = max(1, 4 // mesh.shape["groups"])
    if columns == 2 and chips % 2 == 0:
        ring = list(range(0, chips, 2)) + list(range(chips - 1, 0, -2))
    else:
        ring = list(range(chips))
    return jax.shard_map(
        functools.partial(local, ring),
        mesh=mesh,
        in_specs=in_specs,
        out_specs=out_specs,
        check_vma=False,
    )
```

```python
import functools

import jax
import jax.numpy as jnp
from jax import lax
from jax.experimental import pallas as pl
from jax.experimental.pallas import tpu as pltpu
from jax.sharding import PartitionSpec as P

MIB = 1 << 20


def pack_kernel(x_ref, gain_ref, router_ref, ids_ref, out_ref):
    rows, width = x_ref.shape
    num_experts = router_ref.shape[0]
    as_float = x_ref[...].astype(jnp.float32)
    inv_rms = lax.rsqrt(jnp.mean(as_float * as_float, axis=1, keepdims=True) + 1e-06)
    normed = (as_float * inv_rms * gain_ref[...]).astype(jnp.bfloat16)
    out_ref[:, :width] = normed
    logits = lax.dot_general(
        router_ref[...], normed, (((1,), (1,)), ((), ())), preferred_element_type=jnp.float32
    )
    ids = ids_ref[...]
    expert = lax.broadcasted_iota(jnp.int32, (num_experts, rows), 0)
    named = expert == ids[0:1, :]
    for k in range(1, ids.shape[0]):
        named = named | (expert == ids[k : k + 1, :])
    picked = jnp.where(named, jnp.exp(logits), 0.0)
    weight = picked / jnp.sum(picked, axis=0, keepdims=True)
    high = weight.astype(jnp.bfloat16).astype(jnp.float32)
    parts = [high, weight - high]
    spare = out_ref.shape[1] - width - 2 * num_experts
    if spare:
        parts.append(jnp.zeros((spare, rows), jnp.float32))
    out_ref[:, width:] = jnp.concatenate(parts, axis=0).T.astype(jnp.bfloat16)


def pack(hidden_in, norm_gain, router_weight, expert_ids):
    rows, width = hidden_in.shape
    lanes = -(-2 * router_weight.shape[1] // 128) * 128
    return pl.pallas_call(
        pack_kernel,
        out_shape=jax.ShapeDtypeStruct((rows, width + lanes), jnp.bfloat16),
        compiler_params=pltpu.CompilerParams(vmem_limit_bytes=16 * MIB),
        name="pack_rows",
    )(hidden_in, norm_gain[None, :], router_weight.T, expert_ids.T)


def ffn_kernel(heights, splits, *refs):
    count = len(heights)
    shards = refs[:count]
    gate_ref, up_ref, down_ref, mine_ref = refs[count : count + 4]
    outs = refs[count + 4 : count + 4 + len(splits)]
    x_ref, hidden_ref, weight_ref = refs[-3:]
    width, depth = gate_ref.shape
    top = 0
    for shard, height in zip(shards, heights):
        x_ref[top : top + height, :] = shard[:, :width]
        parts = shard[:, width:].astype(jnp.float32) * mine_ref[...]
        weight_ref[top : top + height, :] = jnp.sum(parts, axis=1, keepdims=True)
        top += height
    tile = 256 if depth % 256 == 0 else depth

    @pl.loop(0, depth // tile)
    def _(j):
        at = pl.ds(pl.multiple_of(j * tile, tile), tile)
        gate_act = jnp.dot(x_ref[...], gate_ref[:, at], preferred_element_type=jnp.float32)
        up_act = jnp.dot(x_ref[...], up_ref[:, at], preferred_element_type=jnp.float32)
        hidden = gate_act / (1.0 + jnp.exp(-gate_act)) * up_act
        hidden_ref[:, at] = hidden.astype(jnp.bfloat16)

    step = 512 if width % 512 == 0 else width

    @pl.loop(0, width // step)
    def _(j):
        at = pl.ds(pl.multiple_of(j * step, step), step)
        out = jnp.dot(hidden_ref[...], down_ref[:, at], preferred_element_type=jnp.float32)
        done = (out * weight_ref[...]).astype(jnp.bfloat16)
        first = 0
        for out_ref, height in zip(outs, splits):
            out_ref[:, at] = done[first : first + height]
            first += height


def ffn(shards, splits, w_gate, w_up, w_down, mine):
    width, depth = w_gate.shape
    heights = [s.shape[0] for s in shards]
    rows = sum(heights)
    return pl.pallas_call(
        functools.partial(ffn_kernel, heights, splits),
        out_shape=[jax.ShapeDtypeStruct((h, width), jnp.bfloat16) for h in splits],
        scratch_shapes=[
            pltpu.VMEM((rows, width), jnp.bfloat16),
            pltpu.VMEM((rows, depth), jnp.bfloat16),
            pltpu.VMEM((rows, 1), jnp.float32),
        ],
        compiler_params=pltpu.CompilerParams(vmem_limit_bytes=20 * MIB),
        cost_estimate=pl.CostEstimate(
            flops=6 * rows * width * depth,
            bytes_accessed=rows * width,
            transcendentals=0,
        ),
        name="expert_ffn",
    )(*shards, w_gate, w_up, w_down, mine)


def combine_kernel(parts, *refs):
    out_ref, at, top = refs[-1], 0, 0
    for height, offsets in parts:
        total = 0.0
        for offset in offsets:
            total = total + refs[at][offset : offset + height, :].astype(jnp.float32)
            at += 1
        out_ref[top : top + height, :] = total.astype(out_ref.dtype)
        top += height


def combine(*parts):
    arrays = [array for _, terms in parts for array, _ in terms]
    heights = [(height, [offset for _, offset in terms]) for height, terms in parts]
    rows = sum(height for height, _ in heights)
    return pl.pallas_call(
        functools.partial(combine_kernel, heights),
        out_shape=jax.ShapeDtypeStruct((rows, arrays[0].shape[1]), arrays[0].dtype),
        compiler_params=pltpu.CompilerParams(vmem_limit_bytes=16 * MIB),
        name="combine_rows",
    )(*arrays)


def local(ring, hidden_in, norm_gain, router_weight, expert_ids, w_gate, w_up, w_down):
    rows = hidden_in.shape[0]
    num_experts = router_weight.shape[1]
    local_experts = w_gate.shape[0]
    chips = len(ring)
    full, half = chips // 2 - 1, rows // 2
    tie = lax.optimization_barrier

    def shift(by):
        pairs = [
            (2 * ring[p] + c, 2 * ring[(p + (by if c == 0 else -by)) % chips] + c)
            for p in range(chips)
            for c in range(2)
        ]
        return lambda x: lax.ppermute(x, "expert", pairs)

    step_x, step_y = shift(1), shift(-1)
    back_x, back_y = step_y, step_x

    def sibling(x):
        return lax.ppermute(x, "expert", [(d, d ^ 1) for d in range(2 * chips)])

    packed = pack(hidden_in, norm_gain, router_weight, expert_ids)
    lane = jnp.arange(packed.shape[1] - hidden_in.shape[1], dtype=jnp.int32)[None, :]
    place = lax.axis_index("expert")

    def run(shards, splits):
        total = None
        for e in range(local_experts):
            here = place * local_experts + e
            mine = ((lane == here) | (lane == num_experts + here)).astype(jnp.float32)
            outs = ffn(shards, splits, w_gate[e], w_up[e], w_down[e], mine)
            if total is None:
                total = outs
            else:
                total = [combine((a.shape[0], [(a, 0), (b, 0)])) for a, b in zip(total, outs)]
        return total

    def near(x, y):
        return run([x, y, sibling(x), sibling(y)], [x.shape[0], y.shape[0], 2 * x.shape[0]])

    other = sibling(packed)
    second, other = tie((packed, other))
    own_kept, sent = run([packed, other], [rows, rows])
    x, y, nears, came = [packed], [second], [], []
    for k in range(1, full + 1):
        x.append(step_x(x[-1]))
        y.append(step_y(y[-1]))
        y[k], sent = tie((y[k], sent))
        came.append(sibling(sent))
        *kept, sent = near(x[k], y[k])
        nears.append(kept)
    far_x, far_y = step_x(x[full][:half]), step_y(y[full][half:])
    far_x, far_y, sent = tie((far_x, far_y, sent))
    came.append(sibling(sent))

    def term(k, stream, part):
        return [
            (nears[k - 1][stream], part * half),
            (came[k], stream * rows + part * half),
        ]

    by_x = back_x(combine((half, term(full, 0, 1))))
    by_y = back_y(combine((half, term(full, 1, 0))))
    far_kept_x, far_kept_y, sent = near(far_x, far_y)
    by_x, by_y, sent = tie((by_x, by_y, sent))
    far_came = sibling(sent)
    far_x = back_x(combine((half, [(far_kept_x, 0), (far_came, 0)])))
    far_y = back_y(combine((half, [(far_kept_y, 0), (far_came, half)])))
    from_x, from_y = [(far_x, 0), (by_x, 0)], [(by_y, 0), (far_y, 0)]
    for k in range(full, 1, -1):
        by_x = back_x(
            combine((half, term(k, 0, 0) + [from_x[0]]), (half, term(k - 1, 0, 1) + [from_x[1]]))
        )
        by_y = back_y(
            combine((half, term(k - 1, 1, 0) + [from_y[0]]), (half, term(k, 1, 1) + [from_y[1]]))
        )
        from_x, from_y = [(by_x, 0), (by_x, half)], [(by_y, 0), (by_y, half)]
    last_x = back_x(combine((half, term(1, 0, 0) + [from_x[0]])))
    last_y = back_y(combine((half, term(1, 1, 1) + [from_y[1]])))
    return combine(
        (half, [(own_kept, 0), (came[0], 0), from_y[0], (last_x, 0)]),
        (half, [(own_kept, half), (came[0], half), from_x[1], (last_y, 0)]),
    )


def solution(mesh):
    in_specs = (
        P(("groups", "expert"), None),
        P(),
        P(),
        P(("groups", "expert"), None),
        P("expert", None, None),
        P("expert", None, None),
        P("expert", None, None),
    )
    out_specs = P(("groups", "expert"), None)
    chips = mesh.shape["expert"] // 2
    columns = max(1, 4 // mesh.shape["groups"])
    if columns == 2 and chips % 2 == 0:
        ring = list(range(0, chips, 2)) + list(range(chips - 1, 0, -2))
    else:
        ring = list(range(chips))
    return jax.shard_map(
        functools.partial(local, ring),
        mesh=mesh,
        in_specs=in_specs,
        out_specs=out_specs,
        check_vma=False,
    )
```

```python
import functools

import jax
import jax.numpy as jnp
from jax import lax
from jax.experimental import pallas as pl
from jax.experimental.pallas import tpu as pltpu
from jax.sharding import PartitionSpec as P

MIB = 1 << 20


def pack_kernel(x_ref, gain_ref, router_ref, ids_ref, out_ref):
    rows, width = x_ref.shape
    num_experts = router_ref.shape[0]
    as_float = x_ref[...].astype(jnp.float32)
    inv_rms = lax.rsqrt(jnp.mean(as_float * as_float, axis=1, keepdims=True) + 1e-06)
    normed = (as_float * inv_rms * gain_ref[...]).astype(jnp.bfloat16)
    out_ref[:, :width] = normed
    logits = lax.dot_general(
        router_ref[...], normed, (((1,), (1,)), ((), ())), preferred_element_type=jnp.float32
    )
    ids = ids_ref[...]
    expert = lax.broadcasted_iota(jnp.int32, (num_experts, rows), 0)
    named = expert == ids[0:1, :]
    for k in range(1, ids.shape[0]):
        named = named | (expert == ids[k : k + 1, :])
    picked = jnp.where(named, jnp.exp(logits), 0.0)
    weight = picked / jnp.sum(picked, axis=0, keepdims=True)
    high = weight.astype(jnp.bfloat16).astype(jnp.float32)
    parts = [high, weight - high]
    spare = out_ref.shape[1] - width - 2 * num_experts
    if spare:
        parts.append(jnp.zeros((spare, rows), jnp.float32))
    out_ref[:, width:] = jnp.concatenate(parts, axis=0).T.astype(jnp.bfloat16)


def pack(hidden_in, norm_gain, router_weight, expert_ids):
    rows, width = hidden_in.shape
    lanes = -(-2 * router_weight.shape[1] // 128) * 128
    return pl.pallas_call(
        pack_kernel,
        out_shape=jax.ShapeDtypeStruct((rows, width + lanes), jnp.bfloat16),
        compiler_params=pltpu.CompilerParams(vmem_limit_bytes=16 * MIB),
        name="pack_rows",
    )(hidden_in, norm_gain[None, :], router_weight.T, expert_ids.T)


def ffn_kernel(heights, experts, *refs):
    count = len(heights)
    shards = refs[:count]
    weights, mine_ref = refs[count : count + 3 * experts], refs[count + 3 * experts]
    outs = refs[count + 3 * experts + 1 : -2]
    x_ref, hidden_ref = refs[-2:]
    width, depth = weights[0].shape
    rows = sum(heights)
    top = 0
    parts = []
    for shard, height in zip(shards, heights):
        x_ref[top : top + height, :] = shard[:, :width]
        parts.append(shard[:, width:].astype(jnp.float32))
        top += height
    beside = jnp.concatenate(parts, axis=0)
    scales = [
        jnp.sum(beside * mine_ref[e : e + 1, :], axis=1, keepdims=True) for e in range(experts)
    ]
    tile = 256 if depth % 256 == 0 else depth
    for e in range(experts):
        gate_ref, up_ref = weights[3 * e], weights[3 * e + 1]

        @pl.loop(0, depth // tile)
        def _(j):
            at = pl.ds(pl.multiple_of(j * tile, tile), tile)
            gate_act = jnp.dot(x_ref[...], gate_ref[:, at], preferred_element_type=jnp.float32)
            up_act = jnp.dot(x_ref[...], up_ref[:, at], preferred_element_type=jnp.float32)
            hidden = gate_act / (1.0 + jnp.exp(-gate_act)) * up_act
            hidden_ref[e, :, at] = hidden.astype(jnp.bfloat16)

    step = 512 if width % 512 == 0 else width

    @pl.loop(0, width // step)
    def _(j):
        at = pl.ds(pl.multiple_of(j * step, step), step)
        total = jnp.zeros((rows, step), jnp.float32)
        for e in range(experts):
            out = jnp.dot(
                hidden_ref[e], weights[3 * e + 2][:, at], preferred_element_type=jnp.float32
            )
            total = total + out * scales[e]
        done = total.astype(jnp.bfloat16)
        first = 0
        for out_ref, height in zip(outs, heights):
            out_ref[:, at] = done[first : first + height]
            first += height


def ffn(shards, weights, mine):
    width, depth = weights[0].shape
    experts = len(weights) // 3
    heights = [s.shape[0] for s in shards]
    rows = sum(heights)
    return pl.pallas_call(
        functools.partial(ffn_kernel, heights, experts),
        out_shape=[jax.ShapeDtypeStruct((h, width), jnp.bfloat16) for h in heights],
        scratch_shapes=[
            pltpu.VMEM((rows, width), jnp.bfloat16),
            pltpu.VMEM((experts, rows, depth), jnp.bfloat16),
        ],
        compiler_params=pltpu.CompilerParams(vmem_limit_bytes=16 * MIB),
        cost_estimate=pl.CostEstimate(
            flops=6 * experts * rows * width * depth,
            bytes_accessed=4 * rows * width,
            transcendentals=0,
        ),
        name="expert_ffn",
    )(*shards, *weights, mine)


def fetch_kernel(*refs):
    count = len(refs) // 2
    sems = refs[-1]
    copies = [
        pltpu.make_async_copy(refs[i], refs[count + i], sems.at[i]) for i in range(count)
    ]
    for copy in copies:
        copy.start()
    for copy in copies:
        copy.wait()


def fetch(arrays):
    count = len(arrays)
    return pl.pallas_call(
        fetch_kernel,
        out_shape=[jax.ShapeDtypeStruct(a.shape, a.dtype) for a in arrays],
        in_specs=[pl.BlockSpec(memory_space=pl.ANY)] * count,
        out_specs=[pl.BlockSpec(memory_space=pltpu.VMEM)] * count,
        scratch_shapes=[pltpu.SemaphoreType.DMA((count,))],
        compiler_params=pltpu.CompilerParams(vmem_limit_bytes=38 * MIB),
        name="fetch_weights",
    )(*arrays)


def combine_kernel(parts, *refs):
    out_ref, at, top = refs[-1], 0, 0
    for height, offsets in parts:
        total = 0.0
        for offset in offsets:
            total = total + refs[at][offset : offset + height, :].astype(jnp.float32)
            at += 1
        out_ref[top : top + height, :] = total.astype(out_ref.dtype)
        top += height


def combine(*parts):
    arrays = [array for _, terms in parts for array, _ in terms]
    heights = [(height, [offset for _, offset in terms]) for height, terms in parts]
    rows = sum(height for height, _ in heights)
    return pl.pallas_call(
        functools.partial(combine_kernel, heights),
        out_shape=jax.ShapeDtypeStruct((rows, arrays[0].shape[1]), arrays[0].dtype),
        compiler_params=pltpu.CompilerParams(vmem_limit_bytes=16 * MIB),
        name="combine_rows",
    )(*arrays)


def local(ring, hidden_in, norm_gain, router_weight, expert_ids, w_gate, w_up, w_down):
    rows = hidden_in.shape[0]
    num_experts = router_weight.shape[1]
    local_experts = w_gate.shape[0]
    chips = len(ring)
    full, half = chips // 2 - 1, rows // 2
    tie = lax.optimization_barrier

    def shift(by):
        pairs = [
            (2 * ring[p] + c, 2 * ring[(p + (by if c == 0 else -by)) % chips] + c)
            for p in range(chips)
            for c in range(2)
        ]
        return lambda x: lax.ppermute(x, "expert", pairs)

    step_x, step_y = shift(1), shift(-1)
    back_x, back_y = step_y, step_x

    def sibling(x):
        return lax.ppermute(x, "expert", [(d, d ^ 1) for d in range(2 * chips)])

    own_weights = [w[e] for e in range(local_experts) for w in (w_gate, w_up, w_down)]
    other_weights = [sibling(w) for w in own_weights]
    held = fetch(own_weights)
    packed = pack(hidden_in, norm_gain, router_weight, expert_ids)
    lane = jnp.arange(packed.shape[1] - hidden_in.shape[1], dtype=jnp.int32)[None, :]
    place = lax.axis_index("expert")
    here = jnp.stack([place, place ^ 1])[:, None] * local_experts
    here = (here + jnp.arange(local_experts)[None, :]).reshape(-1, 1)
    mine = ((lane == here) | (lane == num_experts + here)).astype(jnp.float32)

    def run(*shards):
        return ffn(shards, [*held, *other_weights], mine)

    x, y, sums = [packed], [packed], [None]
    for k in range(1, full + 1):
        x.append(step_x(x[-1]))
        y.append(step_y(y[-1]))
        if k == 1:
            y[k], *held = tie((y[k], *held))
        else:
            x[k], sums[k - 1] = tie((x[k], sums[k - 1]))
        if k < full:
            sums.append(run(x[k], y[k]))
    far_x, far_y = step_x(x[full][:half]), step_y(y[full][half:])
    (sum_x,) = run(x[full])
    far_x, far_y, sum_x = tie((far_x, far_y, sum_x))

    far_sum_x, far_sum_y = run(far_x, far_y)
    by_x = back_x(combine((half, [(sum_x, half)])))
    by_x, far_sum_x, far_sum_y = tie((by_x, far_sum_x, far_sum_y))
    by_y = back_y(far_sum_y)
    last_y, _ = tie((y[full], far_sum_y))
    (sum_y,) = run(last_y)
    by_y, sum_y = tie((by_y, sum_y))
    sums.append((sum_x, sum_y))
    from_y = [None, (by_y, 0)]
    for k in range(full, 0, -1):
        parts = [(half, [(sums[k][1], i * half)] + [t for t in [from_y[i]] if t]) for i in (0, 1)]
        by_y = back_y(combine(*parts))
        from_y = [(by_y, 0), (by_y, half)]
    low_term = [(far_sum_x, 0)]
    high_term = (by_x, 0)
    for k in range(full + 1, 0, -1):
        parts = [(half, low_term)]
        if k - 2 >= 1:
            parts.append((half, [(sums[k - 2][0], half), high_term]))
        by_x = back_x(combine(*parts))
        if k - 2 >= 1:
            high_term = (by_x, half)
        if k > 1:
            low_term = [(sums[k - 1][0], 0), (by_x, 0)]
    (own,) = run(packed)
    return combine(
        (half, [(own, 0), (by_x, 0), from_y[0]]),
        (half, [(own, half), high_term, from_y[1]]),
    )


def solution(mesh):
    in_specs = (
        P(("groups", "expert"), None),
        P(),
        P(),
        P(("groups", "expert"), None),
        P("expert", None, None),
        P("expert", None, None),
        P("expert", None, None),
    )
    out_specs = P(("groups", "expert"), None)
    chips = mesh.shape["expert"] // 2
    columns = max(1, 4 // mesh.shape["groups"])
    if columns == 2 and chips % 2 == 0:
        ring = list(range(0, chips, 2)) + list(range(chips - 1, 0, -2))
    else:
        ring = list(range(chips))
    return jax.shard_map(
        functools.partial(local, ring),
        mesh=mesh,
        in_specs=in_specs,
        out_specs=out_specs,
        check_vma=False,
    )
```

```python
import functools

import jax
import jax.numpy as jnp
from jax import lax
from jax.experimental import pallas as pl
from jax.experimental.pallas import tpu as pltpu
from jax.sharding import PartitionSpec as P

MIB = 1 << 20


def pack_kernel(x_ref, gain_ref, router_ref, ids_ref, out_ref):
    rows, width = x_ref.shape
    num_experts = router_ref.shape[0]
    as_float = x_ref[...].astype(jnp.float32)
    inv_rms = lax.rsqrt(jnp.mean(as_float * as_float, axis=1, keepdims=True) + 1e-06)
    normed = (as_float * inv_rms * gain_ref[...]).astype(jnp.bfloat16)
    out_ref[:, :width] = normed
    logits = lax.dot_general(
        router_ref[...], normed, (((1,), (1,)), ((), ())), preferred_element_type=jnp.float32
    )
    ids = ids_ref[...]
    expert = lax.broadcasted_iota(jnp.int32, (num_experts, rows), 0)
    named = expert == ids[0:1, :]
    for k in range(1, ids.shape[0]):
        named = named | (expert == ids[k : k + 1, :])
    picked = jnp.where(named, jnp.exp(logits), 0.0)
    weight = picked / jnp.sum(picked, axis=0, keepdims=True)
    high = weight.astype(jnp.bfloat16).astype(jnp.float32)
    parts = [high, weight - high]
    spare = out_ref.shape[1] - width - 2 * num_experts
    if spare:
        parts.append(jnp.zeros((spare, rows), jnp.float32))
    out_ref[:, width:] = jnp.concatenate(parts, axis=0).T.astype(jnp.bfloat16)


def pack(hidden_in, norm_gain, router_weight, expert_ids):
    rows, width = hidden_in.shape
    lanes = -(-2 * router_weight.shape[1] // 128) * 128
    return pl.pallas_call(
        pack_kernel,
        out_shape=jax.ShapeDtypeStruct((rows, width + lanes), jnp.bfloat16),
        compiler_params=pltpu.CompilerParams(vmem_limit_bytes=16 * MIB),
        name="pack_rows",
    )(hidden_in, norm_gain[None, :], router_weight.T, expert_ids.T)


def ffn_kernel(heights, splits, *refs):
    count = len(heights)
    shards = refs[:count]
    gate_ref, up_ref, down_ref, mine_ref = refs[count : count + 4]
    outs = refs[count + 4 : count + 4 + len(splits)]
    x_ref, hidden_ref, weight_ref = refs[-3:]
    width, depth = gate_ref.shape
    top = 0
    for shard, height in zip(shards, heights):
        x_ref[top : top + height, :] = shard[:, :width]
        parts = shard[:, width:].astype(jnp.float32) * mine_ref[...]
        weight_ref[top : top + height, :] = jnp.sum(parts, axis=1, keepdims=True)
        top += height
    tile = 256 if depth % 256 == 0 else depth

    @pl.loop(0, depth // tile)
    def _(j):
        at = pl.ds(pl.multiple_of(j * tile, tile), tile)
        gate_act = jnp.dot(x_ref[...], gate_ref[:, at], preferred_element_type=jnp.float32)
        up_act = jnp.dot(x_ref[...], up_ref[:, at], preferred_element_type=jnp.float32)
        hidden = gate_act / (1.0 + jnp.exp(-gate_act)) * up_act
        hidden_ref[:, at] = hidden.astype(jnp.bfloat16)

    step = 512 if width % 512 == 0 else width

    @pl.loop(0, width // step)
    def _(j):
        at = pl.ds(pl.multiple_of(j * step, step), step)
        out = jnp.dot(hidden_ref[...], down_ref[:, at], preferred_element_type=jnp.float32)
        done = (out * weight_ref[...]).astype(jnp.bfloat16)
        first = 0
        for out_ref, height in zip(outs, splits):
            out_ref[:, at] = done[first : first + height]
            first += height


def ffn(shards, splits, w_gate, w_up, w_down, mine):
    width, depth = w_gate.shape
    heights = [s.shape[0] for s in shards]
    rows = sum(heights)
    return pl.pallas_call(
        functools.partial(ffn_kernel, heights, splits),
        out_shape=[jax.ShapeDtypeStruct((h, width), jnp.bfloat16) for h in splits],
        scratch_shapes=[
            pltpu.VMEM((rows, width), jnp.bfloat16),
            pltpu.VMEM((rows, depth), jnp.bfloat16),
            pltpu.VMEM((rows, 1), jnp.float32),
        ],
        compiler_params=pltpu.CompilerParams(vmem_limit_bytes=20 * MIB),
        cost_estimate=pl.CostEstimate(
            flops=6 * rows * width * depth,
            bytes_accessed=rows * width,
            transcendentals=0,
        ),
        name="expert_ffn",
    )(*shards, w_gate, w_up, w_down, mine)


def combine_kernel(parts, *refs):
    out_ref, at, top = refs[-1], 0, 0
    for height, offsets in parts:
        total = 0.0
        for offset in offsets:
            total = total + refs[at][offset : offset + height, :].astype(jnp.float32)
            at += 1
        out_ref[top : top + height, :] = total.astype(out_ref.dtype)
        top += height


def combine(*parts):
    arrays = [array for _, terms in parts for array, _ in terms]
    heights = [(height, [offset for _, offset in terms]) for height, terms in parts]
    rows = sum(height for height, _ in heights)
    return pl.pallas_call(
        functools.partial(combine_kernel, heights),
        out_shape=jax.ShapeDtypeStruct((rows, arrays[0].shape[1]), arrays[0].dtype),
        compiler_params=pltpu.CompilerParams(vmem_limit_bytes=16 * MIB),
        name="combine_rows",
    )(*arrays)


def local(ring, hidden_in, norm_gain, router_weight, expert_ids, w_gate, w_up, w_down):
    rows = hidden_in.shape[0]
    num_experts = router_weight.shape[1]
    local_experts = w_gate.shape[0]
    chips = len(ring)
    full, half = chips // 2 - 1, rows // 2
    tie = lax.optimization_barrier

    def shift(by):
        pairs = [
            (2 * ring[p] + c, 2 * ring[(p + (by if c == 0 else -by)) % chips] + c)
            for p in range(chips)
            for c in range(2)
        ]
        return lambda x: lax.ppermute(x, "expert", pairs)

    step_x, step_y = shift(1), shift(-1)
    back_x, back_y = step_y, step_x

    def sibling(x):
        return lax.ppermute(x, "expert", [(d, d ^ 1) for d in range(2 * chips)])

    packed = pack(hidden_in, norm_gain, router_weight, expert_ids)
    lane = jnp.arange(packed.shape[1] - hidden_in.shape[1], dtype=jnp.int32)[None, :]
    place = lax.axis_index("expert")

    def run(shards, splits):
        total = None
        for e in range(local_experts):
            here = place * local_experts + e
            mine = ((lane == here) | (lane == num_experts + here)).astype(jnp.float32)
            outs = ffn(shards, splits, w_gate[e], w_up[e], w_down[e], mine)
            if total is None:
                total = outs
            else:
                total = [combine((a.shape[0], [(a, 0), (b, 0)])) for a, b in zip(total, outs)]
        return total

    def near(x, y):
        return run([x, y, sibling(x), sibling(y)], [x.shape[0], y.shape[0], 2 * x.shape[0]])

    own_kept, own_sent = run([packed, sibling(packed)], [rows, rows])
    x, y, nears, sents = [packed], [packed], [None], [None]
    for k in range(1, full + 1):
        x.append(step_x(x[-1]))
        y.append(step_y(y[-1]))
        if k == 1:
            x[k], own_sent = tie((x[k], own_sent))
        elif k > 2:
            x[k], sents[k - 1] = tie((x[k], sents[k - 1]))
        *kept, sent = near(x[k], y[k])
        nears.append(kept)
        sents.append(sent)
    far_x, far_y = step_x(x[full][:half]), step_y(y[full][half:])
    far_x, far_y, sents[full] = tie((far_x, far_y, sents[full]))
    came = [None] * (full + 1)
    came[2:] = [sibling(sent) for sent in sents[2:]]

    def term(k, stream, part):
        return [
            (nears[k][stream], part * half),
            (came[k], stream * rows + part * half),
        ]

    by_x = back_x(combine((half, term(full, 0, 1))))
    far_kept_x, far_kept_y, sent = near(far_x, far_y)
    by_x, sent = tie((by_x, sent))
    far_came = sibling(sent)
    by_y = back_y(combine((half, [(far_kept_y, 0), (far_came, half)])))
    late_x = back_x(combine((half, [(far_kept_x, 0), (far_came, 0)])))
    late_x, by_y, sents[1] = tie((late_x, by_y, sents[1]))
    came[1] = sibling(sents[1])
    from_x, from_y = [[(late_x, 0)], [(by_x, 0)]], [[], [(by_y, 0)]]
    for k in range(full, 0, -1):
        halves = (0,) if k == full else (0, 1)
        by_x = back_x(combine(*[(half, term(k, 0, i) + from_x[i]) for i in halves]))
        for i in halves:
            from_x[i] = [(by_x, i * half)]
        by_y = back_y(combine(*[(half, term(k, 1, i) + from_y[i]) for i in (0, 1)]))
        from_y = [[(by_y, 0)], [(by_y, half)]]
    own_came = sibling(own_sent)
    return combine(
        *[
            (half, [(own_kept, i * half), (own_came, i * half)] + from_x[i] + from_y[i])
            for i in (0, 1)
        ]
    )


def solution(mesh):
    in_specs = (
        P(("groups", "expert"), None),
        P(),
        P(),
        P(("groups", "expert"), None),
        P("expert", None, None),
        P("expert", None, None),
        P("expert", None, None),
    )
    out_specs = P(("groups", "expert"), None)
    chips = mesh.shape["expert"] // 2
    columns = max(1, 4 // mesh.shape["groups"])
    if columns == 2 and chips % 2 == 0:
        ring = list(range(0, chips, 2)) + list(range(chips - 1, 0, -2))
    else:
        ring = list(range(chips))
    return jax.shard_map(
        functools.partial(local, ring),
        mesh=mesh,
        in_specs=in_specs,
        out_specs=out_specs,
        check_vma=False,
    )
```

```python
import functools

import jax
import jax.numpy as jnp
from jax import lax
from jax.experimental import pallas as pl
from jax.experimental.pallas import tpu as pltpu
from jax.sharding import PartitionSpec as P

MIB = 1 << 20


def pack_kernel(x_ref, gain_ref, router_ref, ids_ref, out_ref):
    rows, width = x_ref.shape
    num_experts = router_ref.shape[0]
    as_float = x_ref[...].astype(jnp.float32)
    inv_rms = lax.rsqrt(jnp.mean(as_float * as_float, axis=1, keepdims=True) + 1e-06)
    normed = (as_float * inv_rms * gain_ref[...]).astype(jnp.bfloat16)
    out_ref[:, :width] = normed
    logits = lax.dot_general(
        router_ref[...], normed, (((1,), (1,)), ((), ())), preferred_element_type=jnp.float32
    )
    ids = ids_ref[...]
    expert = lax.broadcasted_iota(jnp.int32, (num_experts, rows), 0)
    named = expert == ids[0:1, :]
    for k in range(1, ids.shape[0]):
        named = named | (expert == ids[k : k + 1, :])
    picked = jnp.where(named, jnp.exp(logits), 0.0)
    weight = picked / jnp.sum(picked, axis=0, keepdims=True)
    high = weight.astype(jnp.bfloat16).astype(jnp.float32)
    parts = [high, weight - high]
    spare = out_ref.shape[1] - width - 2 * num_experts
    if spare:
        parts.append(jnp.zeros((spare, rows), jnp.float32))
    out_ref[:, width:] = jnp.concatenate(parts, axis=0).T.astype(jnp.bfloat16)


def pack(hidden_in, norm_gain, router_weight, expert_ids):
    rows, width = hidden_in.shape
    lanes = -(-2 * router_weight.shape[1] // 128) * 128
    return pl.pallas_call(
        pack_kernel,
        out_shape=jax.ShapeDtypeStruct((rows, width + lanes), jnp.bfloat16),
        compiler_params=pltpu.CompilerParams(vmem_limit_bytes=16 * MIB),
        name="pack_rows",
    )(hidden_in, norm_gain[None, :], router_weight.T, expert_ids.T)


def ffn_kernel(heights, splits, *refs):
    count = len(heights)
    shards = refs[:count]
    gate_ref, up_ref, down_ref, mine_ref = refs[count : count + 4]
    outs = refs[count + 4 : count + 4 + len(splits)]
    x_ref, hidden_ref, weight_ref = refs[-3:]
    width, depth = gate_ref.shape
    top = 0
    for shard, height in zip(shards, heights):
        x_ref[top : top + height, :] = shard[:, :width]
        parts = shard[:, width:].astype(jnp.float32) * mine_ref[...]
        weight_ref[top : top + height, :] = jnp.sum(parts, axis=1, keepdims=True)
        top += height
    tile = 256 if depth % 256 == 0 else depth

    @pl.loop(0, depth // tile)
    def _(j):
        at = pl.ds(pl.multiple_of(j * tile, tile), tile)
        gate_act = jnp.dot(x_ref[...], gate_ref[:, at], preferred_element_type=jnp.float32)
        up_act = jnp.dot(x_ref[...], up_ref[:, at], preferred_element_type=jnp.float32)
        hidden = gate_act / (1.0 + jnp.exp(-gate_act)) * up_act
        hidden_ref[:, at] = hidden.astype(jnp.bfloat16)

    step = 512 if width % 512 == 0 else width

    @pl.loop(0, width // step)
    def _(j):
        at = pl.ds(pl.multiple_of(j * step, step), step)
        out = jnp.dot(hidden_ref[...], down_ref[:, at], preferred_element_type=jnp.float32)
        done = (out * weight_ref[...]).astype(jnp.bfloat16)
        first = 0
        for out_ref, height in zip(outs, splits):
            out_ref[:, at] = done[first : first + height]
            first += height


def ffn(shards, splits, w_gate, w_up, w_down, mine):
    width, depth = w_gate.shape
    heights = [s.shape[0] for s in shards]
    rows = sum(heights)
    return pl.pallas_call(
        functools.partial(ffn_kernel, heights, splits),
        out_shape=[jax.ShapeDtypeStruct((h, width), jnp.bfloat16) for h in splits],
        scratch_shapes=[
            pltpu.VMEM((rows, width), jnp.bfloat16),
            pltpu.VMEM((rows, depth), jnp.bfloat16),
            pltpu.VMEM((rows, 1), jnp.float32),
        ],
        compiler_params=pltpu.CompilerParams(vmem_limit_bytes=20 * MIB),
        cost_estimate=pl.CostEstimate(
            flops=6 * rows * width * depth,
            bytes_accessed=rows * width,
            transcendentals=0,
        ),
        name="expert_ffn",
    )(*shards, w_gate, w_up, w_down, mine)


def beside_kernel(x_ref, *refs):
    refs[-1][...] = x_ref[...]


def beside_weights(x, *weights):
    return pl.pallas_call(
        beside_kernel,
        out_shape=jax.ShapeDtypeStruct(x.shape, x.dtype),
        in_specs=[pl.BlockSpec(memory_space=pltpu.VMEM)] * (1 + len(weights)),
        out_specs=pl.BlockSpec(memory_space=pltpu.VMEM),
        compiler_params=pltpu.CompilerParams(vmem_limit_bytes=16 * MIB),
        name="beside_weights",
    )(x, *weights)


def combine_kernel(parts, *refs):
    out_ref, at, top = refs[-1], 0, 0
    for height, offsets in parts:
        total = 0.0
        for offset in offsets:
            total = total + refs[at][offset : offset + height, :].astype(jnp.float32)
            at += 1
        out_ref[top : top + height, :] = total.astype(out_ref.dtype)
        top += height


def combine(*parts):
    arrays = [array for _, terms in parts for array, _ in terms]
    heights = [(height, [offset for _, offset in terms]) for height, terms in parts]
    rows = sum(height for height, _ in heights)
    return pl.pallas_call(
        functools.partial(combine_kernel, heights),
        out_shape=jax.ShapeDtypeStruct((rows, arrays[0].shape[1]), arrays[0].dtype),
        compiler_params=pltpu.CompilerParams(vmem_limit_bytes=16 * MIB),
        name="combine_rows",
    )(*arrays)


def local(ring, hidden_in, norm_gain, router_weight, expert_ids, w_gate, w_up, w_down):
    rows = hidden_in.shape[0]
    num_experts = router_weight.shape[1]
    local_experts = w_gate.shape[0]
    chips = len(ring)
    full, half = chips // 2 - 1, rows // 2
    tie = lax.optimization_barrier

    def shift(by):
        pairs = [
            (2 * ring[p] + c, 2 * ring[(p + (by if c == 0 else -by)) % chips] + c)
            for p in range(chips)
            for c in range(2)
        ]
        return lambda x: lax.ppermute(x, "expert", pairs)

    step_x, step_y = shift(1), shift(-1)
    back_x, back_y = step_y, step_x

    def sibling(x):
        return lax.ppermute(x, "expert", [(d, d ^ 1) for d in range(2 * chips)])

    packed = pack(hidden_in, norm_gain, router_weight, expert_ids)
    lane = jnp.arange(packed.shape[1] - hidden_in.shape[1], dtype=jnp.int32)[None, :]
    place = lax.axis_index("expert")

    def run(shards, splits):
        total = None
        for e in range(local_experts):
            here = place * local_experts + e
            mine = ((lane == here) | (lane == num_experts + here)).astype(jnp.float32)
            outs = ffn(shards, splits, w_gate[e], w_up[e], w_down[e], mine)
            if total is None:
                total = outs
            else:
                total = [combine((a.shape[0], [(a, 0), (b, 0)])) for a, b in zip(total, outs)]
        return total

    def near(x, y):
        return run([x, y, sibling(x), sibling(y)], [x.shape[0], y.shape[0], 2 * x.shape[0]])

    other, second = tie((sibling(packed), packed))
    x, y = [packed], [beside_weights(second, w_gate, w_up, w_down)]
    for k in range(1, full + 1):
        x.append(step_x(x[-1]))
        y.append(step_y(y[-1]))
    far_x, far_y = step_x(x[full][:half]), step_y(y[full][half:])
    terms, came = [None] * (full + 1), [None] * (full + 1)
    *terms[full], sent = near(x[full], y[full])
    far_x, far_y, sent = tie((far_x, far_y, sent))
    came[full] = sibling(sent)
    far_kept_x, far_kept_y, sent = near(far_x, far_y)
    far_came = sibling(sent)

    by_x = back_x(combine((half, [(far_kept_x, 0), (far_came, 0)])))
    by_y = back_y(combine((half, [(far_kept_y, 0), (far_came, half)])))
    own_kept, sent = run([packed, other], [rows, rows])
    by_x, by_y, sent = tie((by_x, by_y, sent))
    came[0] = sibling(sent)
    from_x, from_y = [[(by_x, 0)], []], [[], [(by_y, 0)]]
    for k in range(full, 0, -1):
        hops = []
        for stream, back, arrived in ((0, back_x, from_x), (1, back_y, from_y)):
            parts = []
            for i in (0, 1):
                at = i * half
                ours = [(terms[k][stream], at), (came[k], stream * rows + at)]
                parts.append((half, ours + arrived[i]))
            hops.append(back(combine(*parts)))
        if k > 1:
            *terms[k - 1], sent = near(x[k - 1], y[k - 1])
            *hops, sent = tie((*hops, sent))
            came[k - 1] = sibling(sent)
        from_x, from_y = [[[(hop, 0)], [(hop, half)]] for hop in hops]
    return combine(
        *[
            (half, [(own_kept, i * half), (came[0], i * half)] + from_x[i] + from_y[i])
            for i in (0, 1)
        ]
    )


def solution(mesh):
    in_specs = (
        P(("groups", "expert"), None),
        P(),
        P(),
        P(("groups", "expert"), None),
        P("expert", None, None),
        P("expert", None, None),
        P("expert", None, None),
    )
    out_specs = P(("groups", "expert"), None)
    chips = mesh.shape["expert"] // 2
    columns = max(1, 4 // mesh.shape["groups"])
    if columns == 2 and chips % 2 == 0:
        ring = list(range(0, chips, 2)) + list(range(chips - 1, 0, -2))
    else:
        ring = list(range(chips))
    return jax.shard_map(
        functools.partial(local, ring),
        mesh=mesh,
        in_specs=in_specs,
        out_specs=out_specs,
        check_vma=False,
    )
```

```python
import functools

import jax
import jax.numpy as jnp
from jax import lax
from jax.experimental import pallas as pl
from jax.experimental.pallas import tpu as pltpu
from jax.sharding import PartitionSpec as P

MIB = 1 << 20


def pack_kernel(x_ref, gain_ref, router_ref, ids_ref, out_ref):
    rows, width = x_ref.shape
    num_experts = router_ref.shape[0]
    as_float = x_ref[...].astype(jnp.float32)
    inv_rms = lax.rsqrt(jnp.mean(as_float * as_float, axis=1, keepdims=True) + 1e-06)
    normed = (as_float * inv_rms * gain_ref[...]).astype(jnp.bfloat16)
    out_ref[:, :width] = normed
    logits = lax.dot_general(
        router_ref[...], normed, (((1,), (1,)), ((), ())), preferred_element_type=jnp.float32
    )
    ids = ids_ref[...]
    expert = lax.broadcasted_iota(jnp.int32, (num_experts, rows), 0)
    named = expert == ids[0:1, :]
    for k in range(1, ids.shape[0]):
        named = named | (expert == ids[k : k + 1, :])
    picked = jnp.where(named, jnp.exp(logits), 0.0)
    weight = picked / jnp.sum(picked, axis=0, keepdims=True)
    high = weight.astype(jnp.bfloat16).astype(jnp.float32)
    parts = [high, weight - high]
    spare = out_ref.shape[1] - width - 2 * num_experts
    if spare:
        parts.append(jnp.zeros((spare, rows), jnp.float32))
    out_ref[:, width:] = jnp.concatenate(parts, axis=0).T.astype(jnp.bfloat16)


def pack(hidden_in, norm_gain, router_weight, expert_ids):
    rows, width = hidden_in.shape
    lanes = -(-2 * router_weight.shape[1] // 128) * 128
    return pl.pallas_call(
        pack_kernel,
        out_shape=jax.ShapeDtypeStruct((rows, width + lanes), jnp.bfloat16),
        compiler_params=pltpu.CompilerParams(vmem_limit_bytes=16 * MIB),
        name="pack_rows",
    )(hidden_in, norm_gain[None, :], router_weight.T, expert_ids.T)


def ffn_kernel(heights, splits, *refs):
    count = len(heights)
    shards = refs[:count]
    gate_ref, up_ref, down_ref, mine_ref = refs[count : count + 4]
    outs = refs[count + 4 : count + 4 + len(splits)]
    x_ref, hidden_ref, weight_ref = refs[-3:]
    width, depth = gate_ref.shape
    top = 0
    for shard, height in zip(shards, heights):
        x_ref[top : top + height, :] = shard[:, :width]
        parts = shard[:, width:].astype(jnp.float32) * mine_ref[...]
        weight_ref[top : top + height, :] = jnp.sum(parts, axis=1, keepdims=True)
        top += height
    tile = 256 if depth % 256 == 0 else depth

    @pl.loop(0, depth // tile)
    def _(j):
        at = pl.ds(pl.multiple_of(j * tile, tile), tile)
        gate_act = jnp.dot(x_ref[...], gate_ref[:, at], preferred_element_type=jnp.float32)
        up_act = jnp.dot(x_ref[...], up_ref[:, at], preferred_element_type=jnp.float32)
        hidden = gate_act / (1.0 + jnp.exp(-gate_act)) * up_act
        hidden_ref[:, at] = hidden.astype(jnp.bfloat16)

    step = 512 if width % 512 == 0 else width

    @pl.loop(0, width // step)
    def _(j):
        at = pl.ds(pl.multiple_of(j * step, step), step)
        out = jnp.dot(hidden_ref[...], down_ref[:, at], preferred_element_type=jnp.float32)
        done = (out * weight_ref[...]).astype(jnp.bfloat16)
        first = 0
        for out_ref, height in zip(outs, splits):
            out_ref[:, at] = done[first : first + height]
            first += height


def ffn(shards, splits, w_gate, w_up, w_down, mine):
    width, depth = w_gate.shape
    heights = [s.shape[0] for s in shards]
    rows = sum(heights)
    return pl.pallas_call(
        functools.partial(ffn_kernel, heights, splits),
        out_shape=[jax.ShapeDtypeStruct((h, width), jnp.bfloat16) for h in splits],
        scratch_shapes=[
            pltpu.VMEM((rows, width), jnp.bfloat16),
            pltpu.VMEM((rows, depth), jnp.bfloat16),
            pltpu.VMEM((rows, 1), jnp.float32),
        ],
        compiler_params=pltpu.CompilerParams(vmem_limit_bytes=20 * MIB),
        cost_estimate=pl.CostEstimate(
            flops=6 * rows * width * depth,
            bytes_accessed=rows * width,
            transcendentals=0,
        ),
        name="expert_ffn",
    )(*shards, w_gate, w_up, w_down, mine)


def beside_kernel(x_ref, *refs):
    refs[-1][...] = x_ref[...]


def beside_weights(x, *weights):
    return pl.pallas_call(
        beside_kernel,
        out_shape=jax.ShapeDtypeStruct(x.shape, x.dtype),
        in_specs=[pl.BlockSpec(memory_space=pltpu.VMEM)] * (1 + len(weights)),
        out_specs=pl.BlockSpec(memory_space=pltpu.VMEM),
        compiler_params=pltpu.CompilerParams(vmem_limit_bytes=16 * MIB),
        name="beside_weights",
    )(x, *weights)


def join_kernel(first_ref, second_ref, out_ref):
    rows = first_ref.shape[0]
    out_ref[:rows, :] = first_ref[...]
    out_ref[rows:, :] = second_ref[...]


def join(first, second):
    rows = first.shape[0] + second.shape[0]
    return pl.pallas_call(
        join_kernel,
        out_shape=jax.ShapeDtypeStruct((rows, first.shape[1]), first.dtype),
        compiler_params=pltpu.CompilerParams(vmem_limit_bytes=16 * MIB),
        name="join_rows",
    )(first, second)


def combine_kernel(parts, *refs):
    out_ref, at, top = refs[-1], 0, 0
    for height, offsets in parts:
        total = 0.0
        for offset in offsets:
            total = total + refs[at][offset : offset + height, :].astype(jnp.float32)
            at += 1
        out_ref[top : top + height, :] = total.astype(out_ref.dtype)
        top += height


def combine(*parts):
    arrays = [array for _, terms in parts for array, _ in terms]
    heights = [(height, [offset for _, offset in terms]) for height, terms in parts]
    rows = sum(height for height, _ in heights)
    return pl.pallas_call(
        functools.partial(combine_kernel, heights),
        out_shape=jax.ShapeDtypeStruct((rows, arrays[0].shape[1]), arrays[0].dtype),
        compiler_params=pltpu.CompilerParams(vmem_limit_bytes=16 * MIB),
        name="combine_rows",
    )(*arrays)


def local(ring, hidden_in, norm_gain, router_weight, expert_ids, w_gate, w_up, w_down):
    rows = hidden_in.shape[0]
    num_experts = router_weight.shape[1]
    local_experts = w_gate.shape[0]
    chips = len(ring)
    full, half = chips // 2 - 1, rows // 2
    tie = lax.optimization_barrier

    def shift(by):
        pairs = [
            (2 * ring[p] + c, 2 * ring[(p + (by if c == 0 else -by)) % chips] + c)
            for p in range(chips)
            for c in range(2)
        ]
        return lambda x: lax.ppermute(x, "expert", pairs)

    step_x, step_y = shift(1), shift(-1)
    back_x, back_y = step_y, step_x

    def sibling(x):
        return lax.ppermute(x, "expert", [(d, d ^ 1) for d in range(2 * chips)])

    packed = pack(hidden_in, norm_gain, router_weight, expert_ids)
    lane = jnp.arange(packed.shape[1] - hidden_in.shape[1], dtype=jnp.int32)[None, :]
    place = lax.axis_index("expert")

    here = place * local_experts + jnp.arange(local_experts, dtype=jnp.int32)[:, None]
    mine = ((lane == here) | (lane == num_experts + here)).astype(jnp.float32)

    def run(shards, splits):
        total = None
        for e in range(local_experts):
            outs = ffn(shards, splits, w_gate[e], w_up[e], w_down[e], mine[e : e + 1])
            if total is None:
                total = outs
            else:
                total = [combine((a.shape[0], [(a, 0), (b, 0)])) for a, b in zip(total, outs)]
        return total

    def near(x, y):
        return run([x, y, sibling(x), sibling(y)], [x.shape[0], y.shape[0], x.shape[0] + y.shape[0]])

    other, packed = tie((sibling(packed), packed))
    x, y = [packed, step_x(packed[:half])], [packed, step_y(packed)]
    mine = beside_weights(mine, w_gate, w_up, w_down)
    x[1], mine = tie((x[1], mine))
    for k in range(2, full + 2):
        x.append(step_x(join(x[1], packed[half:]) if k == 2 else x[-1]))
        y.append(step_y(y[-1] if k <= full else y[-1][half:]))

    results = {}

    def call(k):
        results[k] = near(x[k], y[k]) if k else run([packed, other], [rows, rows])
        return results[k][-1]

    def tied(hop, k):
        hop, sent = tie((hop, call(k)))
        results[k] = [*results[k][:-1], sibling(sent)]
        return hop

    x[full + 1] = tied(x[full + 1], full)
    results[full + 1] = [*near(x[full + 1], y[full + 1])]
    results[full + 1][-1] = sibling(results[full + 1][-1])
    from_x, from_y = [[], []], [[], []]
    for k in range(full + 1, 0, -1):
        kept_x, kept_y, came = results[k]
        halves_x, halves_y = (0,) if k == 1 else (0, 1), (1,) if k > full else (0, 1)
        parts_x, parts_y = [], []
        for at, i in enumerate(halves_x):
            parts_x.append((half, [(kept_x, at * half), (came, at * half)] + from_x[i]))
        for at, i in enumerate(halves_y):
            top = x[k].shape[0] + at * half
            parts_y.append((half, [(kept_y, at * half), (came, top)] + from_y[i]))
        by_x, by_y = back_x(combine(*parts_x)), back_y(combine(*parts_y))
        if k > 1:
            if k > full:
                by_y = tied(by_y, k - 2)
            else:
                by_x = tied(by_x, k - 2)
        for at, i in enumerate(halves_x):
            from_x[i] = [(by_x, at * half)]
        for at, i in enumerate(halves_y):
            from_y[i] = [(by_y, at * half)]
    own_kept, own_came = results[0]
    return combine(
        *[
            (half, [(own_kept, i * half), (own_came, i * half)] + from_x[i] + from_y[i])
            for i in (0, 1)
        ]
    )


def solution(mesh):
    in_specs = (
        P(("groups", "expert"), None),
        P(),
        P(),
        P(("groups", "expert"), None),
        P("expert", None, None),
        P("expert", None, None),
        P("expert", None, None),
    )
    out_specs = P(("groups", "expert"), None)
    chips = mesh.shape["expert"] // 2
    columns = max(1, 4 // mesh.shape["groups"])
    if columns == 2 and chips % 2 == 0:
        ring = list(range(0, chips, 2)) + list(range(chips - 1, 0, -2))
    else:
        ring = list(range(chips))
    return jax.shard_map(
        functools.partial(local, ring),
        mesh=mesh,
        in_specs=in_specs,
        out_specs=out_specs,
        check_vma=False,
    )
```

```python
import functools

import jax
import jax.numpy as jnp
from jax import lax
from jax.experimental import pallas as pl
from jax.experimental.pallas import tpu as pltpu
from jax.sharding import PartitionSpec as P

MIB = 1 << 20


def pack_kernel(x_ref, gain_ref, router_ref, ids_ref, out_ref):
    rows, width = x_ref.shape
    num_experts = router_ref.shape[0]
    as_float = x_ref[...].astype(jnp.float32)
    inv_rms = lax.rsqrt(jnp.mean(as_float * as_float, axis=1, keepdims=True) + 1e-06)
    normed = (as_float * inv_rms * gain_ref[...]).astype(jnp.bfloat16)
    out_ref[:, :width] = normed
    logits = lax.dot_general(
        router_ref[...], normed, (((1,), (1,)), ((), ())), preferred_element_type=jnp.float32
    )
    ids = ids_ref[...]
    expert = lax.broadcasted_iota(jnp.int32, (num_experts, rows), 0)
    named = expert == ids[0:1, :]
    for k in range(1, ids.shape[0]):
        named = named | (expert == ids[k : k + 1, :])
    picked = jnp.where(named, jnp.exp(logits), 0.0)
    weight = picked / jnp.sum(picked, axis=0, keepdims=True)
    high = weight.astype(jnp.bfloat16).astype(jnp.float32)
    parts = [high, weight - high]
    spare = out_ref.shape[1] - width - 2 * num_experts
    if spare:
        parts.append(jnp.zeros((spare, rows), jnp.float32))
    out_ref[:, width:] = jnp.concatenate(parts, axis=0).T.astype(jnp.bfloat16)


def pack(hidden_in, norm_gain, router_weight, expert_ids):
    rows, width = hidden_in.shape
    lanes = -(-2 * router_weight.shape[1] // 128) * 128
    return pl.pallas_call(
        pack_kernel,
        out_shape=jax.ShapeDtypeStruct((rows, width + lanes), jnp.bfloat16),
        compiler_params=pltpu.CompilerParams(vmem_limit_bytes=16 * MIB),
        name="pack_rows",
    )(hidden_in, norm_gain[None, :], router_weight.T, expert_ids.T)


def ffn_kernel(heights, splits, *refs):
    count = len(heights)
    shards = refs[:count]
    gate_ref, up_ref, down_ref, mine_ref = refs[count : count + 4]
    outs = refs[count + 4 : count + 4 + len(splits)]
    x_ref, hidden_ref, weight_ref = refs[-3:]
    width, depth = gate_ref.shape
    top = 0
    for shard, height in zip(shards, heights):
        x_ref[top : top + height, :] = shard[:, :width]
        parts = shard[:, width:].astype(jnp.float32) * mine_ref[...]
        weight_ref[top : top + height, :] = jnp.sum(parts, axis=1, keepdims=True)
        top += height
    tile = 256 if depth % 256 == 0 else depth

    @pl.loop(0, depth // tile)
    def _(j):
        at = pl.ds(pl.multiple_of(j * tile, tile), tile)
        gate_act = jnp.dot(x_ref[...], gate_ref[:, at], preferred_element_type=jnp.float32)
        up_act = jnp.dot(x_ref[...], up_ref[:, at], preferred_element_type=jnp.float32)
        hidden = gate_act / (1.0 + jnp.exp(-gate_act)) * up_act
        hidden_ref[:, at] = hidden.astype(jnp.bfloat16)

    step = 512 if width % 512 == 0 else width

    @pl.loop(0, width // step)
    def _(j):
        at = pl.ds(pl.multiple_of(j * step, step), step)
        out = jnp.dot(hidden_ref[...], down_ref[:, at], preferred_element_type=jnp.float32)
        done = (out * weight_ref[...]).astype(jnp.bfloat16)
        first = 0
        for out_ref, height in zip(outs, splits):
            out_ref[:, at] = done[first : first + height]
            first += height


def ffn(shards, splits, w_gate, w_up, w_down, mine):
    width, depth = w_gate.shape
    heights = [s.shape[0] for s in shards]
    rows = sum(heights)
    return pl.pallas_call(
        functools.partial(ffn_kernel, heights, splits),
        out_shape=[jax.ShapeDtypeStruct((h, width), jnp.bfloat16) for h in splits],
        scratch_shapes=[
            pltpu.VMEM((rows, width), jnp.bfloat16),
            pltpu.VMEM((rows, depth), jnp.bfloat16),
            pltpu.VMEM((rows, 1), jnp.float32),
        ],
        compiler_params=pltpu.CompilerParams(vmem_limit_bytes=20 * MIB),
        cost_estimate=pl.CostEstimate(
            flops=6 * rows * width * depth,
            bytes_accessed=rows * width,
            transcendentals=0,
        ),
        name="expert_ffn",
    )(*shards, w_gate, w_up, w_down, mine)


def combine_kernel(parts, *refs):
    out_ref, at, top = refs[-1], 0, 0
    for height, offsets in parts:
        total = 0.0
        for offset in offsets:
            total = total + refs[at][offset : offset + height, :].astype(jnp.float32)
            at += 1
        out_ref[top : top + height, :] = total.astype(out_ref.dtype)
        top += height


def combine(*parts):
    arrays = [array for _, terms in parts for array, _ in terms]
    heights = [(height, [offset for _, offset in terms]) for height, terms in parts]
    rows = sum(height for height, _ in heights)
    return pl.pallas_call(
        functools.partial(combine_kernel, heights),
        out_shape=jax.ShapeDtypeStruct((rows, arrays[0].shape[1]), arrays[0].dtype),
        compiler_params=pltpu.CompilerParams(vmem_limit_bytes=16 * MIB),
        name="combine_rows",
    )(*arrays)


def local(ring, hidden_in, norm_gain, router_weight, expert_ids, w_gate, w_up, w_down):
    rows = hidden_in.shape[0]
    num_experts = router_weight.shape[1]
    local_experts = w_gate.shape[0]
    chips = len(ring)
    full, half = chips // 2 - 1, rows // 2
    tie = lax.optimization_barrier

    def shift(by):
        pairs = [
            (2 * ring[p] + c, 2 * ring[(p + by) % chips] + c)
            for p in range(chips)
            for c in range(2)
        ]
        return lambda x: lax.ppermute(x, "expert", pairs)

    step_x, step_y = shift(1), shift(-1)
    back_x, back_y = step_y, step_x

    def sibling(x):
        return lax.ppermute(x, "expert", [(d, d ^ 1) for d in range(2 * chips)])

    packed = pack(hidden_in, norm_gain, router_weight, expert_ids)
    lane = jnp.arange(packed.shape[1] - hidden_in.shape[1], dtype=jnp.int32)[None, :]
    place = lax.axis_index("expert")

    def run(shards, splits):
        total = None
        for e in range(local_experts):
            here = place * local_experts + e
            mine = ((lane == here) | (lane == num_experts + here)).astype(jnp.float32)
            outs = ffn(shards, splits, w_gate[e], w_up[e], w_down[e], mine)
            if total is None:
                total = outs
            else:
                total = [combine((a.shape[0], [(a, 0), (b, 0)])) for a, b in zip(total, outs)]
        return total

    def near(x, y):
        return run([x, y, sibling(x), sibling(y)], [x.shape[0], y.shape[0], 2 * x.shape[0]])

    own_kept, sent = run([packed, sibling(packed)], [rows, rows])
    x, y = [packed], [packed]
    for k in range(1, full + 1):
        x.append(step_x(x[-1]))
        y.append(step_y(y[-1]))
        if k == 1:
            x[k], y[k], sent = tie((x[k], y[k], sent))
            own_came = sibling(sent)
    far_x, far_y = step_x(x[full][:half]), step_y(y[full][half:])
    terms, came = [None] * (full + 1), [None] * (full + 1)
    *terms[full], sent = near(x[full], y[full])
    far_x, far_y, sent = tie((far_x, far_y, sent))
    came[full] = sibling(sent)
    far_kept_x, far_kept_y, sent = near(far_x, far_y)
    far_came = sibling(sent)

    def beside(hops, k):
        if k < 1:
            return hops
        *terms[k], sent = near(x[k], y[k])
        *hops, sent = tie((*hops, sent))
        came[k] = sibling(sent)
        return hops

    by_x = back_x(combine((half, [(far_kept_x, 0), (far_came, 0)])))
    by_y = back_y(combine((half, [(far_kept_y, 0), (far_came, half)])))
    by_x, by_y = beside((by_x, by_y), full - 1)
    from_x, from_y = [[(by_x, 0)], []], [[], [(by_y, 0)]]
    for k in range(full, 0, -1):
        hops = []
        for stream, back, arrived in ((0, back_x, from_x), (1, back_y, from_y)):
            parts = []
            for i in (0, 1):
                at = i * half
                ours = [(terms[k][stream], at), (came[k], stream * rows + at)]
                parts.append((half, ours + arrived[i]))
            hops.append(back(combine(*parts)))
        hops = beside(hops, k - 2)
        from_x, from_y = [[[(hop, 0)], [(hop, half)]] for hop in hops]
    return combine(
        *[
            (half, [(own_kept, i * half), (own_came, i * half)] + from_x[i] + from_y[i])
            for i in (0, 1)
        ]
    )


def solution(mesh):
    in_specs = (
        P(("groups", "expert"), None),
        P(),
        P(),
        P(("groups", "expert"), None),
        P("expert", None, None),
        P("expert", None, None),
        P("expert", None, None),
    )
    out_specs = P(("groups", "expert"), None)
    chips = mesh.shape["expert"] // 2
    columns = max(1, 4 // mesh.shape["groups"])
    if columns == 2 and chips % 2 == 0:
        ring = list(range(0, chips, 2)) + list(range(chips - 1, 0, -2))
    else:
        ring = list(range(chips))
    return jax.shard_map(
        functools.partial(local, ring),
        mesh=mesh,
        in_specs=in_specs,
        out_specs=out_specs,
        check_vma=False,
    )
```

```python
import functools

import jax
import jax.numpy as jnp
from jax import lax
from jax.experimental import pallas as pl
from jax.experimental.pallas import tpu as pltpu
from jax.sharding import PartitionSpec as P

MIB = 1 << 20


def pack_kernel(x_ref, gain_ref, router_ref, ids_ref, *outs):
    rows, width = x_ref.shape
    num_experts = router_ref.shape[0]
    as_float = x_ref[...].astype(jnp.float32)
    inv_rms = lax.rsqrt(jnp.mean(as_float * as_float, axis=1, keepdims=True) + 1e-06)
    normed = (as_float * inv_rms * gain_ref[...]).astype(jnp.bfloat16)
    half = rows // 2
    ranges = [(0, rows), (0, half), (half, rows)]
    for (low, high), out_ref in zip(ranges, outs):
        out_ref[:, :width] = normed[low:high]
    logits = lax.dot_general(
        router_ref[...], normed, (((1,), (1,)), ((), ())), preferred_element_type=jnp.float32
    )
    ids = ids_ref[...]
    expert = lax.broadcasted_iota(jnp.int32, (num_experts, rows), 0)
    named = expert == ids[0:1, :]
    for k in range(1, ids.shape[0]):
        named = named | (expert == ids[k : k + 1, :])
    picked = jnp.where(named, jnp.exp(logits), 0.0)
    weight = picked / jnp.sum(picked, axis=0, keepdims=True)
    high = weight.astype(jnp.bfloat16).astype(jnp.float32)
    parts = [high, weight - high]
    spare = outs[0].shape[1] - width - 2 * num_experts
    if spare:
        parts.append(jnp.zeros((spare, rows), jnp.float32))
    beside = jnp.concatenate(parts, axis=0).T.astype(jnp.bfloat16)
    for (low, high), out_ref in zip(ranges, outs):
        out_ref[:, width:] = beside[low:high]


def pack(hidden_in, norm_gain, router_weight, expert_ids):
    rows, width = hidden_in.shape
    lanes = -(-2 * router_weight.shape[1] // 128) * 128
    return pl.pallas_call(
        pack_kernel,
        out_shape=[
            jax.ShapeDtypeStruct((r, width + lanes), jnp.bfloat16)
            for r in (rows, rows // 2, rows // 2)
        ],
        compiler_params=pltpu.CompilerParams(vmem_limit_bytes=16 * MIB),
        name="pack_rows",
    )(hidden_in, norm_gain[None, :], router_weight.T, expert_ids.T)


def ffn_kernel(heights, splits, *refs):
    count = len(heights)
    shards = refs[:count]
    gate_ref, up_ref, down_ref, mine_ref = refs[count : count + 4]
    outs = refs[count + 4 : count + 4 + len(splits)]
    x_ref, hidden_ref, weight_ref = refs[-3:]
    width, depth = gate_ref.shape
    top = 0
    for shard, height in zip(shards, heights):
        x_ref[top : top + height, :] = shard[:, :width]
        parts = shard[:, width:].astype(jnp.float32) * mine_ref[...]
        weight_ref[top : top + height, :] = jnp.sum(parts, axis=1, keepdims=True)
        top += height
    tile = 256 if depth % 256 == 0 else depth

    @pl.loop(0, depth // tile)
    def _(j):
        at = pl.ds(pl.multiple_of(j * tile, tile), tile)
        gate_act = jnp.dot(x_ref[...], gate_ref[:, at], preferred_element_type=jnp.float32)
        up_act = jnp.dot(x_ref[...], up_ref[:, at], preferred_element_type=jnp.float32)
        hidden = gate_act / (1.0 + jnp.exp(-gate_act)) * up_act
        hidden_ref[:, at] = hidden.astype(jnp.bfloat16)

    step = 512 if width % 512 == 0 else width

    @pl.loop(0, width // step)
    def _(j):
        at = pl.ds(pl.multiple_of(j * step, step), step)
        out = jnp.dot(hidden_ref[...], down_ref[:, at], preferred_element_type=jnp.float32)
        done = (out * weight_ref[...]).astype(jnp.bfloat16)
        first = 0
        for out_ref, height in zip(outs, splits):
            out_ref[:, at] = done[first : first + height]
            first += height


def ffn(shards, splits, w_gate, w_up, w_down, mine):
    width, depth = w_gate.shape
    heights = [s.shape[0] for s in shards]
    rows = sum(heights)
    return pl.pallas_call(
        functools.partial(ffn_kernel, heights, splits),
        out_shape=[jax.ShapeDtypeStruct((h, width), jnp.bfloat16) for h in splits],
        scratch_shapes=[
            pltpu.VMEM((rows, width), jnp.bfloat16),
            pltpu.VMEM((rows, depth), jnp.bfloat16),
            pltpu.VMEM((rows, 1), jnp.float32),
        ],
        compiler_params=pltpu.CompilerParams(vmem_limit_bytes=20 * MIB),
        cost_estimate=pl.CostEstimate(
            flops=6 * rows * width * depth,
            bytes_accessed=rows * width,
            transcendentals=0,
        ),
        name="expert_ffn",
    )(*shards, w_gate, w_up, w_down, mine)


def beside_kernel(x_ref, *refs):
    refs[-1][...] = x_ref[...]


def beside_weights(x, *weights):
    return pl.pallas_call(
        beside_kernel,
        out_shape=jax.ShapeDtypeStruct(x.shape, x.dtype),
        in_specs=[pl.BlockSpec(memory_space=pltpu.VMEM)] * (1 + len(weights)),
        out_specs=pl.BlockSpec(memory_space=pltpu.VMEM),
        compiler_params=pltpu.CompilerParams(vmem_limit_bytes=16 * MIB),
        name="beside_weights",
    )(x, *weights)


def join_kernel(*refs):
    out_ref, top = refs[-1], 0
    for ref in refs[:-1]:
        out_ref[top : top + ref.shape[0], :] = ref[...]
        top += ref.shape[0]


def join(arrays):
    rows = sum(a.shape[0] for a in arrays)
    return pl.pallas_call(
        join_kernel,
        out_shape=jax.ShapeDtypeStruct((rows, arrays[0].shape[1]), arrays[0].dtype),
        compiler_params=pltpu.CompilerParams(vmem_limit_bytes=16 * MIB),
        name="join_rows",
    )(*arrays)


def combine_kernel(parts, *refs):
    out_ref, at, top = refs[-1], 0, 0
    for height, offsets in parts:
        total = 0.0
        for offset in offsets:
            total = total + refs[at][offset : offset + height, :].astype(jnp.float32)
            at += 1
        out_ref[top : top + height, :] = total.astype(out_ref.dtype)
        top += height


def combine(*parts):
    arrays = [array for _, terms in parts for array, _ in terms]
    heights = [(height, [offset for _, offset in terms]) for height, terms in parts]
    rows = sum(height for height, _ in heights)
    return pl.pallas_call(
        functools.partial(combine_kernel, heights),
        out_shape=jax.ShapeDtypeStruct((rows, arrays[0].shape[1]), arrays[0].dtype),
        compiler_params=pltpu.CompilerParams(vmem_limit_bytes=16 * MIB),
        name="combine_rows",
    )(*arrays)


def local(ring, hidden_in, norm_gain, router_weight, expert_ids, w_gate, w_up, w_down):
    rows = hidden_in.shape[0]
    num_experts = router_weight.shape[1]
    local_experts = w_gate.shape[0]
    chips = len(ring)
    full, half = chips // 2 - 1, rows // 2
    tie = lax.optimization_barrier

    def shift(by):
        pairs = [
            (2 * ring[p] + c, 2 * ring[(p + by) % chips] + c)
            for p in range(chips)
            for c in range(2)
        ]
        return lambda x: lax.ppermute(x, "expert", pairs)

    ahead, behind = shift(1), shift(-1)

    def sibling(x):
        return lax.ppermute(x, "expert", [(d, d ^ 1) for d in range(2 * chips)])

    packed, first, second = pack(hidden_in, norm_gain, router_weight, expert_ids)
    lane = jnp.arange(packed.shape[1] - hidden_in.shape[1], dtype=jnp.int32)[None, :]
    place = lax.axis_index("expert")

    here = place * local_experts + jnp.arange(local_experts, dtype=jnp.int32)[:, None]
    mine = ((lane == here) | (lane == num_experts + here)).astype(jnp.float32)

    def run(shards, splits):
        total = None
        for e in range(local_experts):
            outs = ffn(shards, splits, w_gate[e], w_up[e], w_down[e], mine[e : e + 1])
            if total is None:
                total = outs
            else:
                total = [combine((a.shape[0], [(a, 0), (b, 0)])) for a, b in zip(total, outs)]
        return total

    def near(ours, theirs, count):
        return run([ours, theirs], [half] * count + [half * count])

    mine = beside_weights(mine, w_gate, w_up, w_down)
    long_a, long_b, short_a, short_b = [first], [second], [first], [second]
    for k in range(1, full + 2):
        long_a.append(ahead(long_a[-1]))
        long_b.append(behind(long_b[-1]))
        if k <= full:
            short_a.append(behind(short_a[-1]))
            short_b.append(ahead(short_b[-1]))
        if k == 1:
            long_a[1], long_b[1], mine = tie((long_a[1], long_b[1], mine))
            own_kept, sent = run([packed, sibling(packed)], [rows, rows])
        elif k == 2:
            long_a[2], long_b[2], sent = tie((long_a[2], long_b[2], sent))
            own_came = sibling(sent)

    def slot(k):
        ours = join([long_a[k], short_b[k], short_a[k], long_b[k]])
        return near(ours, sibling(ours), 4)

    terms, came = [None] * (full + 1), [None] * (full + 1)
    *terms[full], sent = slot(full)
    far_a, far_b, sent = tie((long_a[-1], long_b[-1], sent))
    came[full] = sibling(sent)
    far = join([far_a, far_b])
    far_a, far_b, far_sent = near(far, sibling(far), 2)

    def part(k, i, *more):
        return combine((half, [(terms[k][i], 0), (came[k], i * half), *((m, 0) for m in more)]))

    def beside(hops, k):
        if k < 1:
            return hops
        *terms[k], sent = slot(k)
        *hops, sent = tie((*hops, sent))
        came[k] = sibling(sent)
        return hops

    by_short_b, by_short_a = behind(part(full, 1)), ahead(part(full, 2))
    by_short_b, by_short_a, far_sent = tie((by_short_b, by_short_a, far_sent))
    far_came = sibling(far_sent)
    by_long_a = behind(combine((half, [(far_a, 0), (far_came, 0)])))
    by_long_b = ahead(combine((half, [(far_b, 0), (far_came, half)])))
    by_long_a, by_long_b = beside((by_long_a, by_long_b), full - 1)
    for k in range(full, 0, -1):
        hops = [behind(part(k, 0, by_long_a)), ahead(part(k, 3, by_long_b))]
        if k > 1:
            hops += [behind(part(k - 1, 1, by_short_b)), ahead(part(k - 1, 2, by_short_a))]
        by_long_a, by_long_b, *shorts = beside(hops, k - 2)
        if k > 1:
            by_short_b, by_short_a = shorts
    return combine(
        (half, [(own_kept, 0), (own_came, 0), (by_long_a, 0), (by_short_a, 0)]),
        (half, [(own_kept, half), (own_came, half), (by_long_b, 0), (by_short_b, 0)]),
    )


def solution(mesh):
    in_specs = (
        P(("groups", "expert"), None),
        P(),
        P(),
        P(("groups", "expert"), None),
        P("expert", None, None),
        P("expert", None, None),
        P("expert", None, None),
    )
    out_specs = P(("groups", "expert"), None)
    chips = mesh.shape["expert"] // 2
    columns = max(1, 4 // mesh.shape["groups"])
    if columns == 2 and chips % 2 == 0:
        ring = list(range(0, chips, 2)) + list(range(chips - 1, 0, -2))
    else:
        ring = list(range(chips))
    return jax.shard_map(
        functools.partial(local, ring),
        mesh=mesh,
        in_specs=in_specs,
        out_specs=out_specs,
        check_vma=False,
    )
```

```python
import functools

import jax
import jax.numpy as jnp
from jax import lax
from jax.experimental import pallas as pl
from jax.experimental.pallas import tpu as pltpu
from jax.sharding import PartitionSpec as P

MIB = 1 << 20


def pack_kernel(*refs):
    sources, outs, held, sems = refs[:4], refs[4:-5], refs[-5:-1], refs[-1]
    copies = [
        pltpu.make_async_copy(source, place, sems.at[i])
        for i, (source, place) in enumerate(zip(sources, held))
    ]
    for copy in copies:
        copy.start()
    for copy in copies:
        copy.wait()
    x_ref, gain_ref, router_ref, ids_ref = held
    rows, width = x_ref.shape
    num_experts = router_ref.shape[0]
    as_float = x_ref[...].astype(jnp.float32)
    inv_rms = lax.rsqrt(jnp.mean(as_float * as_float, axis=1, keepdims=True) + 1e-06)
    normed = (as_float * inv_rms * gain_ref[...]).astype(jnp.bfloat16)
    half = rows // 2
    ranges = [(0, rows), (0, half), (half, rows)]
    for (low, high), out_ref in zip(ranges, outs):
        out_ref[:, :width] = normed[low:high]
    logits = lax.dot_general(
        router_ref[...], normed, (((1,), (1,)), ((), ())), preferred_element_type=jnp.float32
    )
    ids = ids_ref[...]
    expert = lax.broadcasted_iota(jnp.int32, (num_experts, rows), 0)
    named = expert == ids[0:1, :]
    for k in range(1, ids.shape[0]):
        named = named | (expert == ids[k : k + 1, :])
    picked = jnp.where(named, jnp.exp(logits), 0.0)
    weight = picked / jnp.sum(picked, axis=0, keepdims=True)
    high = weight.astype(jnp.bfloat16).astype(jnp.float32)
    parts = [high, weight - high]
    spare = outs[0].shape[1] - width - 2 * num_experts
    if spare:
        parts.append(jnp.zeros((spare, rows), jnp.float32))
    beside = jnp.concatenate(parts, axis=0).T.astype(jnp.bfloat16)
    for (low, high), out_ref in zip(ranges, outs):
        out_ref[:, width:] = beside[low:high]


def pack(hidden_in, norm_gain, router_weight, expert_ids):
    rows, width = hidden_in.shape
    lanes = -(-2 * router_weight.shape[1] // 128) * 128
    sources = [hidden_in, norm_gain[None, :], router_weight.T, expert_ids.T]
    return pl.pallas_call(
        pack_kernel,
        out_shape=[
            jax.ShapeDtypeStruct((r, width + lanes), jnp.bfloat16)
            for r in (rows, rows // 2, rows // 2)
        ],
        in_specs=[pl.BlockSpec(memory_space=pl.ANY)] * len(sources),
        scratch_shapes=[pltpu.VMEM(a.shape, a.dtype) for a in sources]
        + [pltpu.SemaphoreType.DMA((len(sources),))],
        compiler_params=pltpu.CompilerParams(vmem_limit_bytes=58 * MIB),
        name="pack_rows",
    )(*sources)


def ffn_kernel(heights, splits, *refs):
    count = len(heights)
    shards = refs[:count]
    gate_ref, up_ref, down_ref, mine_ref = refs[count : count + 4]
    outs = refs[count + 4 : count + 4 + len(splits)]
    x_ref, hidden_ref, weight_ref = refs[-3:]
    width, depth = gate_ref.shape
    top = 0
    for shard, height in zip(shards, heights):
        x_ref[top : top + height, :] = shard[:, :width]
        parts = shard[:, width:].astype(jnp.float32) * mine_ref[...]
        weight_ref[top : top + height, :] = jnp.sum(parts, axis=1, keepdims=True)
        top += height
    tile = 256 if depth % 256 == 0 else depth

    @pl.loop(0, depth // tile)
    def _(j):
        at = pl.ds(pl.multiple_of(j * tile, tile), tile)
        gate_act = jnp.dot(x_ref[...], gate_ref[:, at], preferred_element_type=jnp.float32)
        up_act = jnp.dot(x_ref[...], up_ref[:, at], preferred_element_type=jnp.float32)
        hidden = gate_act / (1.0 + jnp.exp(-gate_act)) * up_act
        hidden_ref[:, at] = hidden.astype(jnp.bfloat16)

    step = 512 if width % 512 == 0 else width

    @pl.loop(0, width // step)
    def _(j):
        at = pl.ds(pl.multiple_of(j * step, step), step)
        out = jnp.dot(hidden_ref[...], down_ref[:, at], preferred_element_type=jnp.float32)
        done = (out * weight_ref[...]).astype(jnp.bfloat16)
        first = 0
        for out_ref, height in zip(outs, splits):
            out_ref[:, at] = done[first : first + height]
            first += height


def ffn(shards, splits, w_gate, w_up, w_down, mine):
    width, depth = w_gate.shape
    heights = [s.shape[0] for s in shards]
    rows = sum(heights)
    return pl.pallas_call(
        functools.partial(ffn_kernel, heights, splits),
        out_shape=[jax.ShapeDtypeStruct((h, width), jnp.bfloat16) for h in splits],
        scratch_shapes=[
            pltpu.VMEM((rows, width), jnp.bfloat16),
            pltpu.VMEM((rows, depth), jnp.bfloat16),
            pltpu.VMEM((rows, 1), jnp.float32),
        ],
        compiler_params=pltpu.CompilerParams(vmem_limit_bytes=20 * MIB),
        cost_estimate=pl.CostEstimate(
            flops=6 * rows * width * depth,
            bytes_accessed=rows * width,
            transcendentals=0,
        ),
        name="expert_ffn",
    )(*shards, w_gate, w_up, w_down, mine)


def beside_kernel(x_ref, *refs):
    refs[-1][...] = x_ref[...]


def beside_weights(x, *weights):
    return pl.pallas_call(
        beside_kernel,
        out_shape=jax.ShapeDtypeStruct(x.shape, x.dtype),
        in_specs=[pl.BlockSpec(memory_space=pltpu.VMEM)] * (1 + len(weights)),
        out_specs=pl.BlockSpec(memory_space=pltpu.VMEM),
        compiler_params=pltpu.CompilerParams(vmem_limit_bytes=16 * MIB),
        name="beside_weights",
    )(x, *weights)


def join_kernel(*refs):
    out_ref, top = refs[-1], 0
    for ref in refs[:-1]:
        out_ref[top : top + ref.shape[0], :] = ref[...]
        top += ref.shape[0]


def join(arrays):
    rows = sum(a.shape[0] for a in arrays)
    return pl.pallas_call(
        join_kernel,
        out_shape=jax.ShapeDtypeStruct((rows, arrays[0].shape[1]), arrays[0].dtype),
        compiler_params=pltpu.CompilerParams(vmem_limit_bytes=16 * MIB),
        name="join_rows",
    )(*arrays)


def combine_kernel(parts, *refs):
    out_ref, at, top = refs[-1], 0, 0
    for height, offsets in parts:
        total = 0.0
        for offset in offsets:
            total = total + refs[at][offset : offset + height, :].astype(jnp.float32)
            at += 1
        out_ref[top : top + height, :] = total.astype(out_ref.dtype)
        top += height


def combine(*parts):
    arrays = [array for _, terms in parts for array, _ in terms]
    heights = [(height, [offset for _, offset in terms]) for height, terms in parts]
    rows = sum(height for height, _ in heights)
    return pl.pallas_call(
        functools.partial(combine_kernel, heights),
        out_shape=jax.ShapeDtypeStruct((rows, arrays[0].shape[1]), arrays[0].dtype),
        compiler_params=pltpu.CompilerParams(vmem_limit_bytes=16 * MIB),
        name="combine_rows",
    )(*arrays)


def local(ring, hidden_in, norm_gain, router_weight, expert_ids, w_gate, w_up, w_down):
    rows = hidden_in.shape[0]
    num_experts = router_weight.shape[1]
    local_experts = w_gate.shape[0]
    chips = len(ring)
    full, half = chips // 2 - 1, rows // 2
    tie = lax.optimization_barrier

    def shift(by):
        pairs = [
            (2 * ring[p] + c, 2 * ring[(p + by) % chips] + c)
            for p in range(chips)
            for c in range(2)
        ]
        return lambda x: lax.ppermute(x, "expert", pairs)

    ahead, behind = shift(1), shift(-1)

    def sibling(x):
        return lax.ppermute(x, "expert", [(d, d ^ 1) for d in range(2 * chips)])

    packed, first, second = pack(hidden_in, norm_gain, router_weight, expert_ids)
    lane = jnp.arange(packed.shape[1] - hidden_in.shape[1], dtype=jnp.int32)[None, :]
    place = lax.axis_index("expert")

    here = place * local_experts + jnp.arange(local_experts, dtype=jnp.int32)[:, None]
    mine = ((lane == here) | (lane == num_experts + here)).astype(jnp.float32)

    def run(shards, splits):
        total = None
        for e in range(local_experts):
            outs = ffn(shards, splits, w_gate[e], w_up[e], w_down[e], mine[e : e + 1])
            if total is None:
                total = outs
            else:
                total = [combine((a.shape[0], [(a, 0), (b, 0)])) for a, b in zip(total, outs)]
        return total

    def near(ours, theirs, count):
        return run([ours, theirs], [half] * count + [half * count])

    mine = beside_weights(mine, w_gate, w_up, w_down)
    long_a, long_b, short_a, short_b = [first], [second], [first], [second]
    terms, came = [None] * (full + 1), [None] * (full + 1)

    def beside(hops, k):
        if k < 1:
            return hops
        ours = join([long_a[k], short_b[k], short_a[k], long_b[k]])
        *terms[k], sent = near(ours, sibling(ours), 4)
        *hops, sent = tie((*hops, sent))
        came[k] = sibling(sent)
        return hops

    for k in range(1, full + 2):
        long_a.append(ahead(long_a[-1]))
        long_b.append(behind(long_b[-1]))
        if k <= full:
            short_a.append(behind(short_a[-1]))
            short_b.append(ahead(short_b[-1]))
        if k == 1:
            long_a[1], long_b[1], mine = tie((long_a[1], long_b[1], mine))
            own_kept, sent = run([packed, sibling(packed)], [rows, rows])
        elif k == 2:
            long_a[2], long_b[2], sent = tie((long_a[2], long_b[2], sent))
            own_came = sibling(sent)
        else:
            long_a[k], long_b[k] = beside((long_a[k], long_b[k]), k - 2)
    far = join([long_a[-1], long_b[-1]])
    far_a, far_b, sent = near(far, sibling(far), 2)
    far_came = sibling(sent)

    def part(k, i, *more):
        return combine((half, [(terms[k][i], 0), (came[k], i * half), *((m, 0) for m in more)]))

    by_long_a = behind(combine((half, [(far_a, 0), (far_came, 0)])))
    by_long_b = ahead(combine((half, [(far_b, 0), (far_came, half)])))
    by_long_a, by_long_b = beside((by_long_a, by_long_b), full)
    by_short_a, by_short_b = (), ()
    for k in range(full, 0, -1):
        by_long_a, by_long_b = behind(part(k, 0, by_long_a)), ahead(part(k, 3, by_long_b))
        by_short_b, by_short_a = behind(part(k, 1, *by_short_b)), ahead(part(k, 2, *by_short_a))
        by_short_b, by_short_a = (by_short_b,), (by_short_a,)
    (by_short_a,), (by_short_b,) = by_short_a, by_short_b
    return combine(
        (half, [(own_kept, 0), (own_came, 0), (by_long_a, 0), (by_short_a, 0)]),
        (half, [(own_kept, half), (own_came, half), (by_long_b, 0), (by_short_b, 0)]),
    )


def solution(mesh):
    in_specs = (
        P(("groups", "expert"), None),
        P(),
        P(),
        P(("groups", "expert"), None),
        P("expert", None, None),
        P("expert", None, None),
        P("expert", None, None),
    )
    out_specs = P(("groups", "expert"), None)
    chips = mesh.shape["expert"] // 2
    columns = max(1, 4 // mesh.shape["groups"])
    if columns == 2 and chips % 2 == 0:
        ring = list(range(0, chips, 2)) + list(range(chips - 1, 0, -2))
    else:
        ring = list(range(chips))
    return jax.shard_map(
        functools.partial(local, ring),
        mesh=mesh,
        in_specs=in_specs,
        out_specs=out_specs,
        check_vma=False,
    )
```

```python
import functools

import jax
import jax.numpy as jnp
from jax import lax
from jax.experimental import pallas as pl
from jax.experimental.pallas import tpu as pltpu
from jax.sharding import PartitionSpec as P

MIB = 1 << 20


def pack_kernel(*refs):
    sources, outs, held, sems = refs[:4], refs[4:-5], refs[-5:-1], refs[-1]
    copies = [
        pltpu.make_async_copy(source, place, sems.at[i])
        for i, (source, place) in enumerate(zip(sources, held))
    ]
    for copy in copies:
        copy.start()
    for copy in copies:
        copy.wait()
    x_ref, gain_ref, router_ref, ids_ref = held
    rows, width = x_ref.shape
    num_experts = router_ref.shape[0]
    as_float = x_ref[...].astype(jnp.float32)
    inv_rms = lax.rsqrt(jnp.mean(as_float * as_float, axis=1, keepdims=True) + 1e-06)
    normed = (as_float * inv_rms * gain_ref[...]).astype(jnp.bfloat16)
    half = rows // 2
    ranges = [(0, rows), (0, half), (half, rows)]
    for (low, high), out_ref in zip(ranges, outs):
        out_ref[:, :width] = normed[low:high]
    logits = lax.dot_general(
        router_ref[...], normed, (((1,), (1,)), ((), ())), preferred_element_type=jnp.float32
    )
    ids = ids_ref[...]
    expert = lax.broadcasted_iota(jnp.int32, (num_experts, rows), 0)
    named = expert == ids[0:1, :]
    for k in range(1, ids.shape[0]):
        named = named | (expert == ids[k : k + 1, :])
    picked = jnp.where(named, jnp.exp(logits), 0.0)
    weight = picked / jnp.sum(picked, axis=0, keepdims=True)
    high = weight.astype(jnp.bfloat16).astype(jnp.float32)
    parts = [high, weight - high]
    spare = outs[0].shape[1] - width - 2 * num_experts
    if spare:
        parts.append(jnp.zeros((spare, rows), jnp.float32))
    beside = jnp.concatenate(parts, axis=0).T.astype(jnp.bfloat16)
    for (low, high), out_ref in zip(ranges, outs):
        out_ref[:, width:] = beside[low:high]


def pack(hidden_in, norm_gain, router_weight, expert_ids):
    rows, width = hidden_in.shape
    lanes = -(-2 * router_weight.shape[1] // 128) * 128
    sources = [hidden_in, norm_gain[None, :], router_weight.T, expert_ids.T]
    return pl.pallas_call(
        pack_kernel,
        out_shape=[
            jax.ShapeDtypeStruct((r, width + lanes), jnp.bfloat16)
            for r in (rows, rows // 2, rows // 2)
        ],
        in_specs=[pl.BlockSpec(memory_space=pl.ANY)] * len(sources),
        scratch_shapes=[pltpu.VMEM(a.shape, a.dtype) for a in sources]
        + [pltpu.SemaphoreType.DMA((len(sources),))],
        compiler_params=pltpu.CompilerParams(vmem_limit_bytes=58 * MIB),
        name="pack_rows",
    )(*sources)


def ffn_kernel(heights, splits, *refs):
    count = len(heights)
    shards = refs[:count]
    gate_ref, up_ref, down_ref, mine_ref = refs[count : count + 4]
    outs = refs[count + 4 : count + 4 + len(splits)]
    x_ref, hidden_ref, weight_ref = refs[-3:]
    width, depth = gate_ref.shape
    top = 0
    for shard, height in zip(shards, heights):
        x_ref[top : top + height, :] = shard[:, :width]
        parts = shard[:, width:].astype(jnp.float32) * mine_ref[...]
        weight_ref[top : top + height, :] = jnp.sum(parts, axis=1, keepdims=True)
        top += height
    tile = 256 if depth % 256 == 0 else depth

    @pl.loop(0, depth // tile)
    def _(j):
        at = pl.ds(pl.multiple_of(j * tile, tile), tile)
        gate_act = jnp.dot(x_ref[...], gate_ref[:, at], preferred_element_type=jnp.float32)
        up_act = jnp.dot(x_ref[...], up_ref[:, at], preferred_element_type=jnp.float32)
        hidden = gate_act / (1.0 + jnp.exp(-gate_act)) * up_act
        hidden_ref[:, at] = hidden.astype(jnp.bfloat16)

    step = 512 if width % 512 == 0 else width

    @pl.loop(0, width // step)
    def _(j):
        at = pl.ds(pl.multiple_of(j * step, step), step)
        out = jnp.dot(hidden_ref[...], down_ref[:, at], preferred_element_type=jnp.float32)
        done = (out * weight_ref[...]).astype(jnp.bfloat16)
        first = 0
        for out_ref, height in zip(outs, splits):
            out_ref[:, at] = done[first : first + height]
            first += height


def ffn(shards, splits, w_gate, w_up, w_down, mine):
    width, depth = w_gate.shape
    heights = [s.shape[0] for s in shards]
    rows = sum(heights)
    return pl.pallas_call(
        functools.partial(ffn_kernel, heights, splits),
        out_shape=[jax.ShapeDtypeStruct((h, width), jnp.bfloat16) for h in splits],
        scratch_shapes=[
            pltpu.VMEM((rows, width), jnp.bfloat16),
            pltpu.VMEM((rows, depth), jnp.bfloat16),
            pltpu.VMEM((rows, 1), jnp.float32),
        ],
        compiler_params=pltpu.CompilerParams(vmem_limit_bytes=20 * MIB),
        cost_estimate=pl.CostEstimate(
            flops=6 * rows * width * depth,
            bytes_accessed=rows * width,
            transcendentals=0,
        ),
        name="expert_ffn",
    )(*shards, w_gate, w_up, w_down, mine)


def beside_kernel(x_ref, *refs):
    refs[-1][...] = x_ref[...]


def beside_weights(x, *weights):
    return pl.pallas_call(
        beside_kernel,
        out_shape=jax.ShapeDtypeStruct(x.shape, x.dtype),
        in_specs=[pl.BlockSpec(memory_space=pltpu.VMEM)] * (1 + len(weights)),
        out_specs=pl.BlockSpec(memory_space=pltpu.VMEM),
        compiler_params=pltpu.CompilerParams(vmem_limit_bytes=16 * MIB),
        name="beside_weights",
    )(x, *weights)


def join_kernel(*refs):
    out_ref, top = refs[-1], 0
    for ref in refs[:-1]:
        out_ref[top : top + ref.shape[0], :] = ref[...]
        top += ref.shape[0]


def join(arrays):
    rows = sum(a.shape[0] for a in arrays)
    return pl.pallas_call(
        join_kernel,
        out_shape=jax.ShapeDtypeStruct((rows, arrays[0].shape[1]), arrays[0].dtype),
        compiler_params=pltpu.CompilerParams(vmem_limit_bytes=16 * MIB),
        name="join_rows",
    )(*arrays)


def combine_kernel(parts, *refs):
    out_ref, at, top = refs[-1], 0, 0
    for height, offsets in parts:
        total = 0.0
        for offset in offsets:
            total = total + refs[at][offset : offset + height, :].astype(jnp.float32)
            at += 1
        out_ref[top : top + height, :] = total.astype(out_ref.dtype)
        top += height


def combine(*parts):
    arrays = [array for _, terms in parts for array, _ in terms]
    heights = [(height, [offset for _, offset in terms]) for height, terms in parts]
    rows = sum(height for height, _ in heights)
    return pl.pallas_call(
        functools.partial(combine_kernel, heights),
        out_shape=jax.ShapeDtypeStruct((rows, arrays[0].shape[1]), arrays[0].dtype),
        compiler_params=pltpu.CompilerParams(vmem_limit_bytes=16 * MIB),
        name="combine_rows",
    )(*arrays)


def local(ring, hidden_in, norm_gain, router_weight, expert_ids, w_gate, w_up, w_down):
    rows = hidden_in.shape[0]
    num_experts = router_weight.shape[1]
    local_experts = w_gate.shape[0]
    chips = len(ring)
    full, half = chips // 2 - 1, rows // 2
    tie = lax.optimization_barrier

    def shift(by):
        pairs = [
            (2 * ring[p] + c, 2 * ring[(p + by) % chips] + c)
            for p in range(chips)
            for c in range(2)
        ]
        return lambda x: lax.ppermute(x, "expert", pairs)

    ahead, behind = shift(1), shift(-1)

    def sibling(x):
        return lax.ppermute(x, "expert", [(d, d ^ 1) for d in range(2 * chips)])

    packed, first, second = pack(hidden_in, norm_gain, router_weight, expert_ids)
    lane = jnp.arange(packed.shape[1] - hidden_in.shape[1], dtype=jnp.int32)[None, :]
    place = lax.axis_index("expert")

    here = place * local_experts + jnp.arange(local_experts, dtype=jnp.int32)[:, None]
    mine = ((lane == here) | (lane == num_experts + here)).astype(jnp.float32)

    def run(shards, splits):
        total = None
        for e in range(local_experts):
            outs = ffn(shards, splits, w_gate[e], w_up[e], w_down[e], mine[e : e + 1])
            if total is None:
                total = outs
            else:
                total = [combine((a.shape[0], [(a, 0), (b, 0)])) for a, b in zip(total, outs)]
        return total

    def near(ours, theirs, count):
        return run([ours, theirs], [half] * count + [half * count])

    mine = beside_weights(mine, w_gate, w_up, w_down)
    long_a, long_b, short_a, short_b = [first], [second], [first], [second]
    terms, came = [None] * (full + 1), [None] * (full + 1)

    def beside(hops, k):
        if k < 1:
            return hops
        ours = join([long_a[k], short_b[k], short_a[k], long_b[k]])
        *terms[k], sent = near(ours, sibling(ours), 4)
        *hops, sent = tie((*hops, sent))
        came[k] = sibling(sent)
        return hops

    for k in range(1, full + 2):
        long_a.append(ahead(long_a[-1]))
        long_b.append(behind(long_b[-1]))
        if k <= full:
            short_a.append(behind(short_a[-1]))
            short_b.append(ahead(short_b[-1]))
        if k == 1:
            long_a[1], long_b[1], mine = tie((long_a[1], long_b[1], mine))
            own_kept, sent = run([packed, sibling(packed)], [rows, rows])
        elif k == 2:
            long_a[2], long_b[2], sent = tie((long_a[2], long_b[2], sent))
            own_came = sibling(sent)
        else:
            long_a[k], long_b[k] = beside((long_a[k], long_b[k]), k - 2 if k <= full else full)
    far = join([long_a[-1], long_b[-1]])
    far_a, far_b, sent = near(far, sibling(far), 2)

    def part(k, i, *more):
        return combine((half, [(terms[k][i], 0), (came[k], i * half), *((m, 0) for m in more)]))

    by_short_b, by_short_a = behind(part(full, 1)), ahead(part(full, 2))
    by_short_b, by_short_a, sent = tie((by_short_b, by_short_a, sent))
    far_came = sibling(sent)
    by_long_a = behind(combine((half, [(far_a, 0), (far_came, 0)])))
    by_long_b = ahead(combine((half, [(far_b, 0), (far_came, half)])))
    by_long_a, by_long_b = beside((by_long_a, by_long_b), full - 1)
    for k in range(full, 0, -1):
        by_long_a, by_long_b = behind(part(k, 0, by_long_a)), ahead(part(k, 3, by_long_b))
        if k > 1:
            by_short_b, by_short_a = (
                behind(part(k - 1, 1, by_short_b)),
                ahead(part(k - 1, 2, by_short_a)),
            )
    return combine(
        (half, [(own_kept, 0), (own_came, 0), (by_long_a, 0), (by_short_a, 0)]),
        (half, [(own_kept, half), (own_came, half), (by_long_b, 0), (by_short_b, 0)]),
    )


def solution(mesh):
    in_specs = (
        P(("groups", "expert"), None),
        P(),
        P(),
        P(("groups", "expert"), None),
        P("expert", None, None),
        P("expert", None, None),
        P("expert", None, None),
    )
    out_specs = P(("groups", "expert"), None)
    chips = mesh.shape["expert"] // 2
    columns = max(1, 4 // mesh.shape["groups"])
    if columns == 2 and chips % 2 == 0:
        ring = list(range(0, chips, 2)) + list(range(chips - 1, 0, -2))
    else:
        ring = list(range(chips))
    return jax.shard_map(
        functools.partial(local, ring),
        mesh=mesh,
        in_specs=in_specs,
        out_specs=out_specs,
        check_vma=False,
    )
```

```python
import functools

import jax
import jax.numpy as jnp
from jax import lax
from jax.experimental import pallas as pl
from jax.experimental.pallas import tpu as pltpu
from jax.sharding import PartitionSpec as P

MIB = 1 << 20


def pack_kernel(*refs):
    sources, outs, held, sems = refs[:4], refs[4:-5], refs[-5:-1], refs[-1]
    copies = [
        pltpu.make_async_copy(source, place, sems.at[i])
        for i, (source, place) in enumerate(zip(sources, held))
    ]
    for copy in copies:
        copy.start()
    for copy in copies:
        copy.wait()
    x_ref, gain_ref, router_ref, ids_ref = held
    rows, width = x_ref.shape
    num_experts = router_ref.shape[0]
    as_float = x_ref[...].astype(jnp.float32)
    inv_rms = lax.rsqrt(jnp.mean(as_float * as_float, axis=1, keepdims=True) + 1e-06)
    normed = (as_float * inv_rms * gain_ref[...]).astype(jnp.bfloat16)
    half = rows // 2
    ranges = [(0, rows), (0, half), (half, rows)]
    for (low, high), out_ref in zip(ranges, outs):
        out_ref[:, :width] = normed[low:high]
    logits = lax.dot_general(
        router_ref[...], normed, (((1,), (1,)), ((), ())), preferred_element_type=jnp.float32
    )
    ids = ids_ref[...]
    expert = lax.broadcasted_iota(jnp.int32, (num_experts, rows), 0)
    named = expert == ids[0:1, :]
    for k in range(1, ids.shape[0]):
        named = named | (expert == ids[k : k + 1, :])
    picked = jnp.where(named, jnp.exp(logits), 0.0)
    weight = picked / jnp.sum(picked, axis=0, keepdims=True)
    high = weight.astype(jnp.bfloat16).astype(jnp.float32)
    parts = [high, weight - high]
    spare = outs[0].shape[1] - width - 2 * num_experts
    if spare:
        parts.append(jnp.zeros((spare, rows), jnp.float32))
    beside = jnp.concatenate(parts, axis=0).T.astype(jnp.bfloat16)
    for (low, high), out_ref in zip(ranges, outs):
        out_ref[:, width:] = beside[low:high]


def pack(hidden_in, norm_gain, router_weight, expert_ids):
    rows, width = hidden_in.shape
    lanes = -(-2 * router_weight.shape[1] // 128) * 128
    sources = [hidden_in, norm_gain[None, :], router_weight.T, expert_ids.T]
    return pl.pallas_call(
        pack_kernel,
        out_shape=[
            jax.ShapeDtypeStruct((r, width + lanes), jnp.bfloat16)
            for r in (rows, rows // 2, rows // 2)
        ],
        in_specs=[pl.BlockSpec(memory_space=pl.ANY)] * len(sources),
        scratch_shapes=[pltpu.VMEM(a.shape, a.dtype) for a in sources]
        + [pltpu.SemaphoreType.DMA((len(sources),))],
        compiler_params=pltpu.CompilerParams(vmem_limit_bytes=58 * MIB),
        name="pack_rows",
    )(*sources)


def ffn_kernel(heights, splits, *refs):
    count = len(heights)
    shards = refs[:count]
    gate_ref, up_ref, down_ref, mine_ref = refs[count : count + 4]
    outs = refs[count + 4 : count + 4 + len(splits)]
    x_ref, hidden_ref, weight_ref = refs[-3:]
    width, depth = gate_ref.shape
    top = 0
    for shard, height in zip(shards, heights):
        x_ref[top : top + height, :] = shard[:, :width]
        parts = shard[:, width:].astype(jnp.float32) * mine_ref[...]
        weight_ref[top : top + height, :] = jnp.sum(parts, axis=1, keepdims=True)
        top += height
    tile = 256 if depth % 256 == 0 else depth

    @pl.loop(0, depth // tile)
    def _(j):
        at = pl.ds(pl.multiple_of(j * tile, tile), tile)
        gate_act = jnp.dot(x_ref[...], gate_ref[:, at], preferred_element_type=jnp.float32)
        up_act = jnp.dot(x_ref[...], up_ref[:, at], preferred_element_type=jnp.float32)
        hidden = gate_act / (1.0 + jnp.exp(-gate_act)) * up_act
        hidden_ref[:, at] = hidden.astype(jnp.bfloat16)

    step = 512 if width % 512 == 0 else width

    @pl.loop(0, width // step)
    def _(j):
        at = pl.ds(pl.multiple_of(j * step, step), step)
        out = jnp.dot(hidden_ref[...], down_ref[:, at], preferred_element_type=jnp.float32)
        done = (out * weight_ref[...]).astype(jnp.bfloat16)
        first = 0
        for out_ref, height in zip(outs, splits):
            out_ref[:, at] = done[first : first + height]
            first += height


def ffn(shards, splits, w_gate, w_up, w_down, mine):
    width, depth = w_gate.shape
    heights = [s.shape[0] for s in shards]
    rows = sum(heights)
    return pl.pallas_call(
        functools.partial(ffn_kernel, heights, splits),
        out_shape=[jax.ShapeDtypeStruct((h, width), jnp.bfloat16) for h in splits],
        scratch_shapes=[
            pltpu.VMEM((rows, width), jnp.bfloat16),
            pltpu.VMEM((rows, depth), jnp.bfloat16),
            pltpu.VMEM((rows, 1), jnp.float32),
        ],
        compiler_params=pltpu.CompilerParams(vmem_limit_bytes=20 * MIB),
        cost_estimate=pl.CostEstimate(
            flops=6 * rows * width * depth,
            bytes_accessed=rows * width,
            transcendentals=0,
        ),
        name="expert_ffn",
    )(*shards, w_gate, w_up, w_down, mine)


def beside_kernel(x_ref, *refs):
    refs[-1][...] = x_ref[...]


def beside_weights(x, *weights):
    return pl.pallas_call(
        beside_kernel,
        out_shape=jax.ShapeDtypeStruct(x.shape, x.dtype),
        in_specs=[pl.BlockSpec(memory_space=pltpu.VMEM)] * (1 + len(weights)),
        out_specs=pl.BlockSpec(memory_space=pltpu.VMEM),
        compiler_params=pltpu.CompilerParams(vmem_limit_bytes=16 * MIB),
        name="beside_weights",
    )(x, *weights)


def join_kernel(*refs):
    out_ref, top = refs[-1], 0
    for ref in refs[:-1]:
        out_ref[top : top + ref.shape[0], :] = ref[...]
        top += ref.shape[0]


def join(arrays):
    rows = sum(a.shape[0] for a in arrays)
    return pl.pallas_call(
        join_kernel,
        out_shape=jax.ShapeDtypeStruct((rows, arrays[0].shape[1]), arrays[0].dtype),
        compiler_params=pltpu.CompilerParams(vmem_limit_bytes=16 * MIB),
        name="join_rows",
    )(*arrays)


def combine_kernel(parts, *refs):
    out_ref, at, top = refs[-1], 0, 0
    for height, offsets in parts:
        total = 0.0
        for offset in offsets:
            total = total + refs[at][offset : offset + height, :].astype(jnp.float32)
            at += 1
        out_ref[top : top + height, :] = total.astype(out_ref.dtype)
        top += height


def combine(*parts):
    arrays = [array for _, terms in parts for array, _ in terms]
    heights = [(height, [offset for _, offset in terms]) for height, terms in parts]
    rows = sum(height for height, _ in heights)
    return pl.pallas_call(
        functools.partial(combine_kernel, heights),
        out_shape=jax.ShapeDtypeStruct((rows, arrays[0].shape[1]), arrays[0].dtype),
        compiler_params=pltpu.CompilerParams(vmem_limit_bytes=16 * MIB),
        name="combine_rows",
    )(*arrays)


def local(ring, hidden_in, norm_gain, router_weight, expert_ids, w_gate, w_up, w_down):
    rows = hidden_in.shape[0]
    num_experts = router_weight.shape[1]
    local_experts = w_gate.shape[0]
    chips = len(ring)
    full, half = chips // 2 - 1, rows // 2
    tie = lax.optimization_barrier

    def shift(by):
        pairs = [
            (2 * ring[p] + c, 2 * ring[(p + by) % chips] + c)
            for p in range(chips)
            for c in range(2)
        ]
        return lambda x: lax.ppermute(x, "expert", pairs)

    ahead, behind = shift(1), shift(-1)

    def sibling(x):
        return lax.ppermute(x, "expert", [(d, d ^ 1) for d in range(2 * chips)])

    packed, first, second = pack(hidden_in, norm_gain, router_weight, expert_ids)
    lane = jnp.arange(packed.shape[1] - hidden_in.shape[1], dtype=jnp.int32)[None, :]
    place = lax.axis_index("expert")

    here = place * local_experts + jnp.arange(local_experts, dtype=jnp.int32)[:, None]
    mine = ((lane == here) | (lane == num_experts + here)).astype(jnp.float32)

    def run(shards, splits):
        total = None
        for e in range(local_experts):
            outs = ffn(shards, splits, w_gate[e], w_up[e], w_down[e], mine[e : e + 1])
            if total is None:
                total = outs
            else:
                total = [combine((a.shape[0], [(a, 0), (b, 0)])) for a, b in zip(total, outs)]
        return total

    def near(ours, theirs, count):
        return run([ours, theirs], [half] * count + [half * count])

    mine = beside_weights(mine, w_gate, w_up, w_down)
    long_a, long_b, short_a, short_b = [first], [second], [first], [second]
    terms, came = [None] * (full + 1), [None] * (full + 1)

    def beside(hops, k):
        if k < 1:
            return hops
        ours = join([long_a[k], short_b[k], short_a[k], long_b[k]])
        *terms[k], sent = near(ours, sibling(ours), 4)
        *hops, sent = tie((*hops, sent))
        came[k] = sibling(sent)
        return hops

    for k in range(1, full + 2):
        long_a.append(ahead(long_a[-1]))
        long_b.append(behind(long_b[-1]))
        if k <= full:
            short_a.append(behind(short_a[-1]))
            short_b.append(ahead(short_b[-1]))
        if k == 1:
            long_a[1], long_b[1], mine = tie((long_a[1], long_b[1], mine))
            own_kept, sent = run([packed, sibling(packed)], [rows, rows])
        elif k == 2:
            long_a[2], long_b[2], sent = tie((long_a[2], long_b[2], sent))
            own_came = sibling(sent)
        else:
            long_a[k], long_b[k] = beside((long_a[k], long_b[k]), k - 2 if k <= full else full)
            if k == full:
                long_a[k], own_came = tie((long_a[k], own_came))
    far = join([long_a[-1], long_b[-1]])
    far_a, far_b, sent = near(far, sibling(far), 2)

    def part(k, i, *more):
        return combine((half, [(terms[k][i], 0), (came[k], i * half), *((m, 0) for m in more)]))

    by_short_b, by_short_a = behind(part(full, 1)), ahead(part(full, 2))
    by_short_b, by_short_a, sent = tie((by_short_b, by_short_a, sent))
    far_came = sibling(sent)
    by_long_a = behind(combine((half, [(far_a, 0), (far_came, 0)])))
    by_long_b = ahead(combine((half, [(far_b, 0), (far_came, half)])))
    by_long_a, by_long_b = beside((by_long_a, by_long_b), full - 1)
    for k in range(full, 0, -1):
        by_long_a, by_long_b = behind(part(k, 0, by_long_a)), ahead(part(k, 3, by_long_b))
        if k > 1:
            by_short_b, by_short_a = (
                behind(part(k - 1, 1, by_short_b)),
                ahead(part(k - 1, 2, by_short_a)),
            )
    return combine(
        (half, [(own_kept, 0), (own_came, 0), (by_long_a, 0), (by_short_a, 0)]),
        (half, [(own_kept, half), (own_came, half), (by_long_b, 0), (by_short_b, 0)]),
    )


def solution(mesh):
    in_specs = (
        P(("groups", "expert"), None),
        P(),
        P(),
        P(("groups", "expert"), None),
        P("expert", None, None),
        P("expert", None, None),
        P("expert", None, None),
    )
    out_specs = P(("groups", "expert"), None)
    chips = mesh.shape["expert"] // 2
    columns = max(1, 4 // mesh.shape["groups"])
    if columns == 2 and chips % 2 == 0:
        ring = list(range(0, chips, 2)) + list(range(chips - 1, 0, -2))
    else:
        ring = list(range(chips))
    return jax.shard_map(
        functools.partial(local, ring),
        mesh=mesh,
        in_specs=in_specs,
        out_specs=out_specs,
        check_vma=False,
    )
```

```python
import functools

import jax
import jax.numpy as jnp
from jax import lax
from jax.experimental import pallas as pl
from jax.experimental.pallas import tpu as pltpu
from jax.sharding import PartitionSpec as P

MIB = 1 << 20


def pack_kernel(*refs):
    sources, outs, held, sems = refs[:4], refs[4:-5], refs[-5:-1], refs[-1]
    copies = [
        pltpu.make_async_copy(source, place, sems.at[i])
        for i, (source, place) in enumerate(zip(sources, held))
    ]
    for copy in copies:
        copy.start()
    for copy in copies:
        copy.wait()
    x_ref, gain_ref, router_ref, ids_ref = held
    rows, width = x_ref.shape
    num_experts = router_ref.shape[0]
    as_float = x_ref[...].astype(jnp.float32)
    inv_rms = lax.rsqrt(jnp.mean(as_float * as_float, axis=1, keepdims=True) + 1e-06)
    normed = (as_float * inv_rms * gain_ref[...]).astype(jnp.bfloat16)
    half = rows // 2
    ranges = [(0, rows), (0, half), (half, rows)]
    for (low, high), out_ref in zip(ranges, outs):
        out_ref[:, :width] = normed[low:high]
    logits = lax.dot_general(
        router_ref[...], normed, (((1,), (1,)), ((), ())), preferred_element_type=jnp.float32
    )
    ids = ids_ref[...]
    expert = lax.broadcasted_iota(jnp.int32, (num_experts, rows), 0)
    named = expert == ids[0:1, :]
    for k in range(1, ids.shape[0]):
        named = named | (expert == ids[k : k + 1, :])
    picked = jnp.where(named, jnp.exp(logits), 0.0)
    weight = picked / jnp.sum(picked, axis=0, keepdims=True)
    high = weight.astype(jnp.bfloat16).astype(jnp.float32)
    parts = [high, weight - high]
    spare = outs[0].shape[1] - width - 2 * num_experts
    if spare:
        parts.append(jnp.zeros((spare, rows), jnp.float32))
    beside = jnp.concatenate(parts, axis=0).T.astype(jnp.bfloat16)
    for (low, high), out_ref in zip(ranges, outs):
        out_ref[:, width:] = beside[low:high]


def pack(hidden_in, norm_gain, router_weight, expert_ids):
    rows, width = hidden_in.shape
    lanes = -(-2 * router_weight.shape[1] // 128) * 128
    sources = [hidden_in, norm_gain[None, :], router_weight.T, expert_ids.T]
    return pl.pallas_call(
        pack_kernel,
        out_shape=[
            jax.ShapeDtypeStruct((r, width + lanes), jnp.bfloat16)
            for r in (rows, rows // 2, rows // 2)
        ],
        in_specs=[pl.BlockSpec(memory_space=pl.ANY)] * len(sources),
        scratch_shapes=[pltpu.VMEM(a.shape, a.dtype) for a in sources]
        + [pltpu.SemaphoreType.DMA((len(sources),))],
        compiler_params=pltpu.CompilerParams(vmem_limit_bytes=58 * MIB),
        name="pack_rows",
    )(*sources)


def ffn_kernel(heights, splits, *refs):
    count = len(heights)
    shards = refs[:count]
    gate_ref, up_ref, down_ref, mine_ref = refs[count : count + 4]
    outs = refs[count + 4 : count + 4 + len(splits)]
    x_ref, hidden_ref, weight_ref = refs[-3:]
    width, depth = gate_ref.shape
    top = 0
    for shard, height in zip(shards, heights):
        x_ref[top : top + height, :] = shard[:, :width]
        parts = shard[:, width:].astype(jnp.float32) * mine_ref[...]
        weight_ref[top : top + height, :] = jnp.sum(parts, axis=1, keepdims=True)
        top += height
    tile = 256 if depth % 256 == 0 else depth

    @pl.loop(0, depth // tile)
    def _(j):
        at = pl.ds(pl.multiple_of(j * tile, tile), tile)
        gate_act = jnp.dot(x_ref[...], gate_ref[:, at], preferred_element_type=jnp.float32)
        up_act = jnp.dot(x_ref[...], up_ref[:, at], preferred_element_type=jnp.float32)
        hidden = gate_act / (1.0 + jnp.exp(-gate_act)) * up_act
        hidden_ref[:, at] = hidden.astype(jnp.bfloat16)

    step = 512 if width % 512 == 0 else width

    @pl.loop(0, width // step)
    def _(j):
        at = pl.ds(pl.multiple_of(j * step, step), step)
        out = jnp.dot(hidden_ref[...], down_ref[:, at], preferred_element_type=jnp.float32)
        done = (out * weight_ref[...]).astype(jnp.bfloat16)
        first = 0
        for out_ref, height in zip(outs, splits):
            out_ref[:, at] = done[first : first + height]
            first += height


def ffn(shards, splits, w_gate, w_up, w_down, mine):
    width, depth = w_gate.shape
    heights = [s.shape[0] for s in shards]
    rows = sum(heights)
    return pl.pallas_call(
        functools.partial(ffn_kernel, heights, splits),
        out_shape=[jax.ShapeDtypeStruct((h, width), jnp.bfloat16) for h in splits],
        scratch_shapes=[
            pltpu.VMEM((rows, width), jnp.bfloat16),
            pltpu.VMEM((rows, depth), jnp.bfloat16),
            pltpu.VMEM((rows, 1), jnp.float32),
        ],
        compiler_params=pltpu.CompilerParams(vmem_limit_bytes=20 * MIB),
        cost_estimate=pl.CostEstimate(
            flops=6 * rows * width * depth,
            bytes_accessed=rows * width,
            transcendentals=0,
        ),
        name="expert_ffn",
    )(*shards, w_gate, w_up, w_down, mine)


def beside_kernel(x_ref, *refs):
    refs[-1][...] = x_ref[...]


def beside_weights(x, *weights):
    return pl.pallas_call(
        beside_kernel,
        out_shape=jax.ShapeDtypeStruct(x.shape, x.dtype),
        in_specs=[pl.BlockSpec(memory_space=pltpu.VMEM)] * (1 + len(weights)),
        out_specs=pl.BlockSpec(memory_space=pltpu.VMEM),
        compiler_params=pltpu.CompilerParams(vmem_limit_bytes=16 * MIB),
        name="beside_weights",
    )(x, *weights)


def join_kernel(*refs):
    out_ref, top = refs[-1], 0
    for ref in refs[:-1]:
        out_ref[top : top + ref.shape[0], :] = ref[...]
        top += ref.shape[0]


def join(arrays):
    rows = sum(a.shape[0] for a in arrays)
    return pl.pallas_call(
        join_kernel,
        out_shape=jax.ShapeDtypeStruct((rows, arrays[0].shape[1]), arrays[0].dtype),
        compiler_params=pltpu.CompilerParams(vmem_limit_bytes=16 * MIB),
        name="join_rows",
    )(*arrays)


def combine_kernel(parts, *refs):
    out_ref, at, top = refs[-1], 0, 0
    for height, offsets in parts:
        total = 0.0
        for offset in offsets:
            total = total + refs[at][offset : offset + height, :].astype(jnp.float32)
            at += 1
        out_ref[top : top + height, :] = total.astype(out_ref.dtype)
        top += height


def combine(*parts):
    arrays = [array for _, terms in parts for array, _ in terms]
    heights = [(height, [offset for _, offset in terms]) for height, terms in parts]
    rows = sum(height for height, _ in heights)
    return pl.pallas_call(
        functools.partial(combine_kernel, heights),
        out_shape=jax.ShapeDtypeStruct((rows, arrays[0].shape[1]), arrays[0].dtype),
        compiler_params=pltpu.CompilerParams(vmem_limit_bytes=16 * MIB),
        name="combine_rows",
    )(*arrays)


def local(ring, hidden_in, norm_gain, router_weight, expert_ids, w_gate, w_up, w_down):
    rows = hidden_in.shape[0]
    num_experts = router_weight.shape[1]
    local_experts = w_gate.shape[0]
    chips = len(ring)
    full, half = chips // 2 - 1, rows // 2
    tie = lax.optimization_barrier

    def shift(by):
        pairs = [
            (2 * ring[p] + c, 2 * ring[(p + by) % chips] + c)
            for p in range(chips)
            for c in range(2)
        ]
        return lambda x: lax.ppermute(x, "expert", pairs)

    ahead, behind = shift(1), shift(-1)

    def sibling(x):
        return lax.ppermute(x, "expert", [(d, d ^ 1) for d in range(2 * chips)])

    packed, first, second = pack(hidden_in, norm_gain, router_weight, expert_ids)
    lane = jnp.arange(packed.shape[1] - hidden_in.shape[1], dtype=jnp.int32)[None, :]
    place = lax.axis_index("expert")

    here = place * local_experts + jnp.arange(local_experts, dtype=jnp.int32)[:, None]
    mine = ((lane == here) | (lane == num_experts + here)).astype(jnp.float32)

    def run(shards, splits):
        total = None
        for e in range(local_experts):
            outs = ffn(shards, splits, w_gate[e], w_up[e], w_down[e], mine[e : e + 1])
            if total is None:
                total = outs
            else:
                total = [combine((a.shape[0], [(a, 0), (b, 0)])) for a, b in zip(total, outs)]
        return total

    def near(ours, theirs, count):
        return run([ours, theirs], [half] * count + [half * count])

    mine = beside_weights(mine, w_gate, w_up, w_down)
    long_a, long_b, short_a, short_b = [first], [second], [first], [second]
    terms, came = [None] * (full + 1), [None] * (full + 1)

    def beside(hops, k):
        if k < 1:
            return hops
        ours = join([long_a[k], short_b[k], short_a[k], long_b[k]])
        *terms[k], sent = near(ours, sibling(ours), 4)
        *hops, sent = tie((*hops, sent))
        came[k] = sibling(sent)
        return hops

    for k in range(1, full + 2):
        long_a.append(ahead(long_a[-1]))
        long_b.append(behind(long_b[-1]))
        if k <= full:
            short_a.append(behind(short_a[-1]))
            short_b.append(ahead(short_b[-1]))
        if k == 1:
            long_a[1], long_b[1], mine = tie((long_a[1], long_b[1], mine))
            own_kept, sent = run([packed, sibling(packed)], [rows, rows])
        elif k == 2:
            long_a[2], long_b[2], sent = tie((long_a[2], long_b[2], sent))
            own_came = sibling(sent)
        else:
            long_a[k], long_b[k] = beside((long_a[k], long_b[k]), k - 2 if k <= full else full)
    far = join([long_a[-1], long_b[-1]])
    far_a, far_b, sent = near(far, sibling(far), 2)

    def part(k, i, *more):
        return combine((half, [(terms[k][i], 0), (came[k], i * half), *((m, 0) for m in more)]))

    by_short_b, by_short_a = behind(part(full, 1)), ahead(part(full, 2))
    far_came = sibling(sent)
    by_long_a = behind(combine((half, [(far_a, 0), (far_came, 0)])))
    by_long_b = ahead(combine((half, [(far_b, 0), (far_came, half)])))
    by_long_a, by_long_b, by_short_a, by_short_b = beside(
        (by_long_a, by_long_b, by_short_a, by_short_b), full - 1
    )
    for k in range(full, 0, -1):
        by_long_a, by_long_b = behind(part(k, 0, by_long_a)), ahead(part(k, 3, by_long_b))
        if k > 1:
            by_short_b, by_short_a = (
                behind(part(k - 1, 1, by_short_b)),
                ahead(part(k - 1, 2, by_short_a)),
            )
    return combine(
        (half, [(own_kept, 0), (own_came, 0), (by_long_a, 0), (by_short_a, 0)]),
        (half, [(own_kept, half), (own_came, half), (by_long_b, 0), (by_short_b, 0)]),
    )


def solution(mesh):
    in_specs = (
        P(("groups", "expert"), None),
        P(),
        P(),
        P(("groups", "expert"), None),
        P("expert", None, None),
        P("expert", None, None),
        P("expert", None, None),
    )
    out_specs = P(("groups", "expert"), None)
    chips = mesh.shape["expert"] // 2
    columns = max(1, 4 // mesh.shape["groups"])
    if columns == 2 and chips % 2 == 0:
        ring = list(range(0, chips, 2)) + list(range(chips - 1, 0, -2))
    else:
        ring = list(range(chips))
    return jax.shard_map(
        functools.partial(local, ring),
        mesh=mesh,
        in_specs=in_specs,
        out_specs=out_specs,
        check_vma=False,
    )
```

```python
import functools

import jax
import jax.numpy as jnp
from jax import lax
from jax.experimental import pallas as pl
from jax.experimental.pallas import tpu as pltpu
from jax.sharding import PartitionSpec as P

MIB = 1 << 20


def pack_kernel(*refs):
    sources, outs, held, sems = refs[:4], refs[4:-5], refs[-5:-1], refs[-1]
    copies = [
        pltpu.make_async_copy(source, place, sems.at[i])
        for i, (source, place) in enumerate(zip(sources, held))
    ]
    for copy in copies:
        copy.start()
    for copy in copies:
        copy.wait()
    x_ref, gain_ref, router_ref, ids_ref = held
    rows, width = x_ref.shape
    num_experts = router_ref.shape[0]
    as_float = x_ref[...].astype(jnp.float32)
    inv_rms = lax.rsqrt(jnp.mean(as_float * as_float, axis=1, keepdims=True) + 1e-06)
    normed = (as_float * inv_rms * gain_ref[...]).astype(jnp.bfloat16)
    half = rows // 2
    ranges = [(0, rows), (0, half), (half, rows)]
    for (low, high), out_ref in zip(ranges, outs):
        out_ref[:, :width] = normed[low:high]
    logits = lax.dot_general(
        router_ref[...], normed, (((1,), (1,)), ((), ())), preferred_element_type=jnp.float32
    )
    ids = ids_ref[...]
    expert = lax.broadcasted_iota(jnp.int32, (num_experts, rows), 0)
    named = expert == ids[0:1, :]
    for k in range(1, ids.shape[0]):
        named = named | (expert == ids[k : k + 1, :])
    picked = jnp.where(named, jnp.exp(logits), 0.0)
    weight = picked / jnp.sum(picked, axis=0, keepdims=True)
    high = weight.astype(jnp.bfloat16).astype(jnp.float32)
    parts = [high, weight - high]
    spare = outs[0].shape[1] - width - 2 * num_experts
    if spare:
        parts.append(jnp.zeros((spare, rows), jnp.float32))
    beside = jnp.concatenate(parts, axis=0).T.astype(jnp.bfloat16)
    for (low, high), out_ref in zip(ranges, outs):
        out_ref[:, width:] = beside[low:high]


def pack(hidden_in, norm_gain, router_weight, expert_ids):
    rows, width = hidden_in.shape
    lanes = -(-2 * router_weight.shape[1] // 128) * 128
    sources = [hidden_in, norm_gain[None, :], router_weight.T, expert_ids.T]
    return pl.pallas_call(
        pack_kernel,
        out_shape=[
            jax.ShapeDtypeStruct((r, width + lanes), jnp.bfloat16)
            for r in (rows, rows // 2, rows // 2)
        ],
        in_specs=[pl.BlockSpec(memory_space=pl.ANY)] * len(sources),
        scratch_shapes=[pltpu.VMEM(a.shape, a.dtype) for a in sources]
        + [pltpu.SemaphoreType.DMA((len(sources),))],
        compiler_params=pltpu.CompilerParams(vmem_limit_bytes=58 * MIB),
        name="pack_rows",
    )(*sources)


def ffn_kernel(heights, splits, *refs):
    count = len(heights)
    shards = refs[:count]
    gate_ref, up_ref, down_ref, mine_ref = refs[count : count + 4]
    outs = refs[count + 4 : count + 4 + len(splits)]
    x_ref, hidden_ref, weight_ref = refs[-3:]
    width, depth = gate_ref.shape
    top = 0
    for shard, height in zip(shards, heights):
        x_ref[top : top + height, :] = shard[:, :width]
        parts = shard[:, width:].astype(jnp.float32) * mine_ref[...]
        weight_ref[top : top + height, :] = jnp.sum(parts, axis=1, keepdims=True)
        top += height
    tile = 256 if depth % 256 == 0 else depth

    @pl.loop(0, depth // tile)
    def _(j):
        at = pl.ds(pl.multiple_of(j * tile, tile), tile)
        gate_act = jnp.dot(x_ref[...], gate_ref[:, at], preferred_element_type=jnp.float32)
        up_act = jnp.dot(x_ref[...], up_ref[:, at], preferred_element_type=jnp.float32)
        hidden = gate_act / (1.0 + jnp.exp(-gate_act)) * up_act
        hidden_ref[:, at] = hidden.astype(jnp.bfloat16)

    step = 512 if width % 512 == 0 else width

    @pl.loop(0, width // step)
    def _(j):
        at = pl.ds(pl.multiple_of(j * step, step), step)
        out = jnp.dot(hidden_ref[...], down_ref[:, at], preferred_element_type=jnp.float32)
        done = (out * weight_ref[...]).astype(jnp.bfloat16)
        first = 0
        for out_ref, height in zip(outs, splits):
            out_ref[:, at] = done[first : first + height]
            first += height


def ffn(shards, splits, w_gate, w_up, w_down, mine):
    width, depth = w_gate.shape
    heights = [s.shape[0] for s in shards]
    rows = sum(heights)
    return pl.pallas_call(
        functools.partial(ffn_kernel, heights, splits),
        out_shape=[jax.ShapeDtypeStruct((h, width), jnp.bfloat16) for h in splits],
        scratch_shapes=[
            pltpu.VMEM((rows, width), jnp.bfloat16),
            pltpu.VMEM((rows, depth), jnp.bfloat16),
            pltpu.VMEM((rows, 1), jnp.float32),
        ],
        compiler_params=pltpu.CompilerParams(vmem_limit_bytes=20 * MIB),
        cost_estimate=pl.CostEstimate(
            flops=6 * rows * width * depth,
            bytes_accessed=rows * width,
            transcendentals=0,
        ),
        name="expert_ffn",
    )(*shards, w_gate, w_up, w_down, mine)


def beside_kernel(x_ref, *refs):
    refs[-1][...] = x_ref[...]


def beside_weights(x, *weights):
    return pl.pallas_call(
        beside_kernel,
        out_shape=jax.ShapeDtypeStruct(x.shape, x.dtype),
        in_specs=[pl.BlockSpec(memory_space=pltpu.VMEM)] * (1 + len(weights)),
        out_specs=pl.BlockSpec(memory_space=pltpu.VMEM),
        compiler_params=pltpu.CompilerParams(vmem_limit_bytes=16 * MIB),
        name="beside_weights",
    )(x, *weights)


def join_kernel(*refs):
    out_ref, top = refs[-1], 0
    for ref in refs[:-1]:
        out_ref[top : top + ref.shape[0], :] = ref[...]
        top += ref.shape[0]


def join(arrays):
    rows = sum(a.shape[0] for a in arrays)
    return pl.pallas_call(
        join_kernel,
        out_shape=jax.ShapeDtypeStruct((rows, arrays[0].shape[1]), arrays[0].dtype),
        compiler_params=pltpu.CompilerParams(vmem_limit_bytes=16 * MIB),
        name="join_rows",
    )(*arrays)


def combine_kernel(parts, *refs):
    out_ref, at, top = refs[-1], 0, 0
    for height, offsets in parts:
        total = 0.0
        for offset in offsets:
            total = total + refs[at][offset : offset + height, :].astype(jnp.float32)
            at += 1
        out_ref[top : top + height, :] = total.astype(out_ref.dtype)
        top += height


def combine(*parts):
    arrays = [array for _, terms in parts for array, _ in terms]
    heights = [(height, [offset for _, offset in terms]) for height, terms in parts]
    rows = sum(height for height, _ in heights)
    return pl.pallas_call(
        functools.partial(combine_kernel, heights),
        out_shape=jax.ShapeDtypeStruct((rows, arrays[0].shape[1]), arrays[0].dtype),
        compiler_params=pltpu.CompilerParams(vmem_limit_bytes=16 * MIB),
        name="combine_rows",
    )(*arrays)


def local(ring, hidden_in, norm_gain, router_weight, expert_ids, w_gate, w_up, w_down):
    rows = hidden_in.shape[0]
    num_experts = router_weight.shape[1]
    local_experts = w_gate.shape[0]
    chips = len(ring)
    full, half = chips // 2 - 1, rows // 2
    tie = lax.optimization_barrier

    def shift(by):
        pairs = [
            (2 * ring[p] + c, 2 * ring[(p + by) % chips] + c)
            for p in range(chips)
            for c in range(2)
        ]
        return lambda x: lax.ppermute(x, "expert", pairs)

    ahead, behind = shift(1), shift(-1)

    def sibling(x):
        return lax.ppermute(x, "expert", [(d, d ^ 1) for d in range(2 * chips)])

    packed, first, second = pack(hidden_in, norm_gain, router_weight, expert_ids)
    lane = jnp.arange(packed.shape[1] - hidden_in.shape[1], dtype=jnp.int32)[None, :]
    place = lax.axis_index("expert")

    here = place * local_experts + jnp.arange(local_experts, dtype=jnp.int32)[:, None]
    mine = ((lane == here) | (lane == num_experts + here)).astype(jnp.float32)

    def run(shards, splits):
        total = None
        for e in range(local_experts):
            outs = ffn(shards, splits, w_gate[e], w_up[e], w_down[e], mine[e : e + 1])
            if total is None:
                total = outs
            else:
                total = [combine((a.shape[0], [(a, 0), (b, 0)])) for a, b in zip(total, outs)]
        return total

    def near(ours, theirs, count):
        return run([ours, theirs], [half] * count + [half * count])

    mine = beside_weights(mine, w_gate, w_up, w_down)
    long_a, long_b, short_a, short_b = [first], [second], [first], [second]
    terms, came = [None] * (full + 1), [None] * (full + 1)

    def beside(hops, k):
        if k < 1:
            return hops
        ours = join([long_a[k], short_b[k], short_a[k], long_b[k]])
        *terms[k], sent = near(ours, sibling(ours), 4)
        *hops, sent = tie((*hops, sent))
        came[k] = sibling(sent)
        return hops

    for k in range(1, full + 2):
        long_a.append(ahead(long_a[-1]))
        long_b.append(behind(long_b[-1]))
        if k <= full:
            short_a.append(behind(short_a[-1]))
            short_b.append(ahead(short_b[-1]))
        if k == 1:
            long_a[1], long_b[1], mine = tie((long_a[1], long_b[1], mine))
            own_kept, sent = run([packed, sibling(packed)], [rows, rows])
        elif k == 2:
            long_a[2], long_b[2], sent = tie((long_a[2], long_b[2], sent))
            own_came = sibling(sent)
        else:
            long_a[k], long_b[k] = beside((long_a[k], long_b[k]), 0 if k <= full else full)
    far = join([long_a[-1], long_b[-1]])
    far_a, far_b, sent = near(far, sibling(far), 2)

    def part(k, i, *more):
        return combine((half, [(terms[k][i], 0), (came[k], i * half), *((m, 0) for m in more)]))

    by_short_b, by_short_a = behind(part(full, 1)), ahead(part(full, 2))
    far_came = sibling(sent)
    by_long_a = behind(combine((half, [(far_a, 0), (far_came, 0)])))
    by_long_b = ahead(combine((half, [(far_b, 0), (far_came, half)])))
    by_long_a, by_long_b, by_short_a, by_short_b = beside(
        (by_long_a, by_long_b, by_short_a, by_short_b), full - 1
    )
    for k in range(full, 0, -1):
        by_long_a, by_long_b = behind(part(k, 0, by_long_a)), ahead(part(k, 3, by_long_b))
        if k > 1:
            by_short_b, by_short_a = (
                behind(part(k - 1, 1, by_short_b)),
                ahead(part(k - 1, 2, by_short_a)),
            )
            by_long_a, by_long_b = beside((by_long_a, by_long_b), k - 2)
    return combine(
        (half, [(own_kept, 0), (own_came, 0), (by_long_a, 0), (by_short_a, 0)]),
        (half, [(own_kept, half), (own_came, half), (by_long_b, 0), (by_short_b, 0)]),
    )


def solution(mesh):
    in_specs = (
        P(("groups", "expert"), None),
        P(),
        P(),
        P(("groups", "expert"), None),
        P("expert", None, None),
        P("expert", None, None),
        P("expert", None, None),
    )
    out_specs = P(("groups", "expert"), None)
    chips = mesh.shape["expert"] // 2
    columns = max(1, 4 // mesh.shape["groups"])
    if columns == 2 and chips % 2 == 0:
        ring = list(range(0, chips, 2)) + list(range(chips - 1, 0, -2))
    else:
        ring = list(range(chips))
    return jax.shard_map(
        functools.partial(local, ring),
        mesh=mesh,
        in_specs=in_specs,
        out_specs=out_specs,
        check_vma=False,
    )
```

```python
import functools

import jax
import jax.numpy as jnp
from jax import lax
from jax.experimental import pallas as pl
from jax.experimental.pallas import tpu as pltpu
from jax.sharding import PartitionSpec as P

MIB = 1 << 20


def pack_kernel(*refs):
    sources, outs, held, sems = refs[:4], refs[4:-5], refs[-5:-1], refs[-1]
    copies = [
        pltpu.make_async_copy(source, place, sems.at[i])
        for i, (source, place) in enumerate(zip(sources, held))
    ]
    for copy in copies:
        copy.start()
    for copy in copies:
        copy.wait()
    x_ref, gain_ref, router_ref, ids_ref = held
    rows, width = x_ref.shape
    num_experts = router_ref.shape[0]
    as_float = x_ref[...].astype(jnp.float32)
    inv_rms = lax.rsqrt(jnp.mean(as_float * as_float, axis=1, keepdims=True) + 1e-06)
    normed = (as_float * inv_rms * gain_ref[...]).astype(jnp.bfloat16)
    half = rows // 2
    ranges = [(0, rows), (0, half), (half, rows)]
    for (low, high), out_ref in zip(ranges, outs):
        out_ref[:, :width] = normed[low:high]
    logits = lax.dot_general(
        router_ref[...], normed, (((1,), (1,)), ((), ())), preferred_element_type=jnp.float32
    )
    ids = ids_ref[...]
    expert = lax.broadcasted_iota(jnp.int32, (num_experts, rows), 0)
    named = expert == ids[0:1, :]
    for k in range(1, ids.shape[0]):
        named = named | (expert == ids[k : k + 1, :])
    picked = jnp.where(named, jnp.exp(logits), 0.0)
    weight = picked / jnp.sum(picked, axis=0, keepdims=True)
    high = weight.astype(jnp.bfloat16).astype(jnp.float32)
    parts = [high, weight - high]
    spare = outs[0].shape[1] - width - 2 * num_experts
    if spare:
        parts.append(jnp.zeros((spare, rows), jnp.float32))
    beside = jnp.concatenate(parts, axis=0).T.astype(jnp.bfloat16)
    for (low, high), out_ref in zip(ranges, outs):
        out_ref[:, width:] = beside[low:high]


def pack(hidden_in, norm_gain, router_weight, expert_ids):
    rows, width = hidden_in.shape
    lanes = -(-2 * router_weight.shape[1] // 128) * 128
    sources = [hidden_in, norm_gain[None, :], router_weight.T, expert_ids.T]
    return pl.pallas_call(
        pack_kernel,
        out_shape=[
            jax.ShapeDtypeStruct((r, width + lanes), jnp.bfloat16)
            for r in (rows, rows // 2, rows // 2)
        ],
        in_specs=[pl.BlockSpec(memory_space=pl.ANY)] * len(sources),
        scratch_shapes=[pltpu.VMEM(a.shape, a.dtype) for a in sources]
        + [pltpu.SemaphoreType.DMA((len(sources),))],
        compiler_params=pltpu.CompilerParams(vmem_limit_bytes=58 * MIB),
        name="pack_rows",
    )(*sources)


def ffn_kernel(heights, splits, *refs):
    count = len(heights)
    shards = refs[:count]
    gate_ref, up_ref, down_ref, mine_ref = refs[count : count + 4]
    outs = refs[count + 4 : count + 4 + len(splits)]
    x_ref, hidden_ref, weight_ref = refs[-3:]
    width, depth = gate_ref.shape
    top = 0
    for shard, height in zip(shards, heights):
        x_ref[top : top + height, :] = shard[:, :width]
        parts = shard[:, width:].astype(jnp.float32) * mine_ref[...]
        weight_ref[top : top + height, :] = jnp.sum(parts, axis=1, keepdims=True)
        top += height
    tile = 256 if depth % 256 == 0 else depth

    @pl.loop(0, depth // tile)
    def _(j):
        at = pl.ds(pl.multiple_of(j * tile, tile), tile)
        gate_act = jnp.dot(x_ref[...], gate_ref[:, at], preferred_element_type=jnp.float32)
        up_act = jnp.dot(x_ref[...], up_ref[:, at], preferred_element_type=jnp.float32)
        hidden = gate_act / (1.0 + jnp.exp(-gate_act)) * up_act
        hidden_ref[:, at] = hidden.astype(jnp.bfloat16)

    step = 512 if width % 512 == 0 else width

    @pl.loop(0, width // step)
    def _(j):
        at = pl.ds(pl.multiple_of(j * step, step), step)
        out = jnp.dot(hidden_ref[...], down_ref[:, at], preferred_element_type=jnp.float32)
        done = (out * weight_ref[...]).astype(jnp.bfloat16)
        first = 0
        for out_ref, height in zip(outs, splits):
            out_ref[:, at] = done[first : first + height]
            first += height


def ffn(shards, splits, w_gate, w_up, w_down, mine):
    width, depth = w_gate.shape
    heights = [s.shape[0] for s in shards]
    rows = sum(heights)
    return pl.pallas_call(
        functools.partial(ffn_kernel, heights, splits),
        out_shape=[jax.ShapeDtypeStruct((h, width), jnp.bfloat16) for h in splits],
        scratch_shapes=[
            pltpu.VMEM((rows, width), jnp.bfloat16),
            pltpu.VMEM((rows, depth), jnp.bfloat16),
            pltpu.VMEM((rows, 1), jnp.float32),
        ],
        compiler_params=pltpu.CompilerParams(vmem_limit_bytes=20 * MIB),
        cost_estimate=pl.CostEstimate(
            flops=2 * rows * width * depth,
            bytes_accessed=rows * width,
            transcendentals=0,
        ),
        name="expert_ffn",
    )(*shards, w_gate, w_up, w_down, mine)


def beside_kernel(x_ref, *refs):
    refs[-1][...] = x_ref[...]


def beside_weights(x, *weights):
    return pl.pallas_call(
        beside_kernel,
        out_shape=jax.ShapeDtypeStruct(x.shape, x.dtype),
        in_specs=[pl.BlockSpec(memory_space=pltpu.VMEM)] * (1 + len(weights)),
        out_specs=pl.BlockSpec(memory_space=pltpu.VMEM),
        compiler_params=pltpu.CompilerParams(vmem_limit_bytes=16 * MIB),
        name="beside_weights",
    )(x, *weights)


def join_kernel(*refs):
    out_ref, top = refs[-1], 0
    for ref in refs[:-1]:
        out_ref[top : top + ref.shape[0], :] = ref[...]
        top += ref.shape[0]


def join(arrays):
    rows = sum(a.shape[0] for a in arrays)
    return pl.pallas_call(
        join_kernel,
        out_shape=jax.ShapeDtypeStruct((rows, arrays[0].shape[1]), arrays[0].dtype),
        compiler_params=pltpu.CompilerParams(vmem_limit_bytes=16 * MIB),
        name="join_rows",
    )(*arrays)


def combine_kernel(parts, *refs):
    out_ref, at, top = refs[-1], 0, 0
    for height, offsets in parts:
        total = 0.0
        for offset in offsets:
            total = total + refs[at][offset : offset + height, :].astype(jnp.float32)
            at += 1
        out_ref[top : top + height, :] = total.astype(out_ref.dtype)
        top += height


def combine(*parts):
    arrays = [array for _, terms in parts for array, _ in terms]
    heights = [(height, [offset for _, offset in terms]) for height, terms in parts]
    rows = sum(height for height, _ in heights)
    return pl.pallas_call(
        functools.partial(combine_kernel, heights),
        out_shape=jax.ShapeDtypeStruct((rows, arrays[0].shape[1]), arrays[0].dtype),
        compiler_params=pltpu.CompilerParams(vmem_limit_bytes=16 * MIB),
        name="combine_rows",
    )(*arrays)


def local(ring, hidden_in, norm_gain, router_weight, expert_ids, w_gate, w_up, w_down):
    rows = hidden_in.shape[0]
    num_experts = router_weight.shape[1]
    local_experts = w_gate.shape[0]
    chips = len(ring)
    full, half = chips // 2 - 1, rows // 2
    tie = lax.optimization_barrier

    def shift(by):
        pairs = [
            (2 * ring[p] + c, 2 * ring[(p + by) % chips] + c)
            for p in range(chips)
            for c in range(2)
        ]
        return lambda x: lax.ppermute(x, "expert", pairs)

    ahead, behind = shift(1), shift(-1)

    def sibling(x):
        return lax.ppermute(x, "expert", [(d, d ^ 1) for d in range(2 * chips)])

    packed, first, second = pack(hidden_in, norm_gain, router_weight, expert_ids)
    lane = jnp.arange(packed.shape[1] - hidden_in.shape[1], dtype=jnp.int32)[None, :]
    place = lax.axis_index("expert")

    here = place * local_experts + jnp.arange(local_experts, dtype=jnp.int32)[:, None]
    mine = ((lane == here) | (lane == num_experts + here)).astype(jnp.float32)

    def run(shards, splits):
        total = None
        for e in range(local_experts):
            outs = ffn(shards, splits, w_gate[e], w_up[e], w_down[e], mine[e : e + 1])
            if total is None:
                total = outs
            else:
                total = [combine((a.shape[0], [(a, 0), (b, 0)])) for a, b in zip(total, outs)]
        return total

    def near(ours, theirs, count):
        return run([ours, theirs], [half] * count + [half * count])

    mine = beside_weights(mine, w_gate, w_up, w_down)
    long_a, long_b, short_a, short_b = [first], [second], [first], [second]
    terms, came = [None] * (full + 1), [None] * (full + 1)

    def beside(hops, *distances):
        distances = [k for k in distances if k >= 1]
        sents = []
        for k in distances:
            ours = join([long_a[k], short_b[k], short_a[k], long_b[k]])
            theirs = sibling(ours)
            if sents:
                ours, theirs, sents[-1] = tie((ours, theirs, sents[-1]))
            *terms[k], sent = near(ours, theirs, 4)
            sents.append(sent)
        if distances:
            hops, sents = tie((list(hops), sents))
        for k, sent in zip(distances, sents):
            came[k] = sibling(sent)
        return hops

    for k in range(1, full + 2):
        long_a.append(ahead(long_a[-1]))
        long_b.append(behind(long_b[-1]))
        if k <= full:
            short_a.append(behind(short_a[-1]))
            short_b.append(ahead(short_b[-1]))
        if k == 1:
            long_a[1], long_b[1], mine = tie((long_a[1], long_b[1], mine))
            own_kept, sent = run([packed, sibling(packed)], [rows, rows])
        elif k == 2:
            long_a[2], long_b[2], sent = tie((long_a[2], long_b[2], sent))
            own_came = sibling(sent)
        else:
            long_a[k], long_b[k] = beside((long_a[k], long_b[k]), 0 if k <= full else full)
    far = join([long_a[-1], long_b[-1]])
    far_a, far_b, sent = near(far, sibling(far), 2)

    def part(k, i, *more):
        return combine((half, [(terms[k][i], 0), (came[k], i * half), *((m, 0) for m in more)]))

    by_short_b, by_short_a = behind(part(full, 1)), ahead(part(full, 2))
    far_came = sibling(sent)
    by_long_a = behind(combine((half, [(far_a, 0), (far_came, 0)])))
    by_long_b = ahead(combine((half, [(far_b, 0), (far_came, half)])))
    by_long_a, by_long_b, by_short_a, by_short_b = beside(
        (by_long_a, by_long_b, by_short_a, by_short_b), full - 1, full - 2
    )
    for k in range(full, 0, -1):
        by_long_a, by_long_b = behind(part(k, 0, by_long_a)), ahead(part(k, 3, by_long_b))
        if k > 1:
            by_short_b, by_short_a = (
                behind(part(k - 1, 1, by_short_b)),
                ahead(part(k - 1, 2, by_short_a)),
            )
            by_long_a, by_long_b = beside((by_long_a, by_long_b), k - 3)
    return combine(
        (half, [(own_kept, 0), (own_came, 0), (by_long_a, 0), (by_short_a, 0)]),
        (half, [(own_kept, half), (own_came, half), (by_long_b, 0), (by_short_b, 0)]),
    )


def solution(mesh):
    in_specs = (
        P(("groups", "expert"), None),
        P(),
        P(),
        P(("groups", "expert"), None),
        P("expert", None, None),
        P("expert", None, None),
        P("expert", None, None),
    )
    out_specs = P(("groups", "expert"), None)
    chips = mesh.shape["expert"] // 2
    columns = max(1, 4 // mesh.shape["groups"])
    if columns == 2 and chips % 2 == 0:
        ring = list(range(0, chips, 2)) + list(range(chips - 1, 0, -2))
    else:
        ring = list(range(chips))
    return jax.shard_map(
        functools.partial(local, ring),
        mesh=mesh,
        in_specs=in_specs,
        out_specs=out_specs,
        check_vma=False,
    )
```

```python
import functools

import jax
import jax.numpy as jnp
from jax import lax
from jax.experimental import pallas as pl
from jax.experimental.pallas import tpu as pltpu
from jax.sharding import PartitionSpec as P

MIB = 1 << 20


def pack_kernel(*refs):
    sources, outs, held, sems = refs[:4], refs[4:-5], refs[-5:-1], refs[-1]
    copies = [
        pltpu.make_async_copy(source, place, sems.at[i])
        for i, (source, place) in enumerate(zip(sources, held))
    ]
    for copy in copies:
        copy.start()
    for copy in copies:
        copy.wait()
    x_ref, gain_ref, router_ref, ids_ref = held
    rows, width = x_ref.shape
    num_experts = router_ref.shape[0]
    as_float = x_ref[...].astype(jnp.float32)
    inv_rms = lax.rsqrt(jnp.mean(as_float * as_float, axis=1, keepdims=True) + 1e-06)
    normed = (as_float * inv_rms * gain_ref[...]).astype(jnp.bfloat16)
    half = rows // 2
    ranges = [(0, rows), (0, half), (half, rows)]
    for (low, high), out_ref in zip(ranges, outs):
        out_ref[:, :width] = normed[low:high]
    logits = lax.dot_general(
        router_ref[...], normed, (((1,), (1,)), ((), ())), preferred_element_type=jnp.float32
    )
    ids = ids_ref[...]
    expert = lax.broadcasted_iota(jnp.int32, (num_experts, rows), 0)
    named = expert == ids[0:1, :]
    for k in range(1, ids.shape[0]):
        named = named | (expert == ids[k : k + 1, :])
    picked = jnp.where(named, jnp.exp(logits), 0.0)
    weight = picked / jnp.sum(picked, axis=0, keepdims=True)
    high = weight.astype(jnp.bfloat16).astype(jnp.float32)
    parts = [high, weight - high]
    spare = outs[0].shape[1] - width - 2 * num_experts
    if spare:
        parts.append(jnp.zeros((spare, rows), jnp.float32))
    beside = jnp.concatenate(parts, axis=0).T.astype(jnp.bfloat16)
    for (low, high), out_ref in zip(ranges, outs):
        out_ref[:, width:] = beside[low:high]


def pack(hidden_in, norm_gain, router_weight, expert_ids):
    rows, width = hidden_in.shape
    lanes = -(-2 * router_weight.shape[1] // 128) * 128
    sources = [hidden_in, norm_gain[None, :], router_weight.T, expert_ids.T]
    return pl.pallas_call(
        pack_kernel,
        out_shape=[
            jax.ShapeDtypeStruct((r, width + lanes), jnp.bfloat16)
            for r in (rows, rows // 2, rows // 2)
        ],
        in_specs=[pl.BlockSpec(memory_space=pl.ANY)] * len(sources),
        scratch_shapes=[pltpu.VMEM(a.shape, a.dtype) for a in sources]
        + [pltpu.SemaphoreType.DMA((len(sources),))],
        compiler_params=pltpu.CompilerParams(vmem_limit_bytes=58 * MIB),
        name="pack_rows",
    )(*sources)


def ffn_kernel(heights, splits, *refs):
    count = len(heights)
    shards = refs[:count]
    gate_ref, up_ref, down_ref, mine_ref = refs[count : count + 4]
    outs = refs[count + 4 : count + 4 + len(splits)]
    x_ref, hidden_ref, weight_ref = refs[-3:]
    width, depth = gate_ref.shape
    top = 0
    for shard, height in zip(shards, heights):
        x_ref[top : top + height, :] = shard[:, :width]
        parts = shard[:, width:].astype(jnp.float32) * mine_ref[...]
        weight_ref[top : top + height, :] = jnp.sum(parts, axis=1, keepdims=True)
        top += height
    tile = 256 if depth % 256 == 0 else depth

    @pl.loop(0, depth // tile)
    def _(j):
        at = pl.ds(pl.multiple_of(j * tile, tile), tile)
        gate_act = jnp.dot(x_ref[...], gate_ref[:, at], preferred_element_type=jnp.float32)
        up_act = jnp.dot(x_ref[...], up_ref[:, at], preferred_element_type=jnp.float32)
        hidden = gate_act / (1.0 + jnp.exp(-gate_act)) * up_act
        hidden_ref[:, at] = hidden.astype(jnp.bfloat16)

    step = 512 if width % 512 == 0 else width

    @pl.loop(0, width // step)
    def _(j):
        at = pl.ds(pl.multiple_of(j * step, step), step)
        out = jnp.dot(hidden_ref[...], down_ref[:, at], preferred_element_type=jnp.float32)
        done = (out * weight_ref[...]).astype(jnp.bfloat16)
        first = 0
        for out_ref, height in zip(outs, splits):
            out_ref[:, at] = done[first : first + height]
            first += height


def ffn(shards, splits, w_gate, w_up, w_down, mine):
    width, depth = w_gate.shape
    heights = [s.shape[0] for s in shards]
    rows = sum(heights)
    return pl.pallas_call(
        functools.partial(ffn_kernel, heights, splits),
        out_shape=[jax.ShapeDtypeStruct((h, width), jnp.bfloat16) for h in splits],
        scratch_shapes=[
            pltpu.VMEM((rows, width), jnp.bfloat16),
            pltpu.VMEM((rows, depth), jnp.bfloat16),
            pltpu.VMEM((rows, 1), jnp.float32),
        ],
        compiler_params=pltpu.CompilerParams(vmem_limit_bytes=20 * MIB),
        cost_estimate=pl.CostEstimate(
            flops=6 * rows * width * depth,
            bytes_accessed=rows * width,
            transcendentals=0,
        ),
        name="expert_ffn",
    )(*shards, w_gate, w_up, w_down, mine)


def beside_kernel(x_ref, *refs):
    refs[-1][...] = x_ref[...]


def beside_weights(x, *weights):
    return pl.pallas_call(
        beside_kernel,
        out_shape=jax.ShapeDtypeStruct(x.shape, x.dtype),
        in_specs=[pl.BlockSpec(memory_space=pltpu.VMEM)] * (1 + len(weights)),
        out_specs=pl.BlockSpec(memory_space=pltpu.VMEM),
        compiler_params=pltpu.CompilerParams(vmem_limit_bytes=16 * MIB),
        name="beside_weights",
    )(x, *weights)


def join_kernel(*refs):
    out_ref, top = refs[-1], 0
    for ref in refs[:-1]:
        out_ref[top : top + ref.shape[0], :] = ref[...]
        top += ref.shape[0]


def join(arrays):
    rows = sum(a.shape[0] for a in arrays)
    return pl.pallas_call(
        join_kernel,
        out_shape=jax.ShapeDtypeStruct((rows, arrays[0].shape[1]), arrays[0].dtype),
        compiler_params=pltpu.CompilerParams(vmem_limit_bytes=16 * MIB),
        name="join_rows",
    )(*arrays)


def combine_kernel(parts, *refs):
    out_ref, at, top = refs[-1], 0, 0
    for height, offsets in parts:
        total = 0.0
        for offset in offsets:
            total = total + refs[at][offset : offset + height, :].astype(jnp.float32)
            at += 1
        out_ref[top : top + height, :] = total.astype(out_ref.dtype)
        top += height


def combine(*parts):
    arrays = [array for _, terms in parts for array, _ in terms]
    heights = [(height, [offset for _, offset in terms]) for height, terms in parts]
    rows = sum(height for height, _ in heights)
    return pl.pallas_call(
        functools.partial(combine_kernel, heights),
        out_shape=jax.ShapeDtypeStruct((rows, arrays[0].shape[1]), arrays[0].dtype),
        compiler_params=pltpu.CompilerParams(vmem_limit_bytes=16 * MIB),
        name="combine_rows",
    )(*arrays)


def local(ring, hidden_in, norm_gain, router_weight, expert_ids, w_gate, w_up, w_down):
    rows = hidden_in.shape[0]
    num_experts = router_weight.shape[1]
    local_experts = w_gate.shape[0]
    chips = len(ring)
    full, half = chips // 2 - 1, rows // 2
    tie = lax.optimization_barrier

    def shift(by):
        pairs = [
            (2 * ring[p] + c, 2 * ring[(p + by) % chips] + c)
            for p in range(chips)
            for c in range(2)
        ]
        return lambda x: lax.ppermute(x, "expert", pairs)

    ahead, behind = shift(1), shift(-1)

    def sibling(x):
        return lax.ppermute(x, "expert", [(d, d ^ 1) for d in range(2 * chips)])

    packed, first, second = pack(hidden_in, norm_gain, router_weight, expert_ids)
    lane = jnp.arange(packed.shape[1] - hidden_in.shape[1], dtype=jnp.int32)[None, :]
    place = lax.axis_index("expert")

    here = place * local_experts + jnp.arange(local_experts, dtype=jnp.int32)[:, None]
    mine = ((lane == here) | (lane == num_experts + here)).astype(jnp.float32)

    def run(shards, splits):
        total = None
        for e in range(local_experts):
            outs = ffn(shards, splits, w_gate[e], w_up[e], w_down[e], mine[e : e + 1])
            if total is None:
                total = outs
            else:
                total = [combine((a.shape[0], [(a, 0), (b, 0)])) for a, b in zip(total, outs)]
        return total

    def near(ours, theirs, count):
        return run([ours, theirs], [half] * count + [half * count])

    mine = beside_weights(mine, w_gate, w_up, w_down)
    long_a, long_b, short_a, short_b = [first], [second], [first], [second]
    terms, came = [None] * (full + 1), [None] * (full + 1)

    def beside(hops, k):
        if k < 1:
            return hops
        ours = join([long_a[k], short_b[k], short_a[k], long_b[k]])
        *terms[k], sent = near(ours, sibling(ours), 4)
        *hops, sent = tie((*hops, sent))
        came[k] = sibling(sent)
        return hops

    for k in range(1, full + 2):
        long_a.append(ahead(long_a[-1]))
        long_b.append(behind(long_b[-1]))
        if k <= full:
            short_a.append(behind(short_a[-1]))
            short_b.append(ahead(short_b[-1]))
        if k == 1:
            long_a[1], long_b[1], mine = tie((long_a[1], long_b[1], mine))
            own_kept, sent = run([packed, sibling(packed)], [rows, rows])
        elif k == 2:
            long_a[2], long_b[2], sent = tie((long_a[2], long_b[2], sent))
            own_came = sibling(sent)
        else:
            long_a[k], long_b[k] = beside((long_a[k], long_b[k]), k - 2 if k <= full else full)
            if k == full:
                long_a[k], own_came = tie((long_a[k], own_came))
    far = join([long_a[-1], long_b[-1]])
    far_a, far_b, sent = near(far, sibling(far), 2)

    def part(k, i, *more):
        return combine((half, [(terms[k][i], 0), (came[k], i * half), *((m, 0) for m in more)]))

    by_short_b, by_short_a = behind(part(full, 1)), ahead(part(full, 2))
    far_came = sibling(sent)
    by_long_a = behind(combine((half, [(far_a, 0), (far_came, 0)])))
    by_long_b = ahead(combine((half, [(far_b, 0), (far_came, half)])))
    by_long_a, by_long_b, by_short_a, by_short_b = beside(
        (by_long_a, by_long_b, by_short_a, by_short_b), full - 1
    )
    for k in range(full, 0, -1):
        by_long_a, by_long_b = behind(part(k, 0, by_long_a)), ahead(part(k, 3, by_long_b))
        if k > 1:
            by_short_b, by_short_a = (
                behind(part(k - 1, 1, by_short_b)),
                ahead(part(k - 1, 2, by_short_a)),
            )
    return combine(
        (half, [(own_kept, 0), (own_came, 0), (by_long_a, 0), (by_short_a, 0)]),
        (half, [(own_kept, half), (own_came, half), (by_long_b, 0), (by_short_b, 0)]),
    )


def solution(mesh):
    in_specs = (
        P(("groups", "expert"), None),
        P(),
        P(),
        P(("groups", "expert"), None),
        P("expert", None, None),
        P("expert", None, None),
        P("expert", None, None),
    )
    out_specs = P(("groups", "expert"), None)
    chips = mesh.shape["expert"] // 2
    columns = max(1, 4 // mesh.shape["groups"])
    if columns == 2 and chips % 2 == 0:
        ring = list(range(0, chips, 2)) + list(range(chips - 1, 0, -2))
    else:
        ring = list(range(chips))
    return jax.shard_map(
        functools.partial(local, ring),
        mesh=mesh,
        in_specs=in_specs,
        out_specs=out_specs,
        check_vma=False,
    )
```
